128 devices in a mesh: tm: 2 (over core), tile: 64 (over z, y, x).
Axes of the slice: x: 4, y: 4, z: 4, core: 2. Of those that a mesh axis runs over, the one named last changes fastest.
Arguments:
- frames: bfloat16 [8, 64, 64, 32, 128], P('tm', 'tile'), may hold values from -6 to 6
- w_in: bfloat16 [3, 3, 128, 128], replicated, may hold values from -0.1875 to 0.1875
- w_out: bfloat16 [3, 3, 128, 128], replicated, may hold values from -0.1875 to 0.1875
- decay: float32 [8, 128], P('tm'), may hold values from 0 to 1
- skip: float32 [128], replicated, may hold values from 0.5 to 1.5
Outputs:
- mixed: bfloat16 [8, 64, 64, 32, 128], P('tm', 'tile')
The draws below stay inside these ranges and needn't reach their ends.
All inputs are finite; a program needn't handle non-finite values.
Results may differ from the reference program's by a relative error of at most 0.006.
Values may be sent and summed in bfloat16 or wider, within the bound.
A program may use at most 64 MiB of HBM per device.

```python
import jax
import jax.numpy as jnp
from jax import lax

C = 128
STATE_CHANNELS = 128
TH = 64
TW = 32
TROWS = 4
WINDOW_FRAMES = 8
TILES = 64
TCOLS = 16


def draw_decay(key, part):
    sampler_keys = jax.random.split(key, 6)
    fast_rate = 0.05 ** (1.0 / jax.random.uniform(sampler_keys[0], (STATE_CHANNELS,), jnp.float32, 30.0, 50.0))
    slow_rate = 0.3 ** (1.0 / (WINDOW_FRAMES * jax.random.uniform(sampler_keys[1], (STATE_CHANNELS,), jnp.float32, 0.7, 1.0)))
    fast_mask = jax.random.randint(sampler_keys[2], (STATE_CHANNELS,), 0, 2) == 1
    resting_rate = jnp.where(fast_mask, fast_rate, slow_rate)
    noise_multiplier = jax.random.uniform(sampler_keys[3], (WINDOW_FRAMES, STATE_CHANNELS), jnp.float32, 0.97, 1.0)
    spike_events = jax.random.randint(sampler_keys[4], (WINDOW_FRAMES, 1), 0, 8) == 0
    spike_keep_mask = jax.random.uniform(sampler_keys[5], (WINDOW_FRAMES, STATE_CHANNELS), jnp.float32, 0.5, 0.8)
    return (resting_rate[None, :] * noise_multiplier * jnp.where(spike_events, spike_keep_mask, 1.0)).astype(jnp.float32)


def shard_levels(stream_key, extent, shards, low, largest):
    def one(axis_at, blocks):
        heights = jax.random.uniform(jax.random.fold_in(jax.random.fold_in(stream_key, 6), axis_at), (blocks,), jnp.float32, low / len(shards), largest / len(shards))
        return jnp.repeat(jnp.exp(heights), extent[axis_at] // blocks).reshape((-1,) + (1,) * (len(extent) - axis_at - 1))

    factor_of = one(*shards[0])
    for cut in shards[1:]:
        factor_of = factor_of * one(*cut)
    return factor_of


def gaussian(stream_key, extent, width, most, cuts=(), dtype=jnp.bfloat16):
    drawn = width * jax.random.normal(stream_key, extent, jnp.float32)
    if cuts:
        drawn = drawn * shard_levels(stream_key, extent, cuts, -0.22, 0.18)
    return jnp.clip(drawn, -most, most).astype(dtype)


def setup_inputs(seed: int = 0) -> dict:
    arg_keys = jax.random.split(jax.random.key(seed), 6)
    frames = gaussian(arg_keys[0], (WINDOW_FRAMES, TILES, TH, TW, C), 1.0, 6.0, ((0, 2), (1, 64)))
    w_in = gaussian(arg_keys[1], (3, 3, C, STATE_CHANNELS), (9 * C) ** -0.5, 0.1875)
    w_out = gaussian(arg_keys[2], (3, 3, STATE_CHANNELS, C), (9 * STATE_CHANNELS) ** -0.5, 0.1875)
    decay = draw_decay(jax.random.fold_in(arg_keys[5], 71), 0)
    skip = jnp.clip(jax.random.uniform(arg_keys[4], (C,), jnp.float32, 0.5, 1.5), 0.5, 1.5)
    return {"frames": frames, "w_in": w_in, "w_out": w_out, "decay": decay, "skip": skip}


def build_sequence(tiled):
    count = tiled.shape[0]
    ordered = jnp.roll(tiled, -1, axis=1)
    grid = ordered.reshape(count, TROWS, TCOLS, TH, TW, tiled.shape[-1])
    return grid.transpose(0, 1, 3, 2, 4, 5).reshape(count, TROWS * TH, TCOLS * TW, tiled.shape[-1])


def disassemble(image):
    count = image.shape[0]
    grid = image.reshape(count, TROWS, TH, TCOLS, TW, image.shape[-1])
    ordered = grid.transpose(0, 1, 3, 2, 4, 5).reshape(count, TROWS * TCOLS, TH, TW, image.shape[-1])
    return jnp.roll(ordered, 1, axis=1)


def convolve(picture, weight):
    result = lax.conv_general_dilated(picture[None].astype(jnp.float32), weight.astype(jnp.float32), (1, 1), "SAME", dimension_numbers=("NHWC", "HWIO", "NHWC"), precision=lax.Precision.HIGHEST)
    return result[0]


def reference(frames, w_in, w_out, decay, skip):
    image = build_sequence(frames)

    def advance(state, inputs):
        picture, keep_fraction = inputs
        drive = convolve(picture, w_in)
        state = keep_fraction * state + drive
        state_bf = lax.optimization_barrier(state.astype(jnp.bfloat16))
        mixed = convolve(state_bf, w_out) + skip * picture.astype(jnp.float32)
        return state, mixed.astype(jnp.bfloat16)

    start = jnp.zeros((TROWS * TH, TCOLS * TW, STATE_CHANNELS), jnp.float32)
    final_state, outputs = lax.scan(advance, start, (image, decay))
    return disassemble(outputs)
```

```python
import functools

import jax
import jax.numpy as jnp
from jax import lax
from jax.experimental import pallas as pl
from jax.experimental.pallas import tpu as pltpu
from jax.sharding import PartitionSpec as P

TROWS = 4
C = 128
BF = jnp.bfloat16
F32 = jnp.float32
MESH = pl.DeviceIdType.MESH

TOP = 16


def mm(lhs, rhs):
    return jnp.dot(lhs, rhs, preferred_element_type=F32)


def pair_weights(w, pair):
    zero = jnp.zeros((C, C), BF)
    for i in range(4):
        for b in range(3):
            rows = pl.ds((i * 3 + b) * C, C)
            pair[rows, 0:C] = w[i, b] if i < 3 else zero
            pair[rows, C : 2 * C] = w[i - 1, b] if i > 0 else zero


def side_weights(w, side):
    zero = jnp.zeros((C, C), BF)
    for s in range(2):
        ring = (1, 0, 2) if s == 0 else (1, 2, 0)
        edge = 0 if s == 0 else 2
        for a in range(3):
            for k in range(3):
                rows = pl.ds(k * C, C)
                side[s, rows, a * 2 * C : a * 2 * C + C] = w[a, ring[k]]
                side[s, rows, a * 2 * C + C : (a + 1) * 2 * C] = w[a, edge] if k == 0 else zero


def pair_rows(block, pairs):
    cols, depth = block.shape[1:]
    split = block.reshape(pairs + 1, 2, cols, depth)
    even, odd = split[:, 0], split[:, 1]
    taps = [even[:pairs], odd[:pairs], even[1:], odd[1:]]
    return jnp.concatenate(taps, axis=-1).reshape(pairs * cols, 4 * depth)


def kernel(
    trows, frames, w_in, w_out, decay, skip, out,
    x, x3, s3, loc, w1, w2, pw1, pw2, sw, edge, z, y, ss, stage, lo, inc, so, si, o,
    load_sem, w_sem, send_sem, recv_sem, tsend_sem, trecv_sem, out_sem,
):
    count, rows, cols, _ = frames.shape
    tiles = lax.axis_size("tile")
    tcols = tiles // trows
    me = lax.axis_index("tile")
    tm = lax.axis_index("tm")
    k = lax.rem(me + tiles - 1, tiles)
    column = lax.rem(k, tcols)
    row_index = k // tcols

    loads = [
        pltpu.make_async_copy(frames.at[f], x.at[f, pl.ds(2, rows)], load_sem.at[f])
        for f in range(count)
    ]
    for c in loads:
        c.start()
    wloads = [
        pltpu.make_async_copy(w_in, w1, w_sem.at[0]),
        pltpu.make_async_copy(w_out, w2, w_sem.at[1]),
    ]
    for c in wloads:
        c.start()

    def at(by):
        return lax.rem(me + by + tiles, tiles)

    barrier = pltpu.get_barrier_semaphore()
    steps = (-1, 1, -tcols, tcols, -tcols - 1, -tcols + 1, tcols - 1, tcols + 1)
    for by in steps:
        pl.semaphore_signal(barrier, inc=1, device_id=(tm, at(by)), device_id_type=MESH)
    pl.semaphore_signal(barrier, inc=1, device_id=(1 - tm, me), device_id_type=MESH)

    for f in range(count):
        loads[f].wait()
        first = x[f, 2 : 2 + rows, 0:16, :].astype(F32)[:, 0:8, :]
        stage[0] = first.reshape(rows * 8, C)
        last = x[f, 2 : 2 + rows, cols - 16 : cols, :].astype(F32)[:, 8:16, :]
        stage[1] = last.reshape(rows * 8, C)
        for s in range(2):
            for n in range(2):
                offset = n if s == 0 else 7 - n
                value = stage[s, pl.ds(offset, rows, stride=8), :].astype(BF)
                edge[s, n, f] = value
                if n == 0:
                    z[s, 2, f, TOP : TOP + rows] = value

    pl.semaphore_wait(barrier, 9)

    low, mid, high = pl.ds(0, TOP), pl.ds(TOP, rows), pl.ds(TOP + rows, TOP)
    head, tail = pl.ds(0, TOP), pl.ds(rows - TOP, TOP)
    two = pl.ds(0, 2)
    plan = [
        (edge.at[0], z.at[1, two, :, mid], -1),
        (edge.at[1], z.at[0, two, :, mid], 1),
        (frames.at[:, pl.ds(0, 2)], x.at[:, pl.ds(rows + 2, 2)], -tcols),
        (frames.at[:, pl.ds(rows - 2, 2)], x.at[:, pl.ds(0, 2)], tcols),
        (edge.at[:, 0, :, head], z.at[:, 2, :, high], -tcols),
        (edge.at[:, 0, :, tail], z.at[:, 2, :, low], tcols),
        (edge.at[0, :, :, head], z.at[1, two, :, high], -tcols - 1),
        (edge.at[1, :, :, head], z.at[0, two, :, high], -tcols + 1),
        (edge.at[0, :, :, tail], z.at[1, two, :, low], tcols - 1),
        (edge.at[1, :, :, tail], z.at[0, two, :, low], tcols + 1),
    ]
    sends = [
        pltpu.make_async_remote_copy(
            src_ref=src, dst_ref=dst, send_sem=send_sem.at[i], recv_sem=recv_sem.at[i],
            device_id=(tm, at(by)), device_id_type=MESH,
        )
        for i, (src, dst, by) in enumerate(plan)
    ]
    for c in sends:
        c.start()

    wloads[0].wait()
    pair_weights(w1, pw1)
    side_weights(w1, sw)

    column_of = lax.broadcasted_iota(jnp.int32, (1, cols, C), 1)

    def widen(f, start, size):
        block = x[f, pl.ds(start, size)]
        wide = block.astype(F32)
        left = jnp.where(column_of == 0, 0.0, pltpu.roll(wide, 1, 1))
        right = jnp.where(column_of == cols - 1, 0.0, pltpu.roll(wide, cols - 1, 1))
        x3[f, pl.ds(start, size), :, 0:C] = left.astype(BF)
        x3[f, pl.ds(start, size), :, C : 2 * C] = block
        x3[f, pl.ds(start, size), :, 2 * C : 3 * C] = right.astype(BF)

    for f in range(count):
        @pl.loop(0, rows // 8)
        def _(i):
            widen(f, 2 + i * 8, 8)

    def exchange(i, src, dst):
        return pltpu.make_async_remote_copy(
            src_ref=src, dst_ref=dst, send_sem=tsend_sem.at[i], recv_sem=trecv_sem.at[i],
            device_id=(1 - tm, me), device_id_type=MESH,
        )

    half = rows // 4
    chunks = [(1, half), (1 + half, rows // 2 - 1 - half)]
    hands = [
        exchange(0, lo.at[pl.ds(*chunks[0])], inc.at[pl.ds(*chunks[0])]),
        exchange(1, lo.at[pl.ds(*chunks[1])], inc.at[pl.ds(*chunks[1])]),
        exchange(2, lo.at[pl.ds(0, 1)], inc.at[pl.ds(0, 1)]),
        exchange(3, lo.at[pl.ds(rows // 2, 1)], inc.at[pl.ds(rows // 2, 1)]),
        exchange(4, so, si),
    ]

    def recur(f, q, size, drive):
        drive = drive.reshape(size, cols, 2 * C)
        for e in range(2):
            value = drive[:, :, e * C : (e + 1) * C]
            if f > 0:
                value = decay[f : f + 1, :] * loc[f - 1, pl.ds(q, size), e] + value
            loc[f, pl.ds(q, size), e] = value
            if f == count - 1:
                lo[pl.ds(q, size), e] = value.astype(BF)

    for n, (q, size) in enumerate(chunks):
        for f in range(count):
            lhs = pair_rows(x3[f, 2 * q : 2 * q + 2 * size + 2], size)
            recur(f, q, size, mm(lhs, pw1[...]))

        @pl.when(tm == 0)
        def _():
            hands[n].start()

    for c in sends:
        c.wait_recv()
    for f in range(count):
        widen(f, 0, 2)
        widen(f, rows + 2, 2)

    @pl.when(row_index == 0)
    def _():
        x3[:, 0:2] = jnp.zeros((count, 2, cols, 3 * C), BF)

    @pl.when(row_index == trows - 1)
    def _():
        x3[:, rows + 2 : rows + 4] = jnp.zeros((count, 2, cols, 3 * C), BF)

    for q in (0, rows // 2):
        lhs = jnp.concatenate([pair_rows(x3[f, 2 * q : 2 * q + 4], 1) for f in range(count)], axis=0)
        drive = mm(lhs, pw1[...])
        for f in range(count):
            recur(f, q, 1, drive[f * cols : (f + 1) * cols])

    @pl.when(tm == 0)
    def _():
        hands[2].start()
        hands[3].start()

    span = rows + 2 * TOP
    for s in range(2):
        lhs = jnp.concatenate([z[s, n].reshape(count * span, C) for n in range(3)], axis=-1)
        result = mm(lhs, sw[s])
        for a in range(3):
            y[s, a] = result[:, a * 2 * C : (a + 1) * 2 * C].reshape(count, span, 2 * C)

    @pl.when(row_index == 0)
    def _():
        y[:, :, :, 0:TOP] = jnp.zeros((2, 3, count, TOP, 2 * C), F32)

    @pl.when(row_index == trows - 1)
    def _():
        y[:, :, :, TOP + rows : span] = jnp.zeros((2, 3, count, TOP, 2 * C), F32)

    tall = rows + 16
    for s in range(2):
        inside = jnp.where(column > 0 if s == 0 else column < tcols - 1, 1.0, 0.0).astype(F32)
        for e in range(2):
            lanes = slice(e * C, (e + 1) * C)
            state = None
            for f in range(count):
                drive = (
                    y[s, 0, f, 7 : 7 + tall, lanes] + y[s, 1, f, 8 : 8 + tall, lanes] + y[s, 2, f, 9 : 9 + tall, lanes]
                ) * inside
                state = drive if f == 0 else decay[f : f + 1, :] * state + drive
                ss[s, e, f] = state
            so[s, e] = state.astype(BF)

    @pl.when(tm == 0)
    def _():
        hands[4].start()
        inc[...] = jnp.zeros(inc.shape, BF)
        si[...] = jnp.zeros(si.shape, BF)

    wloads[1].wait()
    pair_weights(w2, pw2)

    @pl.when(tm == 1)
    def _():
        for c in hands:
            c.wait_recv()

    factors = []
    for f in range(count):
        keep = decay[f : f + 1, :]
        factors.append(keep if f == 0 else factors[-1] * keep)
    for s in range(2):
        for e in range(2):
            arrived = si[s, e].astype(F32)
            for f in range(count):
                ss[s, e, f] = ss[s, e, f] + factors[f] * arrived

    column_in = lax.broadcasted_iota(jnp.int32, (cols, C), 0)

    @pl.loop(0, rows // 2 + 1)
    def _(q):
        for e in range(2):
            arrived = inc[q, e].astype(F32)
            at_row = 2 * q + e
            side = pl.ds(at_row + 7, 1)
            for f in range(count):
                state = loc[f, q, e] + factors[f] * arrived
                state = state + jnp.where(column_in == 0, ss[0, 1, f, side, :], 0.0)
                state = state + jnp.where(column_in == cols - 1, ss[1, 1, f, side, :], 0.0)
                left = jnp.where(column_in == 0, ss[0, 0, f, side, :], pltpu.roll(state, 1, 0))
                right = jnp.where(column_in == cols - 1, ss[1, 0, f, side, :], pltpu.roll(state, cols - 1, 0))
                s3[f, at_row, :, 0:C] = left.astype(BF)
                s3[f, at_row, :, C : 2 * C] = state.astype(BF)
                s3[f, at_row, :, 2 * C : 3 * C] = right.astype(BF)

    @pl.when(row_index == 0)
    def _():
        s3[:, 0:1] = jnp.zeros((count, 1, cols, 3 * C), BF)

    @pl.when(row_index == trows - 1)
    def _():
        s3[:, rows + 1 : rows + 2] = jnp.zeros((count, 1, cols, 3 * C), BF)

    stores = []
    for f in range(count):
        for n in range(2):
            lhs = pair_rows(s3[f, 2 * n * half : 2 * (n + 1) * half + 2], half)
            result = mm(lhs, pw2[...]).reshape(half, cols, 2 * C)
            base = 2 * n * half
            video = x[f, 2 + base : 2 + base + 2 * half].astype(F32).reshape(half, 2, cols, C)
            for e in range(2):
                mixed = result[:, :, e * C : (e + 1) * C] + skip[...] * video[:, e]
                o[f, n * half : (n + 1) * half, e] = mixed.astype(BF)
            store = pltpu.make_async_copy(
                o.at[f, pl.ds(n * half, half)], out.at[f, pl.ds(n * half, half)], out_sem.at[2 * f + n]
            )
            store.start()
            stores.append(store)

    for c in sends:
        c.wait_send()

    @pl.when(tm == 0)
    def _():
        for c in hands:
            c.wait_send()

    for c in stores:
        c.wait()


def per_device(frames, w_in, w_out, decay, skip):
    count, _, rows, cols, _ = frames.shape
    pairs = rows // 2 + 1
    span = rows + 2 * TOP
    tall = rows + 16
    anywhere = pl.BlockSpec(memory_space=pl.ANY)
    vmem = pl.BlockSpec(memory_space=pltpu.VMEM)
    out = pl.pallas_call(
        functools.partial(kernel, TROWS),
        out_shape=jax.ShapeDtypeStruct((count, rows // 2, 2, cols, C), BF),
        in_specs=[anywhere, anywhere, anywhere, vmem, vmem],
        out_specs=anywhere,
        scratch_shapes=[
            pltpu.VMEM((count, rows + 4, cols, C), BF),
            pltpu.VMEM((count, rows + 4, cols, 3 * C), BF),
            pltpu.VMEM((count, rows + 2, cols, 3 * C), BF),
            pltpu.VMEM((count, pairs, 2, cols, C), F32),
            pltpu.VMEM((3, 3, C, C), BF),
            pltpu.VMEM((3, 3, C, C), BF),
            pltpu.VMEM((12 * C, 2 * C), BF),
            pltpu.VMEM((12 * C, 2 * C), BF),
            pltpu.VMEM((2, 3 * C, 6 * C), BF),
            pltpu.VMEM((2, 2, count, rows, C), BF),
            pltpu.VMEM((2, 3, count, span, C), BF),
            pltpu.VMEM((2, 3, count, span, 2 * C), F32),
            pltpu.VMEM((2, 2, count, tall, C), F32),
            pltpu.VMEM((2, rows * 8, C), F32),
            pltpu.VMEM((pairs, 2, cols, C), BF),
            pltpu.VMEM((pairs, 2, cols, C), BF),
            pltpu.VMEM((2, 2, tall, C), BF),
            pltpu.VMEM((2, 2, tall, C), BF),
            pltpu.VMEM((count, rows // 2, 2, cols, C), BF),
            pltpu.SemaphoreType.DMA((count,)),
            pltpu.SemaphoreType.DMA((2,)),
            pltpu.SemaphoreType.DMA((10,)),
            pltpu.SemaphoreType.DMA((10,)),
            pltpu.SemaphoreType.DMA((5,)),
            pltpu.SemaphoreType.DMA((5,)),
            pltpu.SemaphoreType.DMA((2 * count,)),
        ],
        compiler_params=pltpu.CompilerParams(
            collective_id=0, has_side_effects=True, vmem_limit_bytes=56 * 2**20
        ),
    )(frames[:, 0], w_in, w_out, decay, skip.reshape(1, C))
    return out.reshape(count, 1, rows, cols, C)


def solution(mesh):
    return jax.shard_map(
        per_device,
        mesh=mesh,
        in_specs=(P("tm", "tile", None, None, None), P(), P(), P("tm", None), P()),
        out_specs=P("tm", "tile", None, None, None),
        check_vma=False,
    )
```

```python
import functools

import jax
import jax.numpy as jnp
from jax import lax
from jax.experimental import pallas as pl
from jax.experimental.pallas import tpu as pltpu
from jax.sharding import PartitionSpec as P

TROWS = 4
C = 128
BF = jnp.bfloat16
F32 = jnp.float32
MESH = pl.DeviceIdType.MESH

TOP = 16


def mm(lhs, rhs):
    return jnp.dot(lhs, rhs, preferred_element_type=F32)


def pair_weights(w, pair):
    zero = jnp.zeros((C, C), BF)
    for i in range(4):
        for b in range(3):
            rows = pl.ds((i * 3 + b) * C, C)
            pair[rows, 0:C] = w[i, b] if i < 3 else zero
            pair[rows, C : 2 * C] = w[i - 1, b] if i > 0 else zero


def side_weights(w, side):
    zero = jnp.zeros((C, C), BF)
    for s in range(2):
        ring = (1, 0, 2) if s == 0 else (1, 2, 0)
        edge = 0 if s == 0 else 2
        for a in range(3):
            for k in range(3):
                rows = pl.ds(k * C, C)
                side[s, rows, a * 2 * C : a * 2 * C + C] = w[a, ring[k]]
                side[s, rows, a * 2 * C + C : (a + 1) * 2 * C] = w[a, edge] if k == 0 else zero


def pair_rows(block, pairs):
    cols, depth = block.shape[1:]
    split = block.reshape(pairs + 1, 2, cols, depth)
    even, odd = split[:, 0], split[:, 1]
    taps = [even[:pairs], odd[:pairs], even[1:], odd[1:]]
    return jnp.concatenate(taps, axis=-1).reshape(pairs * cols, 4 * depth)


def kernel(
    trows, frames, w_in, w_out, decay_in, skip_in, o,
    x, x3, s3, loc, w1, w2, pw1, pw2, sw, edge, z, y, ss, stage, lo, inc, so, si, decay, skip,
    load_sem, w_sem, send_sem, recv_sem, tsend_sem, trecv_sem,
):
    count, rows, cols, _ = frames.shape
    tiles = lax.axis_size("tile")
    tcols = tiles // trows
    me = lax.axis_index("tile")
    tm = lax.axis_index("tm")
    k = lax.rem(me + tiles - 1, tiles)
    column = lax.rem(k, tcols)
    row_index = k // tcols

    loads = [
        pltpu.make_async_copy(frames.at[f], x.at[f, pl.ds(2, rows)], load_sem.at[f])
        for f in range(count)
    ]
    for c in loads:
        c.start()
    wloads = [
        pltpu.make_async_copy(w_in, w1, w_sem.at[0]),
        pltpu.make_async_copy(w_out, w2, w_sem.at[1]),
        pltpu.make_async_copy(decay_in, decay, w_sem.at[2]),
        pltpu.make_async_copy(skip_in, skip, w_sem.at[3]),
    ]
    for c in wloads:
        c.start()

    def at(by):
        return lax.rem(me + by + tiles, tiles)

    barrier = pltpu.get_barrier_semaphore()
    steps = (-1, 1, -tcols, tcols, -tcols - 1, -tcols + 1, tcols - 1, tcols + 1)
    for by in steps:
        pl.semaphore_signal(barrier, inc=1, device_id=(tm, at(by)), device_id_type=MESH)
    pl.semaphore_signal(barrier, inc=1, device_id=(1 - tm, me), device_id_type=MESH)

    for f in range(count):
        loads[f].wait()
        first = x[f, 2 : 2 + rows, 0:16, :].astype(F32)[:, 0:8, :]
        stage[0] = first.reshape(rows * 8, C)
        last = x[f, 2 : 2 + rows, cols - 16 : cols, :].astype(F32)[:, 8:16, :]
        stage[1] = last.reshape(rows * 8, C)
        for s in range(2):
            for n in range(2):
                offset = n if s == 0 else 7 - n
                value = stage[s, pl.ds(offset, rows, stride=8), :].astype(BF)
                edge[s, n, f] = value
                if n == 0:
                    z[s, 2, f, TOP : TOP + rows] = value

    pl.semaphore_wait(barrier, 9)

    low, mid, high = pl.ds(0, TOP), pl.ds(TOP, rows), pl.ds(TOP + rows, TOP)
    head, tail = pl.ds(0, TOP), pl.ds(rows - TOP, TOP)
    two = pl.ds(0, 2)
    plan = [
        (edge.at[0], z.at[1, two, :, mid], -1),
        (edge.at[1], z.at[0, two, :, mid], 1),
        (frames.at[:, pl.ds(0, 2)], x.at[:, pl.ds(rows + 2, 2)], -tcols),
        (frames.at[:, pl.ds(rows - 2, 2)], x.at[:, pl.ds(0, 2)], tcols),
        (edge.at[:, 0, :, head], z.at[:, 2, :, high], -tcols),
        (edge.at[:, 0, :, tail], z.at[:, 2, :, low], tcols),
        (edge.at[0, :, :, head], z.at[1, two, :, high], -tcols - 1),
        (edge.at[1, :, :, head], z.at[0, two, :, high], -tcols + 1),
        (edge.at[0, :, :, tail], z.at[1, two, :, low], tcols - 1),
        (edge.at[1, :, :, tail], z.at[0, two, :, low], tcols + 1),
    ]
    sends = [
        pltpu.make_async_remote_copy(
            src_ref=src, dst_ref=dst, send_sem=send_sem.at[i], recv_sem=recv_sem.at[i],
            device_id=(tm, at(by)), device_id_type=MESH,
        )
        for i, (src, dst, by) in enumerate(plan)
    ]
    for c in sends:
        c.start()

    wloads[0].wait()
    wloads[2].wait()
    wloads[3].wait()
    pair_weights(w1, pw1)
    side_weights(w1, sw)

    column_of = lax.broadcasted_iota(jnp.int32, (1, cols, C), 1)

    def widen(f, start, size):
        block = x[f, pl.ds(start, size)]
        wide = block.astype(F32)
        left = jnp.where(column_of == 0, 0.0, pltpu.roll(wide, 1, 1))
        right = jnp.where(column_of == cols - 1, 0.0, pltpu.roll(wide, cols - 1, 1))
        x3[f, pl.ds(start, size), :, 0:C] = left.astype(BF)
        x3[f, pl.ds(start, size), :, C : 2 * C] = block
        x3[f, pl.ds(start, size), :, 2 * C : 3 * C] = right.astype(BF)

    for f in range(count):
        @pl.loop(0, rows // 8)
        def _(i):
            widen(f, 2 + i * 8, 8)

    def exchange(i, src, dst):
        return pltpu.make_async_remote_copy(
            src_ref=src, dst_ref=dst, send_sem=tsend_sem.at[i], recv_sem=trecv_sem.at[i],
            device_id=(1 - tm, me), device_id_type=MESH,
        )

    half = rows // 4
    chunks = [(1, half), (1 + half, rows // 2 - 1 - half)]
    hands = [
        exchange(0, lo.at[pl.ds(*chunks[0])], inc.at[pl.ds(*chunks[0])]),
        exchange(1, lo.at[pl.ds(*chunks[1])], inc.at[pl.ds(*chunks[1])]),
        exchange(2, lo.at[pl.ds(0, 1)], inc.at[pl.ds(0, 1)]),
        exchange(3, lo.at[pl.ds(rows // 2, 1)], inc.at[pl.ds(rows // 2, 1)]),
        exchange(4, so, si),
    ]

    def recur(f, q, size, drive):
        drive = drive.reshape(size, cols, 2 * C)
        for e in range(2):
            value = drive[:, :, e * C : (e + 1) * C]
            if f > 0:
                value = decay[f : f + 1, :] * loc[f - 1, pl.ds(q, size), e] + value
            loc[f, pl.ds(q, size), e] = value
            if f == count - 1:
                lo[pl.ds(q, size), e] = value.astype(BF)

    for n, (q, size) in enumerate(chunks):
        for f in range(count):
            lhs = pair_rows(x3[f, 2 * q : 2 * q + 2 * size + 2], size)
            recur(f, q, size, mm(lhs, pw1[...]))

        @pl.when(tm == 0)
        def _():
            hands[n].start()

    for c in sends:
        c.wait_recv()
    for f in range(count):
        widen(f, 0, 2)
        widen(f, rows + 2, 2)

    @pl.when(row_index == 0)
    def _():
        x3[:, 0:2] = jnp.zeros((count, 2, cols, 3 * C), BF)

    @pl.when(row_index == trows - 1)
    def _():
        x3[:, rows + 2 : rows + 4] = jnp.zeros((count, 2, cols, 3 * C), BF)

    for q in (0, rows // 2):
        lhs = jnp.concatenate([pair_rows(x3[f, 2 * q : 2 * q + 4], 1) for f in range(count)], axis=0)
        drive = mm(lhs, pw1[...])
        for f in range(count):
            recur(f, q, 1, drive[f * cols : (f + 1) * cols])

    @pl.when(tm == 0)
    def _():
        hands[2].start()
        hands[3].start()

    span = rows + 2 * TOP
    for s in range(2):
        lhs = jnp.concatenate([z[s, n].reshape(count * span, C) for n in range(3)], axis=-1)
        result = mm(lhs, sw[s])
        for a in range(3):
            y[s, a] = result[:, a * 2 * C : (a + 1) * 2 * C].reshape(count, span, 2 * C)

    @pl.when(row_index == 0)
    def _():
        y[:, :, :, 0:TOP] = jnp.zeros((2, 3, count, TOP, 2 * C), F32)

    @pl.when(row_index == trows - 1)
    def _():
        y[:, :, :, TOP + rows : span] = jnp.zeros((2, 3, count, TOP, 2 * C), F32)

    tall = rows + 16
    for s in range(2):
        inside = jnp.where(column > 0 if s == 0 else column < tcols - 1, 1.0, 0.0).astype(F32)
        for e in range(2):
            lanes = slice(e * C, (e + 1) * C)
            state = None
            for f in range(count):
                drive = (
                    y[s, 0, f, 7 : 7 + tall, lanes] + y[s, 1, f, 8 : 8 + tall, lanes] + y[s, 2, f, 9 : 9 + tall, lanes]
                ) * inside
                state = drive if f == 0 else decay[f : f + 1, :] * state + drive
                ss[s, e, f] = state
            so[s, e] = state.astype(BF)

    @pl.when(tm == 0)
    def _():
        hands[4].start()
        inc[...] = jnp.zeros(inc.shape, BF)
        si[...] = jnp.zeros(si.shape, BF)

    wloads[1].wait()
    pair_weights(w2, pw2)

    @pl.when(tm == 1)
    def _():
        for c in hands:
            c.wait_recv()

    factors = []
    for f in range(count):
        keep = decay[f : f + 1, :]
        factors.append(keep if f == 0 else factors[-1] * keep)
    for s in range(2):
        for e in range(2):
            arrived = si[s, e].astype(F32)
            for f in range(count):
                ss[s, e, f] = ss[s, e, f] + factors[f] * arrived

    column_in = lax.broadcasted_iota(jnp.int32, (cols, C), 0)

    @pl.loop(0, rows // 2 + 1)
    def _(q):
        for e in range(2):
            arrived = inc[q, e].astype(F32)
            at_row = 2 * q + e
            side = pl.ds(at_row + 7, 1)
            for f in range(count):
                state = loc[f, q, e] + factors[f] * arrived
                state = state + jnp.where(column_in == 0, ss[0, 1, f, side, :], 0.0)
                state = state + jnp.where(column_in == cols - 1, ss[1, 1, f, side, :], 0.0)
                left = jnp.where(column_in == 0, ss[0, 0, f, side, :], pltpu.roll(state, 1, 0))
                right = jnp.where(column_in == cols - 1, ss[1, 0, f, side, :], pltpu.roll(state, cols - 1, 0))
                s3[f, at_row, :, 0:C] = left.astype(BF)
                s3[f, at_row, :, C : 2 * C] = state.astype(BF)
                s3[f, at_row, :, 2 * C : 3 * C] = right.astype(BF)

    @pl.when(row_index == 0)
    def _():
        s3[:, 0:1] = jnp.zeros((count, 1, cols, 3 * C), BF)

    @pl.when(row_index == trows - 1)
    def _():
        s3[:, rows + 1 : rows + 2] = jnp.zeros((count, 1, cols, 3 * C), BF)

    for f in range(count):
        for n in range(2):
            lhs = pair_rows(s3[f, 2 * n * half : 2 * (n + 1) * half + 2], half)
            result = mm(lhs, pw2[...]).reshape(half, cols, 2 * C)
            base = 2 * n * half
            video = x[f, 2 + base : 2 + base + 2 * half].astype(F32).reshape(half, 2, cols, C)
            for e in range(2):
                mixed = result[:, :, e * C : (e + 1) * C] + skip[...] * video[:, e]
                o[f, n * half : (n + 1) * half, e] = mixed.astype(BF)

    for c in sends:
        c.wait_send()

    @pl.when(tm == 0)
    def _():
        for c in hands:
            c.wait_send()


def write_out(o, out, sem):
    stores = [pltpu.make_async_copy(o.at[f], out.at[f], sem.at[f]) for f in range(o.shape[0])]
    for c in stores:
        c.start()
    for c in stores:
        c.wait()


def per_device(frames, w_in, w_out, decay, skip):
    count, _, rows, cols, _ = frames.shape
    pairs = rows // 2 + 1
    span = rows + 2 * TOP
    tall = rows + 16
    hbm = pl.BlockSpec(memory_space=pltpu.HBM)
    vmem = pl.BlockSpec(memory_space=pltpu.VMEM)
    out = pl.pallas_call(
        functools.partial(kernel, TROWS),
        out_shape=pltpu.VMEM((count, rows // 2, 2, cols, C), BF),
        in_specs=[hbm] * 5,
        out_specs=vmem,
        scratch_shapes=[
            pltpu.VMEM((count, rows + 4, cols, C), BF),
            pltpu.VMEM((count, rows + 4, cols, 3 * C), BF),
            pltpu.VMEM((count, rows + 2, cols, 3 * C), BF),
            pltpu.VMEM((count, pairs, 2, cols, C), F32),
            pltpu.VMEM((3, 3, C, C), BF),
            pltpu.VMEM((3, 3, C, C), BF),
            pltpu.VMEM((12 * C, 2 * C), BF),
            pltpu.VMEM((12 * C, 2 * C), BF),
            pltpu.VMEM((2, 3 * C, 6 * C), BF),
            pltpu.VMEM((2, 2, count, rows, C), BF),
            pltpu.VMEM((2, 3, count, span, C), BF),
            pltpu.VMEM((2, 3, count, span, 2 * C), F32),
            pltpu.VMEM((2, 2, count, tall, C), F32),
            pltpu.VMEM((2, rows * 8, C), F32),
            pltpu.VMEM((pairs, 2, cols, C), BF),
            pltpu.VMEM((pairs, 2, cols, C), BF),
            pltpu.VMEM((2, 2, tall, C), BF),
            pltpu.VMEM((2, 2, tall, C), BF),
            pltpu.VMEM((count, C), F32),
            pltpu.VMEM((1, C), F32),
            pltpu.SemaphoreType.DMA((count,)),
            pltpu.SemaphoreType.DMA((4,)),
            pltpu.SemaphoreType.DMA((10,)),
            pltpu.SemaphoreType.DMA((10,)),
            pltpu.SemaphoreType.DMA((5,)),
            pltpu.SemaphoreType.DMA((5,)),
        ],
        compiler_params=pltpu.CompilerParams(
            collective_id=0, has_side_effects=True, vmem_limit_bytes=44 * 2**20
        ),
    )(*(pltpu.with_memory_space_constraint(a, pltpu.HBM) for a in (frames[:, 0], w_in, w_out, decay, skip.reshape(1, C))))
    out = pl.pallas_call(
        write_out,
        out_shape=jax.ShapeDtypeStruct(out.shape, BF),
        in_specs=[vmem],
        out_specs=hbm,
        scratch_shapes=[pltpu.SemaphoreType.DMA((count,))],
        compiler_params=pltpu.CompilerParams(vmem_limit_bytes=2**20),
    )(pltpu.with_memory_space_constraint(out, pltpu.VMEM))
    return out.reshape(count, 1, rows, cols, C)


def solution(mesh):
    return jax.shard_map(
        per_device,
        mesh=mesh,
        in_specs=(P("tm", "tile", None, None, None), P(), P(), P("tm", None), P()),
        out_specs=P("tm", "tile", None, None, None),
        check_vma=False,
    )
```

```python
import functools

import jax
import jax.numpy as jnp
from jax import lax
from jax.experimental import pallas as pl
from jax.experimental.pallas import tpu as pltpu
from jax.sharding import PartitionSpec as P

TROWS = 4
C = 128
BF = jnp.bfloat16
F32 = jnp.float32
MESH = pl.DeviceIdType.MESH

TOP = 16
TAPS = (0, 2, 1)


def mm(lhs, rhs):
    return jnp.dot(lhs, rhs, preferred_element_type=F32)


def pair_weights(w, pair):
    zero = jnp.zeros((C, C), BF)
    for i in range(4):
        for n, b in enumerate(TAPS):
            rows = pl.ds((i * 3 + n) * C, C)
            pair[rows, 0:C] = w[i, b] if i < 3 else zero
            pair[rows, C : 2 * C] = w[i - 1, b] if i > 0 else zero


def side_weights(w, side, table):
    zero = jnp.zeros((C, C), BF)
    for s in range(2):
        for a in range(3):
            for k, taps in enumerate(table[s]):
                for e, b in enumerate(taps):
                    lanes = pl.ds((a * 2 + e) * C, C)
                    side[s, pl.ds(k * C, C), lanes] = zero if b is None else w[a, b]


SIDE_IN = (((1, 0), (0, None), (2, None)), ((1, 2), (2, None), (0, None)))
SIDE_OUT = (((0, None), (1, 0)), ((2, None), (1, 2)))


def pair_rows(parts, pairs):
    cols = parts[0].shape[1]
    split = [p.reshape(pairs + 1, 2, cols, p.shape[2]) for p in parts]
    taps = []
    for first in (0, 1):
        for parity in (0, 1):
            taps += [p[first : first + pairs, parity] for p in split]
    return jnp.concatenate(taps, axis=-1).reshape(pairs * cols, 12 * C)


def kernel(
    trows, frames, w_in, w_out, decay_in, skip_in, o,
    x, x3, s3, loc, w1, w2, pw1, pw2, sw1, sw2, edge, z, y, y2, ss, own, stage, lo, inc, so, si, ot, decay, skip,
    load_sem, w_sem, send_sem, recv_sem, tsend_sem, trecv_sem,
):
    count, rows, cols, _ = frames.shape
    tiles = lax.axis_size("tile")
    tcols = tiles // trows
    me = lax.axis_index("tile")
    tm = lax.axis_index("tm")
    k = lax.rem(me + tiles - 1, tiles)
    column = lax.rem(k, tcols)
    row_index = k // tcols
    at_top = row_index == 0
    at_bottom = row_index == trows - 1
    pairs = rows // 2
    tall = rows + 16
    span = rows + 2 * TOP

    loads = [
        pltpu.make_async_copy(frames.at[f], x.at[f, pl.ds(2, rows)], load_sem.at[f])
        for f in range(count)
    ]
    for c in loads:
        c.start()
    wloads = [
        pltpu.make_async_copy(src, dst, w_sem.at[i])
        for i, (src, dst) in enumerate(((w_in, w1), (decay_in, decay), (skip_in, skip), (w_out, w2)))
    ]
    for c in wloads:
        c.start()

    def at(by):
        return lax.rem(me + by + tiles, tiles)

    barrier = pltpu.get_barrier_semaphore()
    steps = (-1, 1, -tcols, tcols, -tcols - 1, -tcols + 1, tcols - 1, tcols + 1)
    for by in steps:
        pl.semaphore_signal(barrier, inc=1, device_id=(tm, at(by)), device_id_type=MESH)
    pl.semaphore_signal(barrier, inc=1, device_id=(1 - tm, me), device_id_type=MESH)

    own[:, :, 0:8] = jnp.zeros((2, count, 8, C), F32)
    own[:, :, rows + 8 : rows + 16] = jnp.zeros((2, count, 8, C), F32)

    for f in range(count):
        loads[f].wait()
        first = x[f, 2 : 2 + rows, 0:16, :].astype(F32)[:, 0:8, :]
        stage[0] = first.reshape(rows * 8, C)
        last = x[f, 2 : 2 + rows, cols - 16 : cols, :].astype(F32)[:, 8:16, :]
        stage[1] = last.reshape(rows * 8, C)
        for s in range(2):
            for n in range(2):
                offset = n if s == 0 else 7 - n
                value = stage[s, pl.ds(offset, rows, stride=8), :].astype(BF)
                edge[s, n, f] = value
                if n == 0:
                    z[s, 2, f, TOP : TOP + rows] = value

    pl.semaphore_wait(barrier, 9)

    low, mid, high = pl.ds(0, TOP), pl.ds(TOP, rows), pl.ds(TOP + rows, TOP)
    head, tail = pl.ds(0, TOP), pl.ds(rows - TOP, TOP)
    two = pl.ds(0, 2)
    plan = [
        (edge.at[0], z.at[1, two, :, mid], -1),
        (edge.at[1], z.at[0, two, :, mid], 1),
        (frames.at[:, pl.ds(0, 2)], x.at[:, pl.ds(rows + 2, 2)], -tcols),
        (frames.at[:, pl.ds(rows - 2, 2)], x.at[:, pl.ds(0, 2)], tcols),
        (edge.at[:, 0, :, head], z.at[:, 2, :, high], -tcols),
        (edge.at[:, 0, :, tail], z.at[:, 2, :, low], tcols),
        (edge.at[0, :, :, head], z.at[1, two, :, high], -tcols - 1),
        (edge.at[1, :, :, head], z.at[0, two, :, high], -tcols + 1),
        (edge.at[0, :, :, tail], z.at[1, two, :, low], tcols - 1),
        (edge.at[1, :, :, tail], z.at[0, two, :, low], tcols + 1),
    ]
    sends = [
        pltpu.make_async_remote_copy(
            src_ref=src, dst_ref=dst, send_sem=send_sem.at[i], recv_sem=recv_sem.at[i],
            device_id=(tm, at(by)), device_id_type=MESH,
        )
        for i, (src, dst, by) in enumerate(plan)
    ]
    for c in sends:
        c.start()

    for c in wloads[:3]:
        c.wait()
    pair_weights(w1, pw1)

    in_tile = lax.broadcasted_iota(jnp.int32, (1, 8, C), 1)

    def shifted(wide):
        no_last = jnp.concatenate([wide[:, : cols - 8], jnp.where(in_tile == 7, 0.0, wide[:, cols - 8 :])], axis=1)
        no_first = jnp.concatenate([jnp.where(in_tile == 0, 0.0, wide[:, :8]), wide[:, 8:]], axis=1)
        return pltpu.roll(no_last, 1, 1), pltpu.roll(no_first, cols - 1, 1)

    def widen(f, start, size, real=None):
        wide = x[f, pl.ds(start, size)].astype(F32)
        if real is not None:
            wide = jnp.where(real, wide, 0.0)
            x[f, pl.ds(start, size)] = wide.astype(BF)
        left, right = shifted(wide)
        x3[f, pl.ds(start, size), :, 0:C] = left.astype(BF)
        x3[f, pl.ds(start, size), :, C : 2 * C] = right.astype(BF)

    def exchange(i, src, dst):
        return pltpu.make_async_remote_copy(
            src_ref=src, dst_ref=dst, send_sem=tsend_sem.at[i], recv_sem=trecv_sem.at[i],
            device_id=(1 - tm, me), device_id_type=MESH,
        )

    half = pairs // 2
    chunks = [(1, half), (1 + half, pairs - 1 - half)]
    hands = [exchange(n, lo.at[pl.ds(q, size)], inc.at[pl.ds(q, size)]) for n, (q, size) in enumerate(chunks)]
    late_hands = [
        exchange(2, lo.at[pl.ds(0, 1)], inc.at[pl.ds(0, 1)]),
        exchange(3, lo.at[pl.ds(pairs, 1)], inc.at[pl.ds(pairs, 1)]),
        exchange(4, so, si),
    ]

    def recur(f, q, size, drive):
        drive = drive.reshape(size, cols, 2 * C)
        drive = jnp.stack([drive[:, :, :C], drive[:, :, C:]], axis=1).reshape(size * 2 * cols, C)
        here = pl.ds(q * 2 * cols, size * 2 * cols)
        if f > 0:
            drive = decay[f : f + 1, :] * loc[f - 1, here] + drive
        loc[f, here] = drive
        if f == count - 1:
            lo[pl.ds(q, size)] = drive.astype(BF).reshape(size, 2, cols, C)

    for n, (q, size) in enumerate(chunks):
        for f in range(count):
            end = rows + 2 if n else 2 * half + 4
            for start in range(2 + n * (2 * half + 2), end, 2):
                widen(f, start, 2)
            here = pl.ds(2 * q, 2 * size + 2)
            lhs = pair_rows([x3[f, here], x[f, here]], size)
            recur(f, q, size, mm(lhs, pw1[...]))
        hands[n].start()

    factors = []
    for f in range(count):
        keep = decay[f : f + 1, :]
        factors.append(keep * jnp.where(tm == 0, 0.0, 1.0) if f == 0 else factors[-1] * keep)

    def settle(f, q, real=(None, None)):
        state = loc[f, pl.ds(q * 2 * cols, 2 * cols)].reshape(2, cols, C) + factors[f] * inc[q].astype(F32)
        first = jnp.where(in_tile == 0, 0.0, state[:, :8])
        last = jnp.where(in_tile == 7, 0.0, state[:, cols - 8 :])
        state = jnp.concatenate([first, state[:, 8 : cols - 8], last], axis=1)
        state = jnp.concatenate(
            [state[e : e + 1] if r is None else jnp.where(r, state[e : e + 1], 0.0) for e, r in enumerate(real)],
            axis=0,
        )
        here = pl.ds(2 * q, 2)
        s3[f, here, :, 0:C] = pltpu.roll(state, 1, 1).astype(BF)
        s3[f, here, :, C : 2 * C] = pltpu.roll(state, cols - 1, 1).astype(BF)
        s3[f, here, :, 2 * C : 3 * C] = state.astype(BF)

    def finish(f, p, size, result):
        result = result.reshape(size, cols, 2 * C)
        result = jnp.stack([result[:, :, :C], result[:, :, C:]], axis=1).reshape(2 * size, cols, C)
        mixed = result + skip[...] * x[f, pl.ds(2 + 2 * p, 2 * size)].astype(F32)
        ot[0, f, pl.ds(16 * p, 16 * size)] = mixed[:, :8].reshape(16 * size, C)
        ot[1, f, pl.ds(16 * p, 16 * size)] = mixed[:, cols - 8 :].reshape(16 * size, C)
        o[f, pl.ds(2 * p, 2 * size), 8 : cols - 8] = mixed[:, 8 : cols - 8].astype(BF)

    wloads[3].wait()
    pair_weights(w2, pw2)
    side_weights(w1, sw1, SIDE_IN)
    side_weights(w2, sw2, SIDE_OUT)
    for c in hands:
        c.wait_recv()
    inner = [(1, half - 1), (half, half - 1)]
    for f in range(count):
        for q in range(1, pairs):
            settle(f, q)
        for p, size in inner:
            finish(f, p, size, mm(pair_rows([s3[f, 2 * p : 2 * p + 2 * size + 2]], size), pw2[...]))

    for c in sends:
        c.wait_recv()
    for s in range(2):
        lhs = jnp.concatenate([z[s, n].reshape(count * span, C) for n in range(3)], axis=-1)
        result = mm(lhs, sw1[s])
        for a in range(3):
            y[s, a] = result[:, a * 2 * C : (a + 1) * 2 * C].reshape(count, span, 2 * C)
    for f in range(count):
        widen(f, 0, 2, jnp.logical_not(at_top))
        widen(f, rows + 2, 2, jnp.logical_not(at_bottom))
    lhs = [
        pair_rows([x3[f, 2 * q : 2 * q + 4], x[f, 2 * q : 2 * q + 4]], 1) for q in (0, pairs) for f in range(count)
    ]
    drive = mm(jnp.concatenate(lhs, axis=0), pw1[...])
    for n, q in enumerate((0, pairs)):
        for f in range(count):
            recur(f, q, 1, drive[(n * count + f) * cols : (n * count + f + 1) * cols])
    late_hands[0].start()
    late_hands[1].start()

    @pl.when(at_top)
    def _():
        y[:, 0, :, 8:TOP] = jnp.zeros((2, count, TOP - 8, 2 * C), F32)

    @pl.when(at_bottom)
    def _():
        y[:, 2, :, TOP + rows : TOP + rows + 8] = jnp.zeros((2, count, 8, 2 * C), F32)

    for s in range(2):
        inside = jnp.where(column > 0 if s == 0 else column < tcols - 1, 1.0, 0.0).astype(F32)
        for f in range(count):
            own[s, f, 7 : rows + 9] = loc[f, pl.ds(s * (cols - 1), rows + 2, stride=cols), :]
        for e in range(2):
            lanes = slice(e * C, (e + 1) * C)
            state = None
            for f in range(count):
                drive = (
                    y[s, 0, f, 7 : 7 + tall, lanes] + y[s, 1, f, 8 : 8 + tall, lanes] + y[s, 2, f, 9 : 9 + tall, lanes]
                ) * inside
                state = drive if f == 0 else decay[f : f + 1, :] * state + drive
                whole = state + own[s, f] if e == 1 else state
                ss[s, e, f] = whole
            so[s, e] = whole.astype(BF)
    late_hands[2].start()
    for c in late_hands:
        c.wait_recv()

    place = lax.broadcasted_iota(jnp.int32, (tall, C), 0)
    off = jnp.logical_or(
        jnp.logical_and(place == 7, at_top), jnp.logical_and(place == rows + 8, at_bottom)
    )
    for s in range(2):
        sides = []
        for f in range(count):
            both = [
                jnp.where(off, 0.0, ss[s, e, f] + factors[f] * si[s, e].astype(F32)).astype(BF) for e in range(2)
            ]
            sides.append(jnp.concatenate(both, axis=-1))
        result = mm(jnp.concatenate(sides, axis=0), sw2[s])
        for a in range(3):
            y2[s, a] = result[:, a * 2 * C : (a + 1) * 2 * C].reshape(count, tall, 2 * C)
    for f in range(count):
        settle(f, 0, (jnp.logical_not(at_top), None))
        settle(f, pairs, (None, jnp.logical_not(at_bottom)))
    lhs = [pair_rows([s3[f, 2 * p : 2 * p + 4]], 1) for p in (0, pairs - 1) for f in range(count)]
    result = mm(jnp.concatenate(lhs, axis=0), pw2[...])
    for n, p in enumerate((0, pairs - 1)):
        for f in range(count):
            finish(f, p, 1, result[(n * count + f) * cols : (n * count + f + 1) * cols])

    for f in range(count):
        for s in range(2):
            for e in range(2):
                lanes = slice(e * C, (e + 1) * C)
                here = pl.ds(e if s == 0 else 7 - e, rows, stride=8)
                fix = (
                    y2[s, 0, f, 7 : 7 + rows, lanes] + y2[s, 1, f, 8 : 8 + rows, lanes] + y2[s, 2, f, 9 : 9 + rows, lanes]
                )
                ot[s, f, here, :] = ot[s, f, here, :] + fix
        o[f, :, 0:8] = ot[0, f].reshape(rows, 8, C).astype(BF)
        o[f, :, cols - 8 :] = ot[1, f].reshape(rows, 8, C).astype(BF)

    for c in sends + hands + late_hands:
        c.wait_send()


def write_out(o, out, sem):
    stores = [pltpu.make_async_copy(o.at[f], out.at[f], sem.at[f]) for f in range(o.shape[0])]
    for c in stores:
        c.start()
    for c in stores:
        c.wait()


def per_device(frames, w_in, w_out, decay, skip):
    count, _, rows, cols, _ = frames.shape
    pairs = rows // 2
    span = rows + 2 * TOP
    tall = rows + 16
    hbm = pl.BlockSpec(memory_space=pltpu.HBM)
    vmem = pl.BlockSpec(memory_space=pltpu.VMEM)
    args = (frames[:, 0], w_in, w_out, decay, skip.reshape(1, C))
    out = pl.pallas_call(
        functools.partial(kernel, TROWS),
        out_shape=pltpu.VMEM((count, rows, cols, C), BF),
        in_specs=[hbm] * 5,
        out_specs=vmem,
        scratch_shapes=[
            pltpu.VMEM((count, rows + 4, cols, C), BF),
            pltpu.VMEM((count, rows + 4, cols, 2 * C), BF),
            pltpu.VMEM((count, rows + 2, cols, 3 * C), BF),
            pltpu.VMEM((count, (rows + 8) * cols, C), F32),
            pltpu.VMEM((3, 3, C, C), BF),
            pltpu.VMEM((3, 3, C, C), BF),
            pltpu.VMEM((12 * C, 2 * C), BF),
            pltpu.VMEM((12 * C, 2 * C), BF),
            pltpu.VMEM((2, 3 * C, 6 * C), BF),
            pltpu.VMEM((2, 2 * C, 6 * C), BF),
            pltpu.VMEM((2, 2, count, rows, C), BF),
            pltpu.VMEM((2, 3, count, span, C), BF),
            pltpu.VMEM((2, 3, count, span, 2 * C), F32),
            pltpu.VMEM((2, 3, count, tall, 2 * C), F32),
            pltpu.VMEM((2, 2, count, tall, C), F32),
            pltpu.VMEM((2, count, tall, C), F32),
            pltpu.VMEM((2, rows * 8, C), F32),
            pltpu.VMEM((pairs + 1, 2, cols, C), BF),
            pltpu.VMEM((pairs + 1, 2, cols, C), BF),
            pltpu.VMEM((2, 2, tall, C), BF),
            pltpu.VMEM((2, 2, tall, C), BF),
            pltpu.VMEM((2, count, rows * 8, C), F32),
            pltpu.VMEM((count, C), F32),
            pltpu.VMEM((1, C), F32),
            pltpu.SemaphoreType.DMA((count,)),
            pltpu.SemaphoreType.DMA((4,)),
            pltpu.SemaphoreType.DMA((10,)),
            pltpu.SemaphoreType.DMA((10,)),
            pltpu.SemaphoreType.DMA((5,)),
            pltpu.SemaphoreType.DMA((5,)),
        ],
        compiler_params=pltpu.CompilerParams(
            collective_id=0, has_side_effects=True, vmem_limit_bytes=48 * 2**20
        ),
    )(*(pltpu.with_memory_space_constraint(a, pltpu.HBM) for a in args))
    out = pl.pallas_call(
        write_out,
        out_shape=jax.ShapeDtypeStruct(out.shape, BF),
        in_specs=[vmem],
        out_specs=hbm,
        scratch_shapes=[pltpu.SemaphoreType.DMA((count,))],
        compiler_params=pltpu.CompilerParams(vmem_limit_bytes=2**20),
    )(pltpu.with_memory_space_constraint(out, pltpu.VMEM))
    return out.reshape(count, 1, rows, cols, C)


def solution(mesh):
    return jax.shard_map(
        per_device,
        mesh=mesh,
        in_specs=(P("tm", "tile", None, None, None), P(), P(), P("tm", None), P()),
        out_specs=P("tm", "tile", None, None, None),
        check_vma=False,
    )
```

```python
import functools

import jax
import jax.numpy as jnp
from jax import lax
from jax.experimental import pallas as pl
from jax.experimental.pallas import tpu as pltpu
from jax.sharding import PartitionSpec as P

TROWS = 4
C = 128
BF = jnp.bfloat16
F32 = jnp.float32
MESH = pl.DeviceIdType.MESH

TAPS = 3


def mm(lhs, rhs):
    return jnp.dot(lhs, rhs, preferred_element_type=F32)


def mm_halves(lhs, rhs):
    half = lhs.shape[1] // 2
    return mm(lhs[:, :half], rhs[:half]) + mm(lhs[:, half:], rhs[half:])


def pair_weights(w, pair):
    zero = jnp.zeros((TAPS, C, C), BF)
    pair[3 * TAPS : 4 * TAPS, :, 0:C] = zero
    pair[0:TAPS, :, C : 2 * C] = zero
    return [
        (w.at[i], pair.at[pl.ds((i + e) * TAPS, TAPS), :, pl.ds(e * C, C)]) for i in range(TAPS) for e in range(2)
    ]


def side_weights(w, side, table):
    copies = []
    for s in range(2):
        for k, taps in enumerate(table[s]):
            for e, b in enumerate(taps):
                if b is None:
                    side[s, :, k, :, e * C : (e + 1) * C] = jnp.zeros((TAPS, C, C), BF)
                else:
                    copies.append((w.at[:, b], side.at[s, :, k, :, pl.ds(e * C, C)]))
    return copies


SIDE_IN = (((1, 0), (0, None), (2, None)), ((1, 2), (2, None), (0, None)))
SIDE_OUT = (((0, None), (1, 0)), ((2, None), (1, 2)))


def pair_rows(parts, pairs):
    cols = parts[0].shape[1]
    split = [p.reshape(pairs + 1, 2, cols, p.shape[2]) for p in parts]
    taps = []
    for first in (0, 1):
        for parity in (0, 1):
            taps += [p[first : first + pairs, parity] for p in split]
    return jnp.concatenate(taps, axis=-1).reshape(pairs * cols, 12 * C)


def kernel(
    trows, frames, w_in, w_out, decay_in, skip_in, o,
    x, x3, s3, loc, pw1, pw2, sw1, sw2, edge, corner, z, zc, y, y2, ss, stage, cstage, rim, lo, inc, so, si, ot, decay, skip,
    load_sem, w_sem, send_sem, recv_sem, tsend_sem, trecv_sem,
):
    count, rows, cols, _ = frames.shape
    tiles = lax.axis_size("tile")
    tcols = tiles // trows
    me = lax.axis_index("tile")
    tm = lax.axis_index("tm")
    k = lax.rem(me + tiles - 1, tiles)
    column = lax.rem(k, tcols)
    row_index = k // tcols
    up, down = row_index > 0, row_index < trows - 1
    left, right = column > 0, column < tcols - 1
    pairs = rows // 2
    tall = rows + 16

    loads = [
        pltpu.make_async_copy(frames.at[f], x.at[f, pl.ds(2, rows)], load_sem.at[f])
        for f in range(count)
    ]
    for c in loads:
        c.start()

    both = jnp.logical_and
    around = [
        (-1, left), (1, right), (-tcols, up), (tcols, down),
        (-tcols - 1, both(up, left)), (-tcols + 1, both(up, right)),
        (tcols - 1, both(down, left)), (tcols + 1, both(down, right)),
    ]

    def at(by):
        return lax.rem(me + by + tiles, tiles)

    barrier = pltpu.get_barrier_semaphore()
    greeted = jnp.int32(1)
    for by, there in around:
        greeted = greeted + there.astype(jnp.int32)

        @pl.when(there)
        def _():
            pl.semaphore_signal(barrier, inc=1, device_id=(tm, at(by)), device_id_type=MESH)

    pl.semaphore_signal(barrier, inc=1, device_id=(1 - tm, me), device_id_type=MESH)

    placed = pair_weights(w_in, pw1) + [(decay_in, decay), (skip_in, skip)]
    first_needed = len(placed)
    placed += pair_weights(w_out, pw2)
    then_needed = len(placed)
    placed += side_weights(w_in, sw1, SIDE_IN) + side_weights(w_out, sw2, SIDE_OUT)
    placed = [pltpu.make_async_copy(src, dst, w_sem.at[i]) for i, (src, dst) in enumerate(placed)]
    for c in placed:
        c.start()

    for f in range(count):
        loads[f].wait()
        stage[0] = x[f, 2 : 2 + rows, 0:16, :].astype(F32)[:, 0:8, :].reshape(rows * 8, C)
        stage[1] = x[f, 2 : 2 + rows, cols - 16 : cols, :].astype(F32)[:, 8:16, :].reshape(rows * 8, C)
        for s in range(2):
            for n in range(2):
                offset = n if s == 0 else 7 - n
                edge[s, n, f] = stage[s, pl.ds(offset, rows, stride=8), :].astype(BF)
                for t in range(2):
                    ends = pl.ds(offset + t * (rows - 2) * 8, 2, stride=8)
                    cstage[s, t, n, 2 * f : 2 * f + 2] = stage[s, ends, :]
    rest = jnp.zeros((8, C), F32)
    for s in range(2):
        for t in range(2):
            for n in range(2):
                corner[s, t, n] = jnp.concatenate([cstage[s, t, n], rest], axis=0).astype(BF)

    plan = [
        (edge.at[0], z.at[1]),
        (edge.at[1], z.at[0]),
        (frames.at[:, pl.ds(0, 2)], x.at[:, pl.ds(rows + 2, 2)]),
        (frames.at[:, pl.ds(rows - 2, 2)], x.at[:, pl.ds(0, 2)]),
        (corner.at[0, 0], zc.at[1, 1]),
        (corner.at[1, 0], zc.at[0, 1]),
        (corner.at[0, 1], zc.at[1, 0]),
        (corner.at[1, 1], zc.at[0, 0]),
    ]
    sends = [
        pltpu.make_async_remote_copy(
            src_ref=src, dst_ref=dst, send_sem=send_sem.at[i], recv_sem=recv_sem.at[i],
            device_id=(tm, at(around[i][0])), device_id_type=MESH,
        )
        for i, (src, dst) in enumerate(plan)
    ]
    comes = [around[i ^ 1][1] if i < 4 else around[11 - i][1] for i in range(8)]
    for i, (_, dst) in enumerate(plan):
        @pl.when(jnp.logical_not(comes[i]))
        def _():
            dst[...] = jnp.zeros(dst.shape, BF)

    in_tile = lax.broadcasted_iota(jnp.int32, (1, 8, C), 1)

    def widen(f, start, size):
        wide = x[f, pl.ds(start, size)].astype(F32)
        no_last = jnp.concatenate([wide[:, : cols - 8], jnp.where(in_tile == 7, 0.0, wide[:, cols - 8 :])], axis=1)
        no_first = jnp.concatenate([jnp.where(in_tile == 0, 0.0, wide[:, :8]), wide[:, 8:]], axis=1)
        x3[f, pl.ds(start, size), :, 0:C] = pltpu.roll(no_last, 1, 1).astype(BF)
        x3[f, pl.ds(start, size), :, C : 2 * C] = pltpu.roll(no_first, cols - 1, 1).astype(BF)
        return wide

    def frame_rows(f, here):
        return [x3[f, here, :, 0:C], x[f, here], x3[f, here, :, C : 2 * C]]

    def exchange(i, src, dst):
        return pltpu.make_async_remote_copy(
            src_ref=src, dst_ref=dst, send_sem=tsend_sem.at[i], recv_sem=trecv_sem.at[i],
            device_id=(1 - tm, me), device_id_type=MESH,
        )

    half = pairs // 2
    chunks = [(1, half), (1 + half, pairs - 1 - half)]
    hands = [exchange(n, lo.at[pl.ds(q, size)], inc.at[pl.ds(q, size)]) for n, (q, size) in enumerate(chunks)]
    late_hands = [
        exchange(2, lo.at[pl.ds(0, 1)], inc.at[pl.ds(0, 1)]),
        exchange(3, lo.at[pl.ds(pairs, 1)], inc.at[pl.ds(pairs, 1)]),
        exchange(4, so, si),
    ]
    weights1 = pw1.reshape(4 * TAPS * C, 2 * C)
    weights2 = pw2.reshape(4 * TAPS * C, 2 * C)

    def loc_rows(q, size):
        return pl.ds((2 * q + 7) * cols, size * 2 * cols)

    def recur(f, q, size, drive):
        drive = drive.reshape(size, cols, 2 * C)
        drive = jnp.stack([drive[:, :, :C], drive[:, :, C:]], axis=1).reshape(size * 2 * cols, C)
        here = loc_rows(q, size)
        if f > 0:
            drive = decay[f : f + 1, :] * loc[f - 1, here] + drive
        loc[f, here] = drive
        if f == count - 1:
            lo[pl.ds(q, size)] = drive.astype(BF).reshape(size, 2, cols, C)

    greet_at = jnp.where(me == 0, 1, 0)

    @pl.loop(0, 2)
    def _(step):
        @pl.when(step == greet_at)
        def _():
            pl.semaphore_wait(barrier, greeted)
            for i, c in enumerate(sends):
                pl.when(around[i][1])(c.start)

        @pl.when(step != greet_at)
        def _():
            for c in placed[:first_needed]:
                c.wait()
            for n, (q, size) in enumerate(chunks):
                for f in range(count):
                    end = rows + 2 if n else 2 * half + 4
                    for start in range(2 + n * (2 * half + 2), end, 2):
                        widen(f, start, 2)
                    lhs = pair_rows(frame_rows(f, pl.ds(2 * q, 2 * size + 2)), size)
                    recur(f, q, size, mm(lhs, weights1[...]))
                if n == 0:
                    pl.when(greet_at == 0)(hands[0].start)

    pl.when(greet_at == 1)(hands[0].start)
    hands[1].start()

    factors = []
    for f in range(count):
        keep = decay[f : f + 1, :]
        factors.append(keep * jnp.where(tm == 0, 0.0, 1.0) if f == 0 else factors[-1] * keep)

    def settle(f, q, real=(None, None)):
        state = loc[f, loc_rows(q, 1)].reshape(2, cols, C) + factors[f] * inc[q].astype(F32)
        first = jnp.where(in_tile == 0, 0.0, state[:, :8])
        last = jnp.where(in_tile == 7, 0.0, state[:, cols - 8 :])
        state = jnp.concatenate([first, state[:, 8 : cols - 8], last], axis=1)
        state = jnp.concatenate(
            [state[e : e + 1] if r is None else jnp.where(r, state[e : e + 1], 0.0) for e, r in enumerate(real)],
            axis=0,
        )
        here = pl.ds(2 * q, 2)
        s3[f, here, :, 0:C] = pltpu.roll(state, 1, 1).astype(BF)
        s3[f, here, :, C : 2 * C] = state.astype(BF)
        s3[f, here, :, 2 * C : 3 * C] = pltpu.roll(state, cols - 1, 1).astype(BF)

    def finish(f, p, size, result):
        result = result.reshape(size, cols, 2 * C)
        result = jnp.stack([result[:, :, :C], result[:, :, C:]], axis=1).reshape(2 * size, cols, C)
        mixed = result + skip[...] * x[f, pl.ds(2 + 2 * p, 2 * size)].astype(F32)
        ot[0, f, pl.ds(16 * p, 16 * size)] = mixed[:, :8].reshape(16 * size, C)
        ot[1, f, pl.ds(16 * p, 16 * size)] = mixed[:, cols - 8 :].reshape(16 * size, C)
        o[f, pl.ds(2 * p, 2 * size), 8 : cols - 8] = mixed[:, 8 : cols - 8].astype(BF)

    for c in placed[first_needed:then_needed]:
        c.wait()
    inner = [(1, half - 1), (half, half - 1)]
    for n, (q, size) in enumerate(chunks):
        hands[n].wait_recv()
        p, deep = inner[n]
        for f in range(count):
            for i in range(q, q + size):
                settle(f, i)
            lhs = pair_rows([s3[f, 2 * p : 2 * p + 2 * deep + 2]], deep)
            finish(f, p, deep, mm(lhs, weights2[...]))

    for c in placed[then_needed:]:
        c.wait()
    for i, c in enumerate(sends):
        pl.when(comes[i])(c.wait_recv)
    for f in range(count):
        for t in range(2):
            wide = widen(f, t * (rows + 2), 2)
            rim[t, 0, 16 * f : 16 * f + 16] = wide[:, :8].reshape(16, C)
            rim[t, 1, 16 * f : 16 * f + 16] = wide[:, cols - 8 :].reshape(16, C)
    lhs = [pair_rows(frame_rows(f, pl.ds(2 * q, 4)), 1) for q in (0, pairs) for f in range(count)]
    drive = mm_halves(jnp.concatenate(lhs, axis=0), weights1[...])
    for n, q in enumerate((0, pairs)):
        for f in range(count):
            recur(f, q, 1, drive[(n * count + f) * cols : (n * count + f + 1) * cols])
    late_hands[0].start()
    late_hands[1].start()

    for s in range(2):
        lines = [jnp.concatenate([z[s, 0, f], z[s, 1, f], edge[s, 0, f]], axis=-1) for f in range(count)]
        for t in range(2):
            mine = jnp.concatenate([rim[t, s, pl.ds(7 * s, 8, stride=8), :], rest], axis=0).astype(BF)
            lines.append(jnp.concatenate([zc[s, t, 0], zc[s, t, 1], mine], axis=-1))
        lhs = jnp.concatenate(lines, axis=0)
        for a in range(3):
            result = mm(lhs, sw1[s, a].reshape(3 * C, 2 * C))
            for e in range(2):
                part = result[:, e * C : (e + 1) * C]
                for f in range(count):
                    base = 2 * (8 + f * tall)
                    y[s, a, e, pl.ds(base + 16, rows, stride=2), :] = part[f * rows : (f + 1) * rows]
                    for t in range(2):
                        begin = count * rows + 16 * t + 2 * f
                        y[s, a, e, pl.ds(base + 12 + t * 2 * (rows + 2), 2, stride=2), :] = part[begin : begin + 2]

    for s in range(2):
        inside = jnp.where(left if s == 0 else right, 1.0, 0.0).astype(F32)
        for e in range(2):
            state = None
            for f in range(count):
                base = 2 * (8 + f * tall)
                drive = sum(y[s, a, e, pl.ds(base + 2 * (a - 1), tall, stride=2), :] for a in range(3))
                if e == 0:
                    drive = drive * inside
                state = drive if f == 0 else decay[f : f + 1, :] * state + drive
                whole = state
                if e == 1:
                    whole = state + loc[f, pl.ds(s * (cols - 1), tall, stride=cols), :]
                ss[s, e, f] = whole
            so[s, e] = whole.astype(BF)
    late_hands[2].start()
    late_hands[0].wait_recv()
    late_hands[1].wait_recv()
    for f in range(count):
        settle(f, 0, (up, None))
        settle(f, pairs, (None, down))
    lhs = [pair_rows([s3[f, 2 * p : 2 * p + 4]], 1) for p in (0, pairs - 1) for f in range(count)]
    result = mm_halves(jnp.concatenate(lhs, axis=0), weights2[...])
    for n, p in enumerate((0, pairs - 1)):
        for f in range(count):
            finish(f, p, 1, result[(n * count + f) * cols : (n * count + f + 1) * cols])

    late_hands[2].wait_recv()
    place = lax.broadcasted_iota(jnp.int32, (tall, C), 0)
    off = jnp.logical_or(
        both(place == 7, jnp.logical_not(up)), both(place == rows + 8, jnp.logical_not(down))
    )
    for s in range(2):
        sides = []
        for f in range(count):
            pair = [
                jnp.where(off, 0.0, ss[s, e, f] + factors[f] * si[s, e].astype(F32)).astype(BF) for e in range(2)
            ]
            sides.append(jnp.concatenate(pair, axis=-1))
        lhs = jnp.concatenate(sides, axis=0)
        for a in range(3):
            result = mm(lhs, sw2[s, a].reshape(2 * C, 2 * C))
            for e in range(2):
                y2[s, a, e, pl.ds(16, count * tall, stride=2), :] = result[:, e * C : (e + 1) * C]

    for f in range(count):
        base = 2 * (8 + f * tall + 8)
        for s in range(2):
            for e in range(2):
                here = pl.ds(e if s == 0 else 7 - e, rows, stride=8)
                fix = sum(y2[s, a, e, pl.ds(base + 2 * (a - 1), rows, stride=2), :] for a in range(3))
                ot[s, f, here, :] = ot[s, f, here, :] + fix
        o[f, :, 0:8] = ot[0, f].reshape(rows, 8, C).astype(BF)
        o[f, :, cols - 8 :] = ot[1, f].reshape(rows, 8, C).astype(BF)

    for i, c in enumerate(sends):
        pl.when(around[i][1])(c.wait_send)
    for c in hands + late_hands:
        c.wait_send()


def write_out(o, out, sem):
    stores = [pltpu.make_async_copy(o.at[f], out.at[f], sem.at[f]) for f in range(o.shape[0])]
    for c in stores:
        c.start()
    for c in stores:
        c.wait()


def per_device(frames, w_in, w_out, decay, skip):
    count, _, rows, cols, _ = frames.shape
    tall = rows + 16
    spread = 2 * (count * tall + 16)
    hbm = pl.BlockSpec(memory_space=pltpu.HBM)
    vmem = pl.BlockSpec(memory_space=pltpu.VMEM)
    args = (frames[:, 0], w_in, w_out, decay, skip.reshape(1, C))
    out = pl.pallas_call(
        functools.partial(kernel, TROWS),
        out_shape=pltpu.VMEM((count, rows, cols, C), BF),
        in_specs=[hbm] * 5,
        out_specs=vmem,
        scratch_shapes=[
            pltpu.VMEM((count, rows + 4, cols, C), BF),
            pltpu.VMEM((count, rows + 4, cols, 2 * C), BF),
            pltpu.VMEM((count, rows + 2, cols, 3 * C), BF),
            pltpu.VMEM((count, tall * cols, C), F32),
            pltpu.VMEM((4 * TAPS, C, 2 * C), BF),
            pltpu.VMEM((4 * TAPS, C, 2 * C), BF),
            pltpu.VMEM((2, TAPS, 3, C, 2 * C), BF),
            pltpu.VMEM((2, TAPS, 2, C, 2 * C), BF),
            pltpu.VMEM((2, 2, count, rows, C), BF),
            pltpu.VMEM((2, 2, 2, 16, C), BF),
            pltpu.VMEM((2, 2, count, rows, C), BF),
            pltpu.VMEM((2, 2, 2, 16, C), BF),
            pltpu.VMEM((2, TAPS, 2, spread, C), F32),
            pltpu.VMEM((2, TAPS, 2, spread, C), F32),
            pltpu.VMEM((2, 2, count, tall, C), F32),
            pltpu.VMEM((2, rows * 8, C), F32),
            pltpu.VMEM((2, 2, 2, 8, C), F32),
            pltpu.VMEM((2, 2, 16 * count, C), F32),
            pltpu.VMEM((rows // 2 + 1, 2, cols, C), BF),
            pltpu.VMEM((rows // 2 + 1, 2, cols, C), BF),
            pltpu.VMEM((2, 2, tall, C), BF),
            pltpu.VMEM((2, 2, tall, C), BF),
            pltpu.VMEM((2, count, rows * 8, C), F32),
            pltpu.VMEM((count, C), F32),
            pltpu.VMEM((1, C), F32),
            pltpu.SemaphoreType.DMA((count,)),
            pltpu.SemaphoreType.DMA((28,)),
            pltpu.SemaphoreType.DMA((8,)),
            pltpu.SemaphoreType.DMA((8,)),
            pltpu.SemaphoreType.DMA((5,)),
            pltpu.SemaphoreType.DMA((5,)),
        ],
        compiler_params=pltpu.CompilerParams(
            collective_id=0, has_side_effects=True, vmem_limit_bytes=48 * 2**20
        ),
    )(*(pltpu.with_memory_space_constraint(a, pltpu.HBM) for a in args))
    out = pl.pallas_call(
        write_out,
        out_shape=jax.ShapeDtypeStruct(out.shape, BF),
        in_specs=[vmem],
        out_specs=hbm,
        scratch_shapes=[pltpu.SemaphoreType.DMA((count,))],
        compiler_params=pltpu.CompilerParams(vmem_limit_bytes=2**20),
    )(pltpu.with_memory_space_constraint(out, pltpu.VMEM))
    return out.reshape(count, 1, rows, cols, C)


def solution(mesh):
    return jax.shard_map(
        per_device,
        mesh=mesh,
        in_specs=(P("tm", "tile", None, None, None), P(), P(), P("tm", None), P()),
        out_specs=P("tm", "tile", None, None, None),
        check_vma=False,
    )
```

```python
import functools

import jax
import jax.numpy as jnp
from jax import lax
from jax.experimental import pallas as pl
from jax.experimental.pallas import tpu as pltpu
from jax.sharding import PartitionSpec as P

TROWS = 4
LINE = 4
C = 128
BF = jnp.bfloat16
F32 = jnp.float32
MESH = pl.DeviceIdType.MESH

TAPS = 3


def mm(lhs, rhs):
    return jnp.dot(lhs, rhs, preferred_element_type=F32)


def mm_halves(lhs, rhs):
    half = lhs.shape[1] // 2
    return mm(lhs[:, :half], rhs[:half]) + mm(lhs[:, half:], rhs[half:])


def pair_weights(w, pair):
    zero = jnp.zeros((TAPS, C, C), BF)
    pair[3 * TAPS : 4 * TAPS, :, 0:C] = zero
    pair[0:TAPS, :, C : 2 * C] = zero
    return [
        (w.at[i], pair.at[pl.ds((i + e) * TAPS, TAPS), :, pl.ds(e * C, C)]) for i in range(TAPS) for e in range(2)
    ]


def side_weights(w, side, table):
    copies = []
    for s in range(2):
        for k, taps in enumerate(table[s]):
            for e, b in enumerate(taps):
                if b is None:
                    side[s, :, k, :, e * C : (e + 1) * C] = jnp.zeros((TAPS, C, C), BF)
                else:
                    copies.append((w.at[:, b], side.at[s, :, k, :, pl.ds(e * C, C)]))
    return copies


SIDE_IN = (((1, 0), (0, None), (2, None)), ((1, 2), (2, None), (0, None)))
SIDE_OUT = (((0, None), (1, 0)), ((2, None), (1, 2)))


def pair_rows(parts, pairs):
    cols = parts[0].shape[1]
    split = [p.reshape(pairs + 1, 2, cols, p.shape[2]) for p in parts]
    taps = []
    for first in (0, 1):
        for parity in (0, 1):
            taps += [p[first : first + pairs, parity] for p in split]
    return jnp.concatenate(taps, axis=-1).reshape(pairs * cols, 12 * C)


def kernel(
    trows, frames, w_in, w_out, decay_in, skip_in, o,
    x, x3, s3, loc, pw1, pw2, sw1, sw2, edge, corner, z, zc, y, y2, ss, stage, cstage, rim, lo, inc, so, si, ot, decay, skip,
    load_sem, w_sem, send_sem, recv_sem, tsend_sem, trecv_sem, far_sem,
):
    count, rows, cols, _ = frames.shape
    tiles = lax.axis_size("tile")
    tcols = tiles // trows
    me = lax.axis_index("tile")
    tm = lax.axis_index("tm")
    k = lax.rem(me + tiles - 1, tiles)
    column = lax.rem(k, tcols)
    row_index = k // tcols
    up, down = row_index > 0, row_index < trows - 1
    left, right = column > 0, column < tcols - 1
    pairs = rows // 2
    tall = rows + 16

    loads = [
        pltpu.make_async_copy(frames.at[f], x.at[f, pl.ds(2, rows)], load_sem.at[f])
        for f in range(count)
    ]
    for c in loads:
        c.start()

    both = jnp.logical_and
    around = [
        (-1, left), (1, right), (-tcols, up), (tcols, down),
        (-tcols - 1, both(up, left)), (-tcols + 1, both(up, right)),
        (tcols - 1, both(down, left)), (tcols + 1, both(down, right)),
    ]

    def at(by):
        return lax.rem(me + by + tiles, tiles)

    first = me == 0
    near = [both(there, jnp.logical_not(first)) if i in (0, 4) else there for i, (_, there) in enumerate(around)]
    to_first = {i: both(around[i][1], at(around[i][0]) == 0) for i in (1, 7)}

    barrier = pltpu.get_barrier_semaphore()
    greeted = jnp.int32(1)
    for i, (by, there) in enumerate(around):
        greeted = greeted + near[i].astype(jnp.int32)

        @pl.when(both(there, jnp.logical_not(to_first[i])) if i in to_first else there)
        def _():
            pl.semaphore_signal(barrier, inc=1, device_id=(tm, at(by)), device_id_type=MESH)

    pl.semaphore_signal(barrier, inc=1, device_id=(1 - tm, me), device_id_type=MESH)

    placed = pair_weights(w_in, pw1) + [(decay_in, decay), (skip_in, skip)]
    first_needed = len(placed)
    placed += pair_weights(w_out, pw2)
    then_needed = len(placed)
    placed += side_weights(w_in, sw1, SIDE_IN) + side_weights(w_out, sw2, SIDE_OUT)
    placed = [pltpu.make_async_copy(src, dst, w_sem.at[i]) for i, (src, dst) in enumerate(placed)]
    for c in placed:
        c.start()

    for f in range(count):
        loads[f].wait()
        stage[0] = x[f, 2 : 2 + rows, 0:16, :].astype(F32)[:, 0:8, :].reshape(rows * 8, C)
        stage[1] = x[f, 2 : 2 + rows, cols - 16 : cols, :].astype(F32)[:, 8:16, :].reshape(rows * 8, C)
        for s in range(2):
            for n in range(2):
                offset = n if s == 0 else 7 - n
                edge[s, n, f] = stage[s, pl.ds(offset, rows, stride=8), :].astype(BF)
                for t in range(2):
                    ends = pl.ds(offset + t * (rows - 2) * 8, 2, stride=8)
                    cstage[s, t, n, 2 * f : 2 * f + 2] = stage[s, ends, :]
    rest = jnp.zeros((8, C), F32)
    for s in range(2):
        for t in range(2):
            for n in range(2):
                corner[s, t, n] = jnp.concatenate([cstage[s, t, n], rest], axis=0).astype(BF)

    plan = [
        (edge.at[0], z.at[1]),
        (edge.at[1], z.at[0]),
        (frames.at[:, pl.ds(0, 2)], x.at[:, pl.ds(rows + 2, 2)]),
        (frames.at[:, pl.ds(rows - 2, 2)], x.at[:, pl.ds(0, 2)]),
        (corner.at[0, 0], zc.at[1, 1]),
        (corner.at[1, 0], zc.at[0, 1]),
        (corner.at[0, 1], zc.at[1, 0]),
        (corner.at[1, 1], zc.at[0, 0]),
    ]
    sends = [
        pltpu.make_async_remote_copy(
            src_ref=src, dst_ref=dst, send_sem=send_sem.at[i], recv_sem=recv_sem.at[i],
            device_id=(tm, at(around[i][0])), device_id_type=MESH,
        )
        for i, (src, dst) in enumerate(plan)
    ]
    comes = [around[i ^ 1][1] if i < 4 else around[11 - i][1] for i in range(8)]
    for i, (_, dst) in enumerate(plan):
        @pl.when(jnp.logical_not(comes[i]))
        def _():
            dst[...] = jnp.zeros(dst.shape, BF)

    in_tile = lax.broadcasted_iota(jnp.int32, (1, 8, C), 1)

    def widen(f, start, size):
        wide = x[f, pl.ds(start, size)].astype(F32)
        no_last = jnp.concatenate([wide[:, : cols - 8], jnp.where(in_tile == 7, 0.0, wide[:, cols - 8 :])], axis=1)
        no_first = jnp.concatenate([jnp.where(in_tile == 0, 0.0, wide[:, :8]), wide[:, 8:]], axis=1)
        x3[f, pl.ds(start, size), :, 0:C] = pltpu.roll(no_last, 1, 1).astype(BF)
        x3[f, pl.ds(start, size), :, C : 2 * C] = pltpu.roll(no_first, cols - 1, 1).astype(BF)
        return wide

    def frame_rows(f, here):
        return [x3[f, here, :, 0:C], x[f, here], x3[f, here, :, C : 2 * C]]

    def exchange(i, src, dst):
        return pltpu.make_async_remote_copy(
            src_ref=src, dst_ref=dst, send_sem=tsend_sem.at[i], recv_sem=trecv_sem.at[i],
            device_id=(1 - tm, me), device_id_type=MESH,
        )

    half = pairs // 2
    chunks = [(1, half), (1 + half, pairs - 1 - half)]
    hands = [exchange(n, lo.at[pl.ds(q, size)], inc.at[pl.ds(q, size)]) for n, (q, size) in enumerate(chunks)]
    late_hands = [
        exchange(2, lo.at[pl.ds(0, 1)], inc.at[pl.ds(0, 1)]),
        exchange(3, lo.at[pl.ds(pairs, 1)], inc.at[pl.ds(pairs, 1)]),
        exchange(4, so.at[0], si.at[0]),
        exchange(5, so.at[1], si.at[1]),
    ]
    weights1 = pw1.reshape(4 * TAPS * C, 2 * C)
    weights2 = pw2.reshape(4 * TAPS * C, 2 * C)

    def loc_rows(q, size):
        return pl.ds((2 * q + 7) * cols, size * 2 * cols)

    def recur(f, q, size, drive):
        drive = drive.reshape(size, cols, 2 * C)
        drive = jnp.stack([drive[:, :, :C], drive[:, :, C:]], axis=1).reshape(size * 2 * cols, C)
        here = loc_rows(q, size)
        if f > 0:
            drive = decay[f : f + 1, :] * loc[f - 1, here] + drive
        loc[f, here] = drive
        if f == count - 1:
            lo[pl.ds(q, size)] = drive.astype(BF).reshape(size, 2, cols, C)

    spot = lax.rem(me, LINE)
    long_way = {0: spot == 0, 1: spot == LINE - 1}
    greet_at = jnp.where(first, 1, 0)

    @pl.loop(0, 2)
    def _(step):
        @pl.when(step == greet_at)
        def _():
            pl.semaphore_wait(barrier, greeted)
            for i in (1, 0, 5, 7, 4, 6, 2, 3):
                pl.when(both(near[i], long_way[i]) if i in long_way else near[i])(sends[i].start)
            for i, there in to_first.items():
                @pl.when(there)
                def _():
                    pl.semaphore_signal(far_sem, inc=1, device_id=(tm, at(around[i][0])), device_id_type=MESH)

        @pl.when(step != greet_at)
        def _():
            for c in placed[:first_needed]:
                c.wait()
            for n, (q, size) in enumerate(chunks):
                for f in range(count):
                    end = rows + 2 if n else 2 * half + 4
                    for start in range(2 + n * (2 * half + 2), end, 2):
                        widen(f, start, 2)
                    lhs = pair_rows(frame_rows(f, pl.ds(2 * q, 2 * size + 2)), size)
                    recur(f, q, size, mm(lhs, weights1[...]))
                if n == 0:
                    pl.when(greet_at == 0)(hands[0].start)

    pl.when(greet_at == 1)(hands[0].start)
    hands[1].start()
    for i, far in long_way.items():
        pl.when(both(near[i], jnp.logical_not(far)))(sends[i].start)

    factors = []
    for f in range(count):
        keep = decay[f : f + 1, :]
        factors.append(keep * jnp.where(tm == 0, 0.0, 1.0) if f == 0 else factors[-1] * keep)

    def settle(f, q, real=(None, None)):
        state = loc[f, loc_rows(q, 1)].reshape(2, cols, C) + factors[f] * inc[q].astype(F32)
        first = jnp.where(in_tile == 0, 0.0, state[:, :8])
        last = jnp.where(in_tile == 7, 0.0, state[:, cols - 8 :])
        state = jnp.concatenate([first, state[:, 8 : cols - 8], last], axis=1)
        state = jnp.concatenate(
            [state[e : e + 1] if r is None else jnp.where(r, state[e : e + 1], 0.0) for e, r in enumerate(real)],
            axis=0,
        )
        here = pl.ds(2 * q, 2)
        s3[f, here, :, 0:C] = pltpu.roll(state, 1, 1).astype(BF)
        s3[f, here, :, C : 2 * C] = state.astype(BF)
        s3[f, here, :, 2 * C : 3 * C] = pltpu.roll(state, cols - 1, 1).astype(BF)

    def finish(f, p, size, result):
        result = result.reshape(size, cols, 2 * C)
        result = jnp.stack([result[:, :, :C], result[:, :, C:]], axis=1).reshape(2 * size, cols, C)
        mixed = result + skip[...] * x[f, pl.ds(2 + 2 * p, 2 * size)].astype(F32)
        ot[0, f, pl.ds(16 * p, 16 * size)] = mixed[:, :8].reshape(16 * size, C)
        ot[1, f, pl.ds(16 * p, 16 * size)] = mixed[:, cols - 8 :].reshape(16 * size, C)
        o[f, pl.ds(2 * p, 2 * size), 8 : cols - 8] = mixed[:, 8 : cols - 8].astype(BF)

    for c in placed[first_needed:then_needed]:
        c.wait()
    inner = [(1, half - 1), (half, half - 1)]
    for n, (q, size) in enumerate(chunks):
        hands[n].wait_recv()
        if n == 1:
            @pl.when(first)
            def _():
                pl.semaphore_wait(far_sem, 2)
                sends[0].start()
                sends[4].start()

        p, deep = inner[n]
        for f in range(count):
            for i in range(q, q + size):
                settle(f, i)
            lhs = pair_rows([s3[f, 2 * p : 2 * p + 2 * deep + 2]], deep)
            finish(f, p, deep, mm(lhs, weights2[...]))

    for c in placed[then_needed:]:
        c.wait()

    def arrive(*which):
        for i in which:
            pl.when(comes[i])(sends[i].wait_recv)

    def side_in(s):
        lines = [jnp.concatenate([z[s, 0, f], z[s, 1, f], edge[s, 0, f]], axis=-1) for f in range(count)]
        for t in range(2):
            mine = jnp.concatenate([rim[t, s, pl.ds(7 * s, 8, stride=8), :], rest], axis=0).astype(BF)
            lines.append(jnp.concatenate([zc[s, t, 0], zc[s, t, 1], mine], axis=-1))
        lhs = jnp.concatenate(lines, axis=0)
        for a in range(3):
            result = mm(lhs, sw1[s, a].reshape(3 * C, 2 * C))
            for e in range(2):
                part = result[:, e * C : (e + 1) * C]
                for f in range(count):
                    base = 2 * (8 + f * tall)
                    y[s, a, e, pl.ds(base + 16, rows, stride=2), :] = part[f * rows : (f + 1) * rows]
                    for t in range(2):
                        begin = count * rows + 16 * t + 2 * f
                        y[s, a, e, pl.ds(base + 12 + t * 2 * (rows + 2), 2, stride=2), :] = part[begin : begin + 2]

        inside = jnp.where(left if s == 0 else right, 1.0, 0.0).astype(F32)
        for e in range(2):
            state = None
            for f in range(count):
                base = 2 * (8 + f * tall)
                drive = sum(y[s, a, e, pl.ds(base + 2 * (a - 1), tall, stride=2), :] for a in range(3))
                if e == 0:
                    drive = drive * inside
                state = drive if f == 0 else decay[f : f + 1, :] * state + drive
                whole = state
                if e == 1:
                    whole = state + loc[f, pl.ds(s * (cols - 1), tall, stride=cols), :]
                ss[s, e, f] = whole
            so[s, e] = whole.astype(BF)
        late_hands[2 + s].start()

    place = lax.broadcasted_iota(jnp.int32, (tall, C), 0)
    off = jnp.logical_or(
        both(place == 7, jnp.logical_not(up)), both(place == rows + 8, jnp.logical_not(down))
    )

    def side_out(s):
        late_hands[2 + s].wait_recv()
        sides = []
        for f in range(count):
            pair = [
                jnp.where(off, 0.0, ss[s, e, f] + factors[f] * si[s, e].astype(F32)).astype(BF) for e in range(2)
            ]
            sides.append(jnp.concatenate(pair, axis=-1))
        lhs = jnp.concatenate(sides, axis=0)
        for a in range(3):
            result = mm(lhs, sw2[s, a].reshape(2 * C, 2 * C))
            for e in range(2):
                y2[s, a, e, pl.ds(16, count * tall, stride=2), :] = result[:, e * C : (e + 1) * C]
        for f in range(count):
            base = 2 * (8 + f * tall + 8)
            for e in range(2):
                here = pl.ds(e if s == 0 else 7 - e, rows, stride=8)
                fix = sum(y2[s, a, e, pl.ds(base + 2 * (a - 1), rows, stride=2), :] for a in range(3))
                ot[s, f, here, :] = ot[s, f, here, :] + fix
            begin = s * (cols - 8)
            o[f, :, begin : begin + 8] = ot[s, f].reshape(rows, 8, C).astype(BF)

    arrive(2, 3)
    for f in range(count):
        for t in range(2):
            wide = widen(f, t * (rows + 2), 2)
            rim[t, 0, 16 * f : 16 * f + 16] = wide[:, :8].reshape(16, C)
            rim[t, 1, 16 * f : 16 * f + 16] = wide[:, cols - 8 :].reshape(16, C)
    lhs = [pair_rows(frame_rows(f, pl.ds(2 * q, 4)), 1) for q in (0, pairs) for f in range(count)]
    drive = mm_halves(jnp.concatenate(lhs, axis=0), weights1[...])
    for n, q in enumerate((0, pairs)):
        for f in range(count):
            recur(f, q, 1, drive[(n * count + f) * cols : (n * count + f + 1) * cols])
    late_hands[0].start()
    late_hands[1].start()

    arrive(0, 4, 6)
    side_in(1)

    late_hands[0].wait_recv()
    late_hands[1].wait_recv()
    for f in range(count):
        settle(f, 0, (up, None))
        settle(f, pairs, (None, down))
    lhs = [pair_rows([s3[f, 2 * p : 2 * p + 4]], 1) for p in (0, pairs - 1) for f in range(count)]
    result = mm_halves(jnp.concatenate(lhs, axis=0), weights2[...])
    for n, p in enumerate((0, pairs - 1)):
        for f in range(count):
            finish(f, p, 1, result[(n * count + f) * cols : (n * count + f + 1) * cols])

    arrive(1, 5, 7)
    side_in(0)
    side_out(1)
    side_out(0)

    for i, c in enumerate(sends):
        pl.when(around[i][1])(c.wait_send)
    for c in hands + late_hands:
        c.wait_send()


def write_out(o, out, sem):
    stores = [pltpu.make_async_copy(o.at[f], out.at[f], sem.at[f]) for f in range(o.shape[0])]
    for c in stores:
        c.start()
    for c in stores:
        c.wait()


def per_device(frames, w_in, w_out, decay, skip):
    count, _, rows, cols, _ = frames.shape
    tall = rows + 16
    spread = 2 * (count * tall + 16)
    hbm = pl.BlockSpec(memory_space=pltpu.HBM)
    vmem = pl.BlockSpec(memory_space=pltpu.VMEM)
    args = (frames[:, 0], w_in, w_out, decay, skip.reshape(1, C))
    out = pl.pallas_call(
        functools.partial(kernel, TROWS),
        out_shape=pltpu.VMEM((count, rows, cols, C), BF),
        in_specs=[hbm] * 5,
        out_specs=vmem,
        scratch_shapes=[
            pltpu.VMEM((count, rows + 4, cols, C), BF),
            pltpu.VMEM((count, rows + 4, cols, 2 * C), BF),
            pltpu.VMEM((count, rows + 2, cols, 3 * C), BF),
            pltpu.VMEM((count, tall * cols, C), F32),
            pltpu.VMEM((4 * TAPS, C, 2 * C), BF),
            pltpu.VMEM((4 * TAPS, C, 2 * C), BF),
            pltpu.VMEM((2, TAPS, 3, C, 2 * C), BF),
            pltpu.VMEM((2, TAPS, 2, C, 2 * C), BF),
            pltpu.VMEM((2, 2, count, rows, C), BF),
            pltpu.VMEM((2, 2, 2, 16, C), BF),
            pltpu.VMEM((2, 2, count, rows, C), BF),
            pltpu.VMEM((2, 2, 2, 16, C), BF),
            pltpu.VMEM((2, TAPS, 2, spread, C), F32),
            pltpu.VMEM((2, TAPS, 2, spread, C), F32),
            pltpu.VMEM((2, 2, count, tall, C), F32),
            pltpu.VMEM((2, rows * 8, C), F32),
            pltpu.VMEM((2, 2, 2, 8, C), F32),
            pltpu.VMEM((2, 2, 16 * count, C), F32),
            pltpu.VMEM((rows // 2 + 1, 2, cols, C), BF),
            pltpu.VMEM((rows // 2 + 1, 2, cols, C), BF),
            pltpu.VMEM((2, 2, tall, C), BF),
            pltpu.VMEM((2, 2, tall, C), BF),
            pltpu.VMEM((2, count, rows * 8, C), F32),
            pltpu.VMEM((count, C), F32),
            pltpu.VMEM((1, C), F32),
            pltpu.SemaphoreType.DMA((count,)),
            pltpu.SemaphoreType.DMA((28,)),
            pltpu.SemaphoreType.DMA((8,)),
            pltpu.SemaphoreType.DMA((8,)),
            pltpu.SemaphoreType.DMA((6,)),
            pltpu.SemaphoreType.DMA((6,)),
            pltpu.SemaphoreType.REGULAR,
        ],
        compiler_params=pltpu.CompilerParams(
            collective_id=0, has_side_effects=True, vmem_limit_bytes=48 * 2**20
        ),
    )(*(pltpu.with_memory_space_constraint(a, pltpu.HBM) for a in args))
    out = pl.pallas_call(
        write_out,
        out_shape=jax.ShapeDtypeStruct(out.shape, BF),
        in_specs=[vmem],
        out_specs=hbm,
        scratch_shapes=[pltpu.SemaphoreType.DMA((count,))],
        compiler_params=pltpu.CompilerParams(vmem_limit_bytes=2**20),
    )(pltpu.with_memory_space_constraint(out, pltpu.VMEM))
    return out.reshape(count, 1, rows, cols, C)


def solution(mesh):
    return jax.shard_map(
        per_device,
        mesh=mesh,
        in_specs=(P("tm", "tile", None, None, None), P(), P(), P("tm", None), P()),
        out_specs=P("tm", "tile", None, None, None),
        check_vma=False,
    )
```

```python
import functools

import jax
import jax.numpy as jnp
from jax import lax
from jax.experimental import pallas as pl
from jax.experimental.pallas import tpu as pltpu
from jax.sharding import PartitionSpec as P

TROWS = 4
LINE = 4
C = 128
BF = jnp.bfloat16
F32 = jnp.float32
MESH = pl.DeviceIdType.MESH

TAPS = 3


def mm(lhs, rhs):
    return jnp.dot(lhs, rhs, preferred_element_type=F32)


def mm_halves(lhs, rhs):
    half = lhs.shape[1] // 2
    return mm(lhs[:, :half], rhs[:half]) + mm(lhs[:, half:], rhs[half:])


def pair_weights(w, pair):
    zero = jnp.zeros((TAPS, C, C), BF)
    pair[3 * TAPS : 4 * TAPS, :, 0:C] = zero
    pair[0:TAPS, :, C : 2 * C] = zero
    return [
        (w.at[i], pair.at[pl.ds((i + e) * TAPS, TAPS), :, pl.ds(e * C, C)]) for i in range(TAPS) for e in range(2)
    ]


def side_weights(w, side, table):
    copies = []
    for s in range(2):
        for k, taps in enumerate(table[s]):
            for e, b in enumerate(taps):
                if b is None:
                    side[s, :, k, :, e * C : (e + 1) * C] = jnp.zeros((TAPS, C, C), BF)
                else:
                    copies.append((w.at[:, b], side.at[s, :, k, :, pl.ds(e * C, C)]))
    return copies


SIDE_IN = (((1, 0), (0, None), (2, None)), ((1, 2), (2, None), (0, None)))
SIDE_OUT = (((0, None), (1, 0)), ((2, None), (1, 2)))


def pair_rows(parts, pairs):
    cols = parts[0].shape[1]
    split = [p.reshape(pairs + 1, 2, cols, p.shape[2]) for p in parts]
    taps = []
    for first in (0, 1):
        for parity in (0, 1):
            taps += [p[first : first + pairs, parity] for p in split]
    return jnp.concatenate(taps, axis=-1).reshape(pairs * cols, 12 * C)


def kernel(
    trows, frames, w_in, w_out, decay_in, skip_in, o,
    x, x3, s3, loc, pw1, pw2, sw1, sw2, edge, corner, z, zc, y, y2, ss, stage, cstage, rim, lo, inc, so, si, ot, decay, skip,
    load_sem, w_sem, send_sem, recv_sem, tsend_sem, trecv_sem, far_sem,
):
    count, rows, cols, _ = frames.shape
    tiles = lax.axis_size("tile")
    tcols = tiles // trows
    me = lax.axis_index("tile")
    tm = lax.axis_index("tm")
    k = lax.rem(me + tiles - 1, tiles)
    column = lax.rem(k, tcols)
    row_index = k // tcols
    up, down = row_index > 0, row_index < trows - 1
    left, right = column > 0, column < tcols - 1
    pairs = rows // 2
    tall = rows + 16

    loads = [
        pltpu.make_async_copy(frames.at[f], x.at[f, pl.ds(2, rows)], load_sem.at[f])
        for f in range(count)
    ]
    for c in loads:
        c.start()

    both = jnp.logical_and
    around = [
        (-1, left), (1, right), (-tcols, up), (tcols, down),
        (-tcols - 1, both(up, left)), (-tcols + 1, both(up, right)),
        (tcols - 1, both(down, left)), (tcols + 1, both(down, right)),
    ]

    def at(by):
        return lax.rem(me + by + tiles, tiles)

    first = me == 0
    near = [both(there, jnp.logical_not(first)) for _, there in around]
    to_first = [both(there, at(by) == 0) for by, there in around]

    barrier = pltpu.get_barrier_semaphore()
    greeted, far = jnp.int32(1), jnp.int32(0)
    for i, (by, there) in enumerate(around):
        greeted = greeted + near[i].astype(jnp.int32)
        far = far + both(there, first).astype(jnp.int32)

        @pl.when(both(there, jnp.logical_not(to_first[i])))
        def _():
            pl.semaphore_signal(barrier, inc=1, device_id=(tm, at(by)), device_id_type=MESH)

    pl.semaphore_signal(barrier, inc=1, device_id=(1 - tm, me), device_id_type=MESH)

    placed = pair_weights(w_in, pw1) + [(decay_in, decay), (skip_in, skip)]
    first_needed = len(placed)
    placed += pair_weights(w_out, pw2)
    then_needed = len(placed)
    placed += side_weights(w_in, sw1, SIDE_IN) + side_weights(w_out, sw2, SIDE_OUT)
    placed = [pltpu.make_async_copy(src, dst, w_sem.at[i]) for i, (src, dst) in enumerate(placed)]
    for c in placed:
        c.start()

    for f in range(count):
        loads[f].wait()
        stage[0] = x[f, 2 : 2 + rows, 0:16, :].astype(F32)[:, 0:8, :].reshape(rows * 8, C)
        stage[1] = x[f, 2 : 2 + rows, cols - 16 : cols, :].astype(F32)[:, 8:16, :].reshape(rows * 8, C)
        for s in range(2):
            for n in range(2):
                offset = n if s == 0 else 7 - n
                edge[s, n, f] = stage[s, pl.ds(offset, rows, stride=8), :].astype(BF)
                for t in range(2):
                    ends = pl.ds(offset + t * (rows - 2) * 8, 2, stride=8)
                    cstage[s, t, n, 2 * f : 2 * f + 2] = stage[s, ends, :]
    rest = jnp.zeros((8, C), F32)
    for s in range(2):
        for t in range(2):
            for n in range(2):
                corner[s, t, n] = jnp.concatenate([cstage[s, t, n], rest], axis=0).astype(BF)

    plan = [
        (edge.at[0], z.at[1]),
        (edge.at[1], z.at[0]),
        (frames.at[:, pl.ds(0, 2)], x.at[:, pl.ds(rows + 2, 2)]),
        (frames.at[:, pl.ds(rows - 2, 2)], x.at[:, pl.ds(0, 2)]),
        (corner.at[0, 0], zc.at[1, 1]),
        (corner.at[1, 0], zc.at[0, 1]),
        (corner.at[0, 1], zc.at[1, 0]),
        (corner.at[1, 1], zc.at[0, 0]),
    ]
    sends = [
        pltpu.make_async_remote_copy(
            src_ref=src, dst_ref=dst, send_sem=send_sem.at[i], recv_sem=recv_sem.at[i],
            device_id=(tm, at(around[i][0])), device_id_type=MESH,
        )
        for i, (src, dst) in enumerate(plan)
    ]
    comes = [around[i ^ 1][1] if i < 4 else around[11 - i][1] for i in range(8)]
    for i, (_, dst) in enumerate(plan):
        @pl.when(jnp.logical_not(comes[i]))
        def _():
            dst[...] = jnp.zeros(dst.shape, BF)

    in_tile = lax.broadcasted_iota(jnp.int32, (1, 8, C), 1)

    def widen(f, start, size):
        wide = x[f, pl.ds(start, size)].astype(F32)
        no_last = jnp.concatenate([wide[:, : cols - 8], jnp.where(in_tile == 7, 0.0, wide[:, cols - 8 :])], axis=1)
        no_first = jnp.concatenate([jnp.where(in_tile == 0, 0.0, wide[:, :8]), wide[:, 8:]], axis=1)
        x3[f, pl.ds(start, size), :, 0:C] = pltpu.roll(no_last, 1, 1).astype(BF)
        x3[f, pl.ds(start, size), :, C : 2 * C] = pltpu.roll(no_first, cols - 1, 1).astype(BF)
        return wide

    def frame_rows(f, here):
        return [x3[f, here, :, 0:C], x[f, here], x3[f, here, :, C : 2 * C]]

    def exchange(i, src, dst):
        return pltpu.make_async_remote_copy(
            src_ref=src, dst_ref=dst, send_sem=tsend_sem.at[i], recv_sem=trecv_sem.at[i],
            device_id=(1 - tm, me), device_id_type=MESH,
        )

    half = pairs // 2
    chunks = [(1, half), (1 + half, pairs - 1 - half)]
    hands = [exchange(n, lo.at[pl.ds(q, size)], inc.at[pl.ds(q, size)]) for n, (q, size) in enumerate(chunks)]
    late_hands = [
        exchange(2, lo.at[pl.ds(0, 1)], inc.at[pl.ds(0, 1)]),
        exchange(3, lo.at[pl.ds(pairs, 1)], inc.at[pl.ds(pairs, 1)]),
        exchange(4, so, si),
    ]
    weights1 = pw1.reshape(4 * TAPS * C, 2 * C)
    weights2 = pw2.reshape(4 * TAPS * C, 2 * C)

    def loc_rows(q, size):
        return pl.ds((2 * q + 7) * cols, size * 2 * cols)

    def recur(f, q, size, drive):
        drive = drive.reshape(size, cols, 2 * C)
        drive = jnp.stack([drive[:, :, :C], drive[:, :, C:]], axis=1).reshape(size * 2 * cols, C)
        here = loc_rows(q, size)
        if f > 0:
            drive = decay[f : f + 1, :] * loc[f - 1, here] + drive
        loc[f, here] = drive
        if f == count - 1:
            lo[pl.ds(q, size)] = drive.astype(BF).reshape(size, 2, cols, C)

    def first_conv(n):
        q, size = chunks[n]
        for f in range(count):
            end = rows + 2 if n else 2 * half + 4
            for start in range(2 + n * (2 * half + 2), end, 2):
                widen(f, start, 2)
            lhs = pair_rows(frame_rows(f, pl.ds(2 * q, 2 * size + 2)), size)
            recur(f, q, size, mm(lhs, weights1[...]))

    greet_at = jnp.where(lax.rem(me, LINE) == 0, 1, 0)

    @pl.loop(0, 2)
    def _(step):
        @pl.when(step == greet_at)
        def _():
            pl.semaphore_wait(barrier, greeted)
            for i in (1, 0, 5, 7, 4, 6, 2, 3):
                pl.when(near[i])(sends[i].start)
            for i, (by, _) in enumerate(around):
                @pl.when(to_first[i])
                def _():
                    pl.semaphore_signal(far_sem, inc=1, device_id=(tm, at(by)), device_id_type=MESH)

        @pl.when(step != greet_at)
        def _():
            for c in placed[:first_needed]:
                c.wait()
            first_conv(0)

    hands[0].start()
    first_conv(1)
    hands[1].start()

    factors = []
    for f in range(count):
        keep = decay[f : f + 1, :]
        factors.append(keep * jnp.where(tm == 0, 0.0, 1.0) if f == 0 else factors[-1] * keep)

    def settle(f, q, real=(None, None)):
        state = loc[f, loc_rows(q, 1)].reshape(2, cols, C) + factors[f] * inc[q].astype(F32)
        first = jnp.where(in_tile == 0, 0.0, state[:, :8])
        last = jnp.where(in_tile == 7, 0.0, state[:, cols - 8 :])
        state = jnp.concatenate([first, state[:, 8 : cols - 8], last], axis=1)
        state = jnp.concatenate(
            [state[e : e + 1] if r is None else jnp.where(r, state[e : e + 1], 0.0) for e, r in enumerate(real)],
            axis=0,
        )
        here = pl.ds(2 * q, 2)
        s3[f, here, :, 0:C] = pltpu.roll(state, 1, 1).astype(BF)
        s3[f, here, :, C : 2 * C] = state.astype(BF)
        s3[f, here, :, 2 * C : 3 * C] = pltpu.roll(state, cols - 1, 1).astype(BF)

    def finish(f, p, size, result):
        result = result.reshape(size, cols, 2 * C)
        result = jnp.stack([result[:, :, :C], result[:, :, C:]], axis=1).reshape(2 * size, cols, C)
        mixed = result + skip[...] * x[f, pl.ds(2 + 2 * p, 2 * size)].astype(F32)
        ot[0, f, pl.ds(16 * p, 16 * size)] = mixed[:, :8].reshape(16 * size, C)
        ot[1, f, pl.ds(16 * p, 16 * size)] = mixed[:, cols - 8 :].reshape(16 * size, C)
        o[f, pl.ds(2 * p, 2 * size), 8 : cols - 8] = mixed[:, 8 : cols - 8].astype(BF)

    for c in placed[first_needed:then_needed]:
        c.wait()
    inner = [(1, half - 1), (half, half - 1)]

    def second_conv(n):
        q, size = chunks[n]
        p, deep = inner[n]
        hands[n].wait_recv()
        for f in range(count):
            for i in range(q, q + size):
                settle(f, i)
            lhs = pair_rows([s3[f, 2 * p : 2 * p + 2 * deep + 2]], deep)
            finish(f, p, deep, mm(lhs, weights2[...]))

    second_conv(0)

    @pl.when(first)
    def _():
        pl.semaphore_wait(far_sem, far)
        for i, c in enumerate(sends):
            pl.when(around[i][1])(c.start)

    late_at = jnp.where(first, 1, 0)

    @pl.loop(0, 2)
    def _(step):
        @pl.when(step != late_at)
        def _():
            second_conv(1)

        @pl.when(step == late_at)
        def _():
            for c in placed[then_needed:]:
                c.wait()
            for i, c in enumerate(sends):
                pl.when(comes[i])(c.wait_recv)
            for f in range(count):
                for t in range(2):
                    wide = widen(f, t * (rows + 2), 2)
                    rim[t, 0, 16 * f : 16 * f + 16] = wide[:, :8].reshape(16, C)
                    rim[t, 1, 16 * f : 16 * f + 16] = wide[:, cols - 8 :].reshape(16, C)
            lhs = [pair_rows(frame_rows(f, pl.ds(2 * q, 4)), 1) for q in (0, pairs) for f in range(count)]
            drive = mm_halves(jnp.concatenate(lhs, axis=0), weights1[...])
            for n, q in enumerate((0, pairs)):
                for f in range(count):
                    recur(f, q, 1, drive[(n * count + f) * cols : (n * count + f + 1) * cols])
            late_hands[0].start()
            late_hands[1].start()

            for s in range(2):
                lines = [jnp.concatenate([z[s, 0, f], z[s, 1, f], edge[s, 0, f]], axis=-1) for f in range(count)]
                for t in range(2):
                    mine = jnp.concatenate([rim[t, s, pl.ds(7 * s, 8, stride=8), :], rest], axis=0).astype(BF)
                    lines.append(jnp.concatenate([zc[s, t, 0], zc[s, t, 1], mine], axis=-1))
                lhs = jnp.concatenate(lines, axis=0)
                for a in range(3):
                    result = mm(lhs, sw1[s, a].reshape(3 * C, 2 * C))
                    for e in range(2):
                        part = result[:, e * C : (e + 1) * C]
                        for f in range(count):
                            base = 2 * (8 + f * tall)
                            y[s, a, e, pl.ds(base + 16, rows, stride=2), :] = part[f * rows : (f + 1) * rows]
                            for t in range(2):
                                begin = count * rows + 16 * t + 2 * f
                                y[s, a, e, pl.ds(base + 12 + t * 2 * (rows + 2), 2, stride=2), :] = part[begin : begin + 2]

            for s in range(2):
                inside = jnp.where(left if s == 0 else right, 1.0, 0.0).astype(F32)
                for e in range(2):
                    state = None
                    for f in range(count):
                        base = 2 * (8 + f * tall)
                        drive = sum(y[s, a, e, pl.ds(base + 2 * (a - 1), tall, stride=2), :] for a in range(3))
                        if e == 0:
                            drive = drive * inside
                        state = drive if f == 0 else decay[f : f + 1, :] * state + drive
                        whole = state
                        if e == 1:
                            whole = state + loc[f, pl.ds(s * (cols - 1), tall, stride=cols), :]
                        ss[s, e, f] = whole
                    so[s, e] = whole.astype(BF)
            late_hands[2].start()
    late_hands[0].wait_recv()
    late_hands[1].wait_recv()
    for f in range(count):
        settle(f, 0, (up, None))
        settle(f, pairs, (None, down))
    lhs = [pair_rows([s3[f, 2 * p : 2 * p + 4]], 1) for p in (0, pairs - 1) for f in range(count)]
    result = mm_halves(jnp.concatenate(lhs, axis=0), weights2[...])
    for n, p in enumerate((0, pairs - 1)):
        for f in range(count):
            finish(f, p, 1, result[(n * count + f) * cols : (n * count + f + 1) * cols])

    late_hands[2].wait_recv()
    place = lax.broadcasted_iota(jnp.int32, (tall, C), 0)
    off = jnp.logical_or(
        both(place == 7, jnp.logical_not(up)), both(place == rows + 8, jnp.logical_not(down))
    )
    for s in range(2):
        sides = []
        for f in range(count):
            pair = [
                jnp.where(off, 0.0, ss[s, e, f] + factors[f] * si[s, e].astype(F32)).astype(BF) for e in range(2)
            ]
            sides.append(jnp.concatenate(pair, axis=-1))
        lhs = jnp.concatenate(sides, axis=0)
        for a in range(3):
            result = mm(lhs, sw2[s, a].reshape(2 * C, 2 * C))
            for e in range(2):
                y2[s, a, e, pl.ds(16, count * tall, stride=2), :] = result[:, e * C : (e + 1) * C]

    for f in range(count):
        base = 2 * (8 + f * tall + 8)
        for s in range(2):
            for e in range(2):
                here = pl.ds(e if s == 0 else 7 - e, rows, stride=8)
                fix = sum(y2[s, a, e, pl.ds(base + 2 * (a - 1), rows, stride=2), :] for a in range(3))
                ot[s, f, here, :] = ot[s, f, here, :] + fix
        o[f, :, 0:8] = ot[0, f].reshape(rows, 8, C).astype(BF)
        o[f, :, cols - 8 :] = ot[1, f].reshape(rows, 8, C).astype(BF)

    for i, c in enumerate(sends):
        pl.when(around[i][1])(c.wait_send)
    for c in hands + late_hands:
        c.wait_send()


def write_out(o, out, sem):
    stores = [pltpu.make_async_copy(o.at[f], out.at[f], sem.at[f]) for f in range(o.shape[0])]
    for c in stores:
        c.start()
    for c in stores:
        c.wait()


def per_device(frames, w_in, w_out, decay, skip):
    count, _, rows, cols, _ = frames.shape
    tall = rows + 16
    spread = 2 * (count * tall + 16)
    hbm = pl.BlockSpec(memory_space=pltpu.HBM)
    vmem = pl.BlockSpec(memory_space=pltpu.VMEM)
    args = (frames[:, 0], w_in, w_out, decay, skip.reshape(1, C))
    out = pl.pallas_call(
        functools.partial(kernel, TROWS),
        out_shape=pltpu.VMEM((count, rows, cols, C), BF),
        in_specs=[hbm] * 5,
        out_specs=vmem,
        scratch_shapes=[
            pltpu.VMEM((count, rows + 4, cols, C), BF),
            pltpu.VMEM((count, rows + 4, cols, 2 * C), BF),
            pltpu.VMEM((count, rows + 2, cols, 3 * C), BF),
            pltpu.VMEM((count, tall * cols, C), F32),
            pltpu.VMEM((4 * TAPS, C, 2 * C), BF),
            pltpu.VMEM((4 * TAPS, C, 2 * C), BF),
            pltpu.VMEM((2, TAPS, 3, C, 2 * C), BF),
            pltpu.VMEM((2, TAPS, 2, C, 2 * C), BF),
            pltpu.VMEM((2, 2, count, rows, C), BF),
            pltpu.VMEM((2, 2, 2, 16, C), BF),
            pltpu.VMEM((2, 2, count, rows, C), BF),
            pltpu.VMEM((2, 2, 2, 16, C), BF),
            pltpu.VMEM((2, TAPS, 2, spread, C), F32),
            pltpu.VMEM((2, TAPS, 2, spread, C), F32),
            pltpu.VMEM((2, 2, count, tall, C), F32),
            pltpu.VMEM((2, rows * 8, C), F32),
            pltpu.VMEM((2, 2, 2, 8, C), F32),
            pltpu.VMEM((2, 2, 16 * count, C), F32),
            pltpu.VMEM((rows // 2 + 1, 2, cols, C), BF),
            pltpu.VMEM((rows // 2 + 1, 2, cols, C), BF),
            pltpu.VMEM((2, 2, tall, C), BF),
            pltpu.VMEM((2, 2, tall, C), BF),
            pltpu.VMEM((2, count, rows * 8, C), F32),
            pltpu.VMEM((count, C), F32),
            pltpu.VMEM((1, C), F32),
            pltpu.SemaphoreType.DMA((count,)),
            pltpu.SemaphoreType.DMA((28,)),
            pltpu.SemaphoreType.DMA((8,)),
            pltpu.SemaphoreType.DMA((8,)),
            pltpu.SemaphoreType.DMA((5,)),
            pltpu.SemaphoreType.DMA((5,)),
            pltpu.SemaphoreType.REGULAR,
        ],
        compiler_params=pltpu.CompilerParams(
            collective_id=0, has_side_effects=True, vmem_limit_bytes=48 * 2**20
        ),
    )(*(pltpu.with_memory_space_constraint(a, pltpu.HBM) for a in args))
    out = pl.pallas_call(
        write_out,
        out_shape=jax.ShapeDtypeStruct(out.shape, BF),
        in_specs=[vmem],
        out_specs=hbm,
        scratch_shapes=[pltpu.SemaphoreType.DMA((count,))],
        compiler_params=pltpu.CompilerParams(vmem_limit_bytes=2**20),
    )(pltpu.with_memory_space_constraint(out, pltpu.VMEM))
    return out.reshape(count, 1, rows, cols, C)


def solution(mesh):
    return jax.shard_map(
        per_device,
        mesh=mesh,
        in_specs=(P("tm", "tile", None, None, None), P(), P(), P("tm", None), P()),
        out_specs=P("tm", "tile", None, None, None),
        check_vma=False,
    )
```

```python
import functools

import jax
import jax.numpy as jnp
from jax import lax
from jax.experimental import pallas as pl
from jax.experimental.pallas import tpu as pltpu
from jax.sharding import PartitionSpec as P

TROWS = 4
LINE = 4
C = 128
BF = jnp.bfloat16
F32 = jnp.float32
MESH = pl.DeviceIdType.MESH

TAPS = 3


def mm(lhs, rhs):
    return jnp.dot(lhs, rhs, preferred_element_type=F32)


def mm_halves(lhs, rhs):
    half = lhs.shape[1] // 2
    return mm(lhs[:, :half], rhs[:half]) + mm(lhs[:, half:], rhs[half:])


def pair_zeros(pair):
    zero = jnp.zeros((TAPS, C, C), BF)
    pair[3 * TAPS : 4 * TAPS, :, 0:C] = zero
    pair[0:TAPS, :, C : 2 * C] = zero


def pair_copies(w, pair):
    return [
        (w.at[i], pair.at[pl.ds((i + e) * TAPS, TAPS), :, pl.ds(e * C, C)]) for i in range(TAPS) for e in range(2)
    ]


def side_blocks(table):
    return [(s, k, e, b) for s in range(2) for k, taps in enumerate(table[s]) for e, b in enumerate(taps)]


def side_zeros(side, table):
    for s, k, e, b in side_blocks(table):
        if b is None:
            side[s, :, k, :, e * C : (e + 1) * C] = jnp.zeros((TAPS, C, C), BF)


def side_copies(w, side, table):
    return [
        (w.at[:, b], side.at[s, :, k, :, pl.ds(e * C, C)]) for s, k, e, b in side_blocks(table) if b is not None
    ]


SIDE_IN = (((1, 0), (0, None), (2, None)), ((1, 2), (2, None), (0, None)))
SIDE_OUT = (((0, None), (1, 0)), ((2, None), (1, 2)))


def pair_rows(parts, pairs):
    cols = parts[0].shape[1]
    split = [p.reshape(pairs + 1, 2, cols, p.shape[2]) for p in parts]
    taps = []
    for first in (0, 1):
        for parity in (0, 1):
            taps += [p[first : first + pairs, parity] for p in split]
    return jnp.concatenate(taps, axis=-1).reshape(pairs * cols, 12 * C)


def kernel(
    trows, frames, w_in, w_out, decay_in, skip_in, o,
    x, x3, s3, loc, pw1, pw2, sw1, sw2, edge, corner, z, zc, y, y2, ss, stage, cstage, rim, lo, inc, so, si, ot, decay, skip,
    load_sem, w_sem, send_sem, recv_sem, tsend_sem, trecv_sem, far_sem,
):
    count, rows, cols, _ = frames.shape
    tiles = lax.axis_size("tile")
    tcols = tiles // trows
    me = lax.axis_index("tile")
    tm = lax.axis_index("tm")
    k = lax.rem(me + tiles - 1, tiles)
    column = lax.rem(k, tcols)
    row_index = k // tcols
    up, down = row_index > 0, row_index < trows - 1
    left, right = column > 0, column < tcols - 1
    pairs = rows // 2
    tall = rows + 16

    loads = [
        pltpu.make_async_copy(frames.at[f], x.at[f, pl.ds(2, rows)], load_sem.at[f])
        for f in range(count)
    ]
    for c in loads:
        c.start()

    both = jnp.logical_and
    around = [
        (-1, left), (1, right), (-tcols, up), (tcols, down),
        (-tcols - 1, both(up, left)), (-tcols + 1, both(up, right)),
        (tcols - 1, both(down, left)), (tcols + 1, both(down, right)),
    ]

    def at(by):
        return lax.rem(me + by + tiles, tiles)

    first = me == 0
    near = [both(there, jnp.logical_not(first)) for _, there in around]
    to_first = [both(there, at(by) == 0) for by, there in around]

    barrier = pltpu.get_barrier_semaphore()
    greeted, far = jnp.int32(1), jnp.int32(0)
    for i, (by, there) in enumerate(around):
        greeted = greeted + near[i].astype(jnp.int32)
        far = far + both(there, first).astype(jnp.int32)

        @pl.when(both(there, jnp.logical_not(to_first[i])))
        def _():
            pl.semaphore_signal(barrier, inc=1, device_id=(tm, at(by)), device_id_type=MESH)

    pl.semaphore_signal(barrier, inc=1, device_id=(1 - tm, me), device_id_type=MESH)

    placed = pair_copies(w_in, pw1) + [(decay_in, decay), (skip_in, skip)]
    first_needed = len(placed)
    placed += pair_copies(w_out, pw2)
    then_needed = len(placed)
    placed += side_copies(w_in, sw1, SIDE_IN) + side_copies(w_out, sw2, SIDE_OUT)
    placed = [pltpu.make_async_copy(src, dst, w_sem.at[i]) for i, (src, dst) in enumerate(placed)]
    for c in placed[:first_needed]:
        c.start()

    def greet():
        pl.semaphore_wait(barrier, greeted)
        for i, (by, _) in enumerate(around):
            @pl.when(to_first[i])
            def _():
                pl.semaphore_signal(far_sem, inc=1, device_id=(tm, at(by)), device_id_type=MESH)

    starts_line = lax.rem(me, LINE) == 0
    pl.when(jnp.logical_not(starts_line))(greet)

    for f in range(count):
        loads[f].wait()
        stage[0] = x[f, 2 : 2 + rows, 0:16, :].astype(F32)[:, 0:8, :].reshape(rows * 8, C)
        stage[1] = x[f, 2 : 2 + rows, cols - 16 : cols, :].astype(F32)[:, 8:16, :].reshape(rows * 8, C)
        for s in range(2):
            for n in range(2):
                offset = n if s == 0 else 7 - n
                edge[s, n, f] = stage[s, pl.ds(offset, rows, stride=8), :].astype(BF)
                for t in range(2):
                    ends = pl.ds(offset + t * (rows - 2) * 8, 2, stride=8)
                    cstage[s, t, n, 2 * f : 2 * f + 2] = stage[s, ends, :]
    rest = jnp.zeros((8, C), F32)
    for s in range(2):
        for t in range(2):
            for n in range(2):
                corner[s, t, n] = jnp.concatenate([cstage[s, t, n], rest], axis=0).astype(BF)

    plan = [
        (edge.at[0], z.at[1]),
        (edge.at[1], z.at[0]),
        (frames.at[:, pl.ds(0, 2)], x.at[:, pl.ds(rows + 2, 2)]),
        (frames.at[:, pl.ds(rows - 2, 2)], x.at[:, pl.ds(0, 2)]),
        (corner.at[0, 0], zc.at[1, 1]),
        (corner.at[1, 0], zc.at[0, 1]),
        (corner.at[0, 1], zc.at[1, 0]),
        (corner.at[1, 1], zc.at[0, 0]),
    ]
    sends = [
        pltpu.make_async_remote_copy(
            src_ref=src, dst_ref=dst, send_sem=send_sem.at[i], recv_sem=recv_sem.at[i],
            device_id=(tm, at(around[i][0])), device_id_type=MESH,
        )
        for i, (src, dst) in enumerate(plan)
    ]
    comes = [around[i ^ 1][1] if i < 4 else around[11 - i][1] for i in range(8)]
    in_tile = lax.broadcasted_iota(jnp.int32, (1, 8, C), 1)

    def widen(f, start, size):
        wide = x[f, pl.ds(start, size)].astype(F32)
        no_last = jnp.concatenate([wide[:, : cols - 8], jnp.where(in_tile == 7, 0.0, wide[:, cols - 8 :])], axis=1)
        no_first = jnp.concatenate([jnp.where(in_tile == 0, 0.0, wide[:, :8]), wide[:, 8:]], axis=1)
        x3[f, pl.ds(start, size), :, 0:C] = pltpu.roll(no_last, 1, 1).astype(BF)
        x3[f, pl.ds(start, size), :, C : 2 * C] = pltpu.roll(no_first, cols - 1, 1).astype(BF)
        return wide

    def frame_rows(f, here):
        return [x3[f, here, :, 0:C], x[f, here], x3[f, here, :, C : 2 * C]]

    def exchange(i, src, dst):
        return pltpu.make_async_remote_copy(
            src_ref=src, dst_ref=dst, send_sem=tsend_sem.at[i], recv_sem=trecv_sem.at[i],
            device_id=(1 - tm, me), device_id_type=MESH,
        )

    half = pairs // 2
    chunks = [(1, half), (1 + half, pairs - 1 - half)]
    hands = [exchange(n, lo.at[pl.ds(q, size)], inc.at[pl.ds(q, size)]) for n, (q, size) in enumerate(chunks)]
    late_hands = [
        exchange(2, lo.at[pl.ds(0, 1)], inc.at[pl.ds(0, 1)]),
        exchange(3, lo.at[pl.ds(pairs, 1)], inc.at[pl.ds(pairs, 1)]),
        exchange(4, so, si),
    ]
    weights1 = pw1.reshape(4 * TAPS * C, 2 * C)
    weights2 = pw2.reshape(4 * TAPS * C, 2 * C)

    def loc_rows(q, size):
        return pl.ds((2 * q + 7) * cols, size * 2 * cols)

    def recur(f, q, size, drive):
        drive = drive.reshape(size, cols, 2 * C)
        drive = jnp.stack([drive[:, :, :C], drive[:, :, C:]], axis=1).reshape(size * 2 * cols, C)
        here = loc_rows(q, size)
        if f > 0:
            drive = decay[f : f + 1, :] * loc[f - 1, here] + drive
        loc[f, here] = drive
        if f == count - 1:
            lo[pl.ds(q, size)] = drive.astype(BF).reshape(size, 2, cols, C)

    def first_conv(n):
        q, size = chunks[n]
        for f in range(count):
            end = rows + 2 if n else 2 * half + 4
            for start in range(2 + n * (2 * half + 2), end, 2):
                widen(f, start, 2)
            lhs = pair_rows(frame_rows(f, pl.ds(2 * q, 2 * size + 2)), size)
            recur(f, q, size, mm(lhs, weights1[...]))

    greet_at = jnp.where(starts_line, 1, 0)

    @pl.loop(0, 2)
    def _(step):
        @pl.when(step == greet_at)
        def _():
            pl.when(starts_line)(greet)
            for i in (1, 0, 5, 7, 4, 6, 2, 3):
                pl.when(near[i])(sends[i].start)

        @pl.when(step != greet_at)
        def _():
            for c in placed[first_needed:]:
                c.start()
            pair_zeros(pw1)
            for c in placed[:first_needed]:
                c.wait()
            first_conv(0)

    hands[0].start()
    first_conv(1)
    hands[1].start()

    factors = []
    for f in range(count):
        keep = decay[f : f + 1, :]
        factors.append(keep * jnp.where(tm == 0, 0.0, 1.0) if f == 0 else factors[-1] * keep)

    def settle(f, q, real=(None, None)):
        state = loc[f, loc_rows(q, 1)].reshape(2, cols, C) + factors[f] * inc[q].astype(F32)
        first = jnp.where(in_tile == 0, 0.0, state[:, :8])
        last = jnp.where(in_tile == 7, 0.0, state[:, cols - 8 :])
        state = jnp.concatenate([first, state[:, 8 : cols - 8], last], axis=1)
        state = jnp.concatenate(
            [state[e : e + 1] if r is None else jnp.where(r, state[e : e + 1], 0.0) for e, r in enumerate(real)],
            axis=0,
        )
        here = pl.ds(2 * q, 2)
        s3[f, here, :, 0:C] = pltpu.roll(state, 1, 1).astype(BF)
        s3[f, here, :, C : 2 * C] = state.astype(BF)
        s3[f, here, :, 2 * C : 3 * C] = pltpu.roll(state, cols - 1, 1).astype(BF)

    def finish(f, p, size, result):
        result = result.reshape(size, cols, 2 * C)
        result = jnp.stack([result[:, :, :C], result[:, :, C:]], axis=1).reshape(2 * size, cols, C)
        mixed = result + skip[...] * x[f, pl.ds(2 + 2 * p, 2 * size)].astype(F32)
        ot[0, f, pl.ds(16 * p, 16 * size)] = mixed[:, :8].reshape(16 * size, C)
        ot[1, f, pl.ds(16 * p, 16 * size)] = mixed[:, cols - 8 :].reshape(16 * size, C)
        o[f, pl.ds(2 * p, 2 * size), 8 : cols - 8] = mixed[:, 8 : cols - 8].astype(BF)

    pair_zeros(pw2)
    side_zeros(sw1, SIDE_IN)
    side_zeros(sw2, SIDE_OUT)
    for i, (_, dst) in enumerate(plan):
        @pl.when(jnp.logical_not(comes[i]))
        def _():
            dst[...] = jnp.zeros(dst.shape, BF)

    for c in placed[first_needed:then_needed]:
        c.wait()
    inner = [(1, half - 1), (half, half - 1)]

    def second_conv(n, which):
        q, size = chunks[n]
        p, deep = inner[n]
        for f in which:
            for i in range(q, q + size):
                settle(f, i)
            lhs = pair_rows([s3[f, 2 * p : 2 * p + 2 * deep + 2]], deep)
            finish(f, p, deep, mm(lhs, weights2[...]))

    hands[0].wait_recv()
    second_conv(0, range(count))
    hands[1].wait_recv()
    second_conv(1, range(count // 2))

    @pl.when(first)
    def _():
        pl.semaphore_wait(far_sem, far)
        for i, c in enumerate(sends):
            pl.when(around[i][1])(c.start)

    def arrive(*which):
        for i in which:
            pl.when(comes[i])(sends[i].wait_recv)

    arrive(2, 3)
    for f in range(count):
        for t in range(2):
            wide = widen(f, t * (rows + 2), 2)
            rim[t, 0, 16 * f : 16 * f + 16] = wide[:, :8].reshape(16, C)
            rim[t, 1, 16 * f : 16 * f + 16] = wide[:, cols - 8 :].reshape(16, C)
    lhs = [pair_rows(frame_rows(f, pl.ds(2 * q, 4)), 1) for q in (0, pairs) for f in range(count)]
    drive = mm_halves(jnp.concatenate(lhs, axis=0), weights1[...])
    for n, q in enumerate((0, pairs)):
        for f in range(count):
            recur(f, q, 1, drive[(n * count + f) * cols : (n * count + f + 1) * cols])
    late_hands[0].start()
    late_hands[1].start()

    sides_at = jnp.where(first, 1, 0)

    @pl.loop(0, 2)
    def _(step):
        @pl.when(step == sides_at)
        def _():
            for c in placed[then_needed:]:
                c.wait()
            arrive(0, 4, 6, 1, 5, 7)
            for s in range(2):
                lines = [jnp.concatenate([z[s, 0, f], z[s, 1, f], edge[s, 0, f]], axis=-1) for f in range(count)]
                for t in range(2):
                    mine = jnp.concatenate([rim[t, s, pl.ds(7 * s, 8, stride=8), :], rest], axis=0).astype(BF)
                    lines.append(jnp.concatenate([zc[s, t, 0], zc[s, t, 1], mine], axis=-1))
                lhs = jnp.concatenate(lines, axis=0)
                for a in range(3):
                    result = mm(lhs, sw1[s, a].reshape(3 * C, 2 * C))
                    for e in range(2):
                        part = result[:, e * C : (e + 1) * C]
                        for f in range(count):
                            base = 2 * (8 + f * tall)
                            y[s, a, e, pl.ds(base + 16, rows, stride=2), :] = part[f * rows : (f + 1) * rows]
                            for t in range(2):
                                begin = count * rows + 16 * t + 2 * f
                                y[s, a, e, pl.ds(base + 12 + t * 2 * (rows + 2), 2, stride=2), :] = part[begin : begin + 2]

            for s in range(2):
                inside = jnp.where(left if s == 0 else right, 1.0, 0.0).astype(F32)
                for e in range(2):
                    state = None
                    for f in range(count):
                        base = 2 * (8 + f * tall)
                        drive = sum(y[s, a, e, pl.ds(base + 2 * (a - 1), tall, stride=2), :] for a in range(3))
                        if e == 0:
                            drive = drive * inside
                        state = drive if f == 0 else decay[f : f + 1, :] * state + drive
                        whole = state
                        if e == 1:
                            whole = state + loc[f, pl.ds(s * (cols - 1), tall, stride=cols), :]
                        ss[s, e, f] = whole
                    so[s, e] = whole.astype(BF)
            late_hands[2].start()

        @pl.when(step != sides_at)
        def _():
            second_conv(1, range(count // 2, count))
            late_hands[0].wait_recv()
            late_hands[1].wait_recv()
            for f in range(count):
                settle(f, 0, (up, None))
                settle(f, pairs, (None, down))
            lhs = [pair_rows([s3[f, 2 * p : 2 * p + 4]], 1) for p in (0, pairs - 1) for f in range(count)]
            result = mm_halves(jnp.concatenate(lhs, axis=0), weights2[...])
            for n, p in enumerate((0, pairs - 1)):
                for f in range(count):
                    finish(f, p, 1, result[(n * count + f) * cols : (n * count + f + 1) * cols])

    late_hands[2].wait_recv()
    place = lax.broadcasted_iota(jnp.int32, (tall, C), 0)
    off = jnp.logical_or(
        both(place == 7, jnp.logical_not(up)), both(place == rows + 8, jnp.logical_not(down))
    )
    for s in range(2):
        sides = []
        for f in range(count):
            pair = [
                jnp.where(off, 0.0, ss[s, e, f] + factors[f] * si[s, e].astype(F32)).astype(BF) for e in range(2)
            ]
            sides.append(jnp.concatenate(pair, axis=-1))
        lhs = jnp.concatenate(sides, axis=0)
        for a in range(3):
            result = mm(lhs, sw2[s, a].reshape(2 * C, 2 * C))
            for e in range(2):
                y2[s, a, e, pl.ds(16, count * tall, stride=2), :] = result[:, e * C : (e + 1) * C]

    for f in range(count):
        base = 2 * (8 + f * tall + 8)
        for s in range(2):
            for e in range(2):
                here = pl.ds(e if s == 0 else 7 - e, rows, stride=8)
                fix = sum(y2[s, a, e, pl.ds(base + 2 * (a - 1), rows, stride=2), :] for a in range(3))
                ot[s, f, here, :] = ot[s, f, here, :] + fix
        o[f, :, 0:8] = ot[0, f].reshape(rows, 8, C).astype(BF)
        o[f, :, cols - 8 :] = ot[1, f].reshape(rows, 8, C).astype(BF)

    for i, c in enumerate(sends):
        pl.when(around[i][1])(c.wait_send)
    for c in hands + late_hands:
        c.wait_send()


def write_out(o, out, sem):
    stores = [pltpu.make_async_copy(o.at[f], out.at[f], sem.at[f]) for f in range(o.shape[0])]
    for c in stores:
        c.start()
    for c in stores:
        c.wait()


def per_device(frames, w_in, w_out, decay, skip):
    count, _, rows, cols, _ = frames.shape
    tall = rows + 16
    spread = 2 * (count * tall + 16)
    hbm = pl.BlockSpec(memory_space=pltpu.HBM)
    vmem = pl.BlockSpec(memory_space=pltpu.VMEM)
    args = (frames[:, 0], w_in, w_out, decay, skip.reshape(1, C))
    out = pl.pallas_call(
        functools.partial(kernel, TROWS),
        out_shape=pltpu.VMEM((count, rows, cols, C), BF),
        in_specs=[hbm] * 5,
        out_specs=vmem,
        scratch_shapes=[
            pltpu.VMEM((count, rows + 4, cols, C), BF),
            pltpu.VMEM((count, rows + 4, cols, 2 * C), BF),
            pltpu.VMEM((count, rows + 2, cols, 3 * C), BF),
            pltpu.VMEM((count, tall * cols, C), F32),
            pltpu.VMEM((4 * TAPS, C, 2 * C), BF),
            pltpu.VMEM((4 * TAPS, C, 2 * C), BF),
            pltpu.VMEM((2, TAPS, 3, C, 2 * C), BF),
            pltpu.VMEM((2, TAPS, 2, C, 2 * C), BF),
            pltpu.VMEM((2, 2, count, rows, C), BF),
            pltpu.VMEM((2, 2, 2, 16, C), BF),
            pltpu.VMEM((2, 2, count, rows, C), BF),
            pltpu.VMEM((2, 2, 2, 16, C), BF),
            pltpu.VMEM((2, TAPS, 2, spread, C), F32),
            pltpu.VMEM((2, TAPS, 2, spread, C), F32),
            pltpu.VMEM((2, 2, count, tall, C), F32),
            pltpu.VMEM((2, rows * 8, C), F32),
            pltpu.VMEM((2, 2, 2, 8, C), F32),
            pltpu.VMEM((2, 2, 16 * count, C), F32),
            pltpu.VMEM((rows // 2 + 1, 2, cols, C), BF),
            pltpu.VMEM((rows // 2 + 1, 2, cols, C), BF),
            pltpu.VMEM((2, 2, tall, C), BF),
            pltpu.VMEM((2, 2, tall, C), BF),
            pltpu.VMEM((2, count, rows * 8, C), F32),
            pltpu.VMEM((count, C), F32),
            pltpu.VMEM((1, C), F32),
            pltpu.SemaphoreType.DMA((count,)),
            pltpu.SemaphoreType.DMA((28,)),
            pltpu.SemaphoreType.DMA((8,)),
            pltpu.SemaphoreType.DMA((8,)),
            pltpu.SemaphoreType.DMA((5,)),
            pltpu.SemaphoreType.DMA((5,)),
            pltpu.SemaphoreType.REGULAR,
        ],
        compiler_params=pltpu.CompilerParams(
            collective_id=0, has_side_effects=True, vmem_limit_bytes=48 * 2**20
        ),
    )(*(pltpu.with_memory_space_constraint(a, pltpu.HBM) for a in args))
    out = pl.pallas_call(
        write_out,
        out_shape=jax.ShapeDtypeStruct(out.shape, BF),
        in_specs=[vmem],
        out_specs=hbm,
        scratch_shapes=[pltpu.SemaphoreType.DMA((count,))],
        compiler_params=pltpu.CompilerParams(vmem_limit_bytes=2**20),
    )(pltpu.with_memory_space_constraint(out, pltpu.VMEM))
    return out.reshape(count, 1, rows, cols, C)


def solution(mesh):
    return jax.shard_map(
        per_device,
        mesh=mesh,
        in_specs=(P("tm", "tile", None, None, None), P(), P(), P("tm", None), P()),
        out_specs=P("tm", "tile", None, None, None),
        check_vma=False,
    )
```

```python
import functools

import jax
import jax.numpy as jnp
from jax import lax
from jax.experimental import pallas as pl
from jax.experimental.pallas import tpu as pltpu
from jax.sharding import PartitionSpec as P

TROWS = 4
LINE = 4
C = 128
BF = jnp.bfloat16
F32 = jnp.float32
MESH = pl.DeviceIdType.MESH

TAPS = 3


def mm(lhs, rhs):
    return jnp.dot(lhs, rhs, preferred_element_type=F32)


def mm_halves(lhs, rhs):
    half = lhs.shape[1] // 2
    return mm(lhs[:, :half], rhs[:half]) + mm(lhs[:, half:], rhs[half:])


def pair_zeros(pair):
    zero = jnp.zeros((TAPS, C, C), BF)
    pair[3 * TAPS : 4 * TAPS, :, 0:C] = zero
    pair[0:TAPS, :, C : 2 * C] = zero


def pair_copies(w, pair):
    return [
        (w.at[i], pair.at[pl.ds((i + e) * TAPS, TAPS), :, pl.ds(e * C, C)]) for i in range(TAPS) for e in range(2)
    ]


def side_blocks(table):
    return [(s, k, e, b) for s in range(2) for k, taps in enumerate(table[s]) for e, b in enumerate(taps)]


def side_zeros(side, table):
    for s, k, e, b in side_blocks(table):
        if b is None:
            side[s, :, k, :, e * C : (e + 1) * C] = jnp.zeros((TAPS, C, C), BF)


def side_copies(w, side, table):
    return [
        (w.at[:, b], side.at[s, :, k, :, pl.ds(e * C, C)]) for s, k, e, b in side_blocks(table) if b is not None
    ]


SIDE_IN = (((1, 0), (0, None), (2, None)), ((1, 2), (2, None), (0, None)))
SIDE_OUT = (((0, None), (1, 0)), ((2, None), (1, 2)))


def pair_rows(parts, pairs):
    cols = parts[0].shape[1]
    split = [p.reshape(pairs + 1, 2, cols, p.shape[2]) for p in parts]
    taps = []
    for first in (0, 1):
        for parity in (0, 1):
            taps += [p[first : first + pairs, parity] for p in split]
    return jnp.concatenate(taps, axis=-1).reshape(pairs * cols, 12 * C)


def kernel(
    trows, frames, w_in, w_out, decay_in, skip_in, o,
    x, x3, s3, loc, pw1, pw2, sw1, sw2, edge, corner, z, zc, y, y2, ss, stage, cstage, rim, lo, inc, so, si, ot, decay, skip,
    load_sem, w_sem, send_sem, recv_sem, tsend_sem, trecv_sem, far_sem,
):
    count, rows, cols, _ = frames.shape
    tiles = lax.axis_size("tile")
    tcols = tiles // trows
    me = lax.axis_index("tile")
    tm = lax.axis_index("tm")
    k = lax.rem(me + tiles - 1, tiles)
    column = lax.rem(k, tcols)
    row_index = k // tcols
    up, down = row_index > 0, row_index < trows - 1
    left, right = column > 0, column < tcols - 1
    pairs = rows // 2
    tall = rows + 16

    loads = [
        pltpu.make_async_copy(frames.at[f], x.at[f, pl.ds(2, rows)], load_sem.at[f])
        for f in range(count)
    ]
    for c in loads:
        c.start()

    both = jnp.logical_and
    around = [
        (-1, left), (1, right), (-tcols, up), (tcols, down),
        (-tcols - 1, both(up, left)), (-tcols + 1, both(up, right)),
        (tcols - 1, both(down, left)), (tcols + 1, both(down, right)),
    ]

    def at(by):
        return lax.rem(me + by + tiles, tiles)

    first = me == 0
    near = [both(there, jnp.logical_not(first)) for _, there in around]
    to_first = [both(there, at(by) == 0) for by, there in around]

    barrier = pltpu.get_barrier_semaphore()
    greeted = jnp.int32(1)
    for i, (by, there) in enumerate(around):
        greeted = greeted + near[i].astype(jnp.int32)

        @pl.when(both(there, jnp.logical_not(to_first[i])))
        def _():
            pl.semaphore_signal(barrier, inc=1, device_id=(tm, at(by)), device_id_type=MESH)

    pl.semaphore_signal(barrier, inc=1, device_id=(1 - tm, me), device_id_type=MESH)

    placed = pair_copies(w_in, pw1) + [(decay_in, decay), (skip_in, skip)]
    first_needed = len(placed)
    placed += pair_copies(w_out, pw2)
    then_needed = len(placed)
    placed += side_copies(w_in, sw1, SIDE_IN) + side_copies(w_out, sw2, SIDE_OUT)
    placed = [pltpu.make_async_copy(src, dst, w_sem.at[i]) for i, (src, dst) in enumerate(placed)]
    for c in placed[:first_needed]:
        c.start()

    def greet():
        pl.semaphore_wait(barrier, greeted)
        for i, (by, _) in enumerate(around):
            @pl.when(to_first[i])
            def _():
                pl.semaphore_signal(far_sem.at[i], inc=1, device_id=(tm, at(by)), device_id_type=MESH)

    starts_line = lax.rem(me, LINE) == 0
    pl.when(jnp.logical_not(starts_line))(greet)

    for f in range(count):
        loads[f].wait()
        stage[0] = x[f, 2 : 2 + rows, 0:16, :].astype(F32)[:, 0:8, :].reshape(rows * 8, C)
        stage[1] = x[f, 2 : 2 + rows, cols - 16 : cols, :].astype(F32)[:, 8:16, :].reshape(rows * 8, C)
        for s in range(2):
            for n in range(2):
                offset = n if s == 0 else 7 - n
                edge[s, n, f] = stage[s, pl.ds(offset, rows, stride=8), :].astype(BF)
                for t in range(2):
                    ends = pl.ds(offset + t * (rows - 2) * 8, 2, stride=8)
                    cstage[s, t, n, 2 * f : 2 * f + 2] = stage[s, ends, :]
    rest = jnp.zeros((8, C), F32)
    for s in range(2):
        for t in range(2):
            for n in range(2):
                corner[s, t, n] = jnp.concatenate([cstage[s, t, n], rest], axis=0).astype(BF)

    plan = [
        (edge.at[0], z.at[1]),
        (edge.at[1], z.at[0]),
        (frames.at[:, pl.ds(0, 2)], x.at[:, pl.ds(rows + 2, 2)]),
        (frames.at[:, pl.ds(rows - 2, 2)], x.at[:, pl.ds(0, 2)]),
        (corner.at[0, 0], zc.at[1, 1]),
        (corner.at[1, 0], zc.at[0, 1]),
        (corner.at[0, 1], zc.at[1, 0]),
        (corner.at[1, 1], zc.at[0, 0]),
    ]
    sends = [
        pltpu.make_async_remote_copy(
            src_ref=src, dst_ref=dst, send_sem=send_sem.at[i], recv_sem=recv_sem.at[i],
            device_id=(tm, at(around[i][0])), device_id_type=MESH,
        )
        for i, (src, dst) in enumerate(plan)
    ]
    comes = [around[i ^ 1][1] if i < 4 else around[11 - i][1] for i in range(8)]
    in_tile = lax.broadcasted_iota(jnp.int32, (1, 8, C), 1)

    def widen(f, start, size):
        wide = x[f, pl.ds(start, size)].astype(F32)
        no_last = jnp.concatenate([wide[:, : cols - 8], jnp.where(in_tile == 7, 0.0, wide[:, cols - 8 :])], axis=1)
        no_first = jnp.concatenate([jnp.where(in_tile == 0, 0.0, wide[:, :8]), wide[:, 8:]], axis=1)
        x3[f, pl.ds(start, size), :, 0:C] = pltpu.roll(no_last, 1, 1).astype(BF)
        x3[f, pl.ds(start, size), :, C : 2 * C] = pltpu.roll(no_first, cols - 1, 1).astype(BF)
        return wide

    def frame_rows(f, here):
        return [x3[f, here, :, 0:C], x[f, here], x3[f, here, :, C : 2 * C]]

    def exchange(i, src, dst):
        return pltpu.make_async_remote_copy(
            src_ref=src, dst_ref=dst, send_sem=tsend_sem.at[i], recv_sem=trecv_sem.at[i],
            device_id=(1 - tm, me), device_id_type=MESH,
        )

    half = pairs // 2
    chunks = [(1, half), (1 + half, pairs - 1 - half)]
    hands = [exchange(n, lo.at[pl.ds(q, size)], inc.at[pl.ds(q, size)]) for n, (q, size) in enumerate(chunks)]
    late_hands = [
        exchange(2, lo.at[pl.ds(0, 1)], inc.at[pl.ds(0, 1)]),
        exchange(3, lo.at[pl.ds(pairs, 1)], inc.at[pl.ds(pairs, 1)]),
        exchange(4, so, si),
    ]
    weights1 = pw1.reshape(4 * TAPS * C, 2 * C)
    weights2 = pw2.reshape(4 * TAPS * C, 2 * C)

    def loc_rows(q, size):
        return pl.ds((2 * q + 7) * cols, size * 2 * cols)

    def recur(f, q, size, drive):
        drive = drive.reshape(size, cols, 2 * C)
        drive = jnp.stack([drive[:, :, :C], drive[:, :, C:]], axis=1).reshape(size * 2 * cols, C)
        here = loc_rows(q, size)
        if f > 0:
            drive = decay[f : f + 1, :] * loc[f - 1, here] + drive
        loc[f, here] = drive
        if f == count - 1:
            lo[pl.ds(q, size)] = drive.astype(BF).reshape(size, 2, cols, C)

    def first_conv(n):
        q, size = chunks[n]
        for f in range(count):
            end = rows + 2 if n else 2 * half + 4
            for start in range(2 + n * (2 * half + 2), end, 2):
                widen(f, start, 2)
            lhs = pair_rows(frame_rows(f, pl.ds(2 * q, 2 * size + 2)), size)
            recur(f, q, size, mm(lhs, weights1[...]))

    greet_at = jnp.where(starts_line, 1, 0)

    @pl.loop(0, 2)
    def _(step):
        @pl.when(step == greet_at)
        def _():
            pl.when(starts_line)(greet)
            for i in (1, 5, 7, 4, 6, 3):
                pl.when(near[i])(sends[i].start)

        @pl.when(step != greet_at)
        def _():
            for c in placed[first_needed:]:
                c.start()
            pair_zeros(pw1)
            for c in placed[:first_needed]:
                c.wait()
            first_conv(0)

    hands[0].start()
    for i in (0, 2):
        pl.when(near[i])(sends[i].start)
    first_conv(1)
    hands[1].start()

    factors = []
    for f in range(count):
        keep = decay[f : f + 1, :]
        factors.append(keep * jnp.where(tm == 0, 0.0, 1.0) if f == 0 else factors[-1] * keep)

    def settle(f, q, real=(None, None)):
        state = loc[f, loc_rows(q, 1)].reshape(2, cols, C) + factors[f] * inc[q].astype(F32)
        first = jnp.where(in_tile == 0, 0.0, state[:, :8])
        last = jnp.where(in_tile == 7, 0.0, state[:, cols - 8 :])
        state = jnp.concatenate([first, state[:, 8 : cols - 8], last], axis=1)
        state = jnp.concatenate(
            [state[e : e + 1] if r is None else jnp.where(r, state[e : e + 1], 0.0) for e, r in enumerate(real)],
            axis=0,
        )
        here = pl.ds(2 * q, 2)
        s3[f, here, :, 0:C] = pltpu.roll(state, 1, 1).astype(BF)
        s3[f, here, :, C : 2 * C] = state.astype(BF)
        s3[f, here, :, 2 * C : 3 * C] = pltpu.roll(state, cols - 1, 1).astype(BF)

    def finish(f, p, size, result):
        result = result.reshape(size, cols, 2 * C)
        result = jnp.stack([result[:, :, :C], result[:, :, C:]], axis=1).reshape(2 * size, cols, C)
        mixed = result + skip[...] * x[f, pl.ds(2 + 2 * p, 2 * size)].astype(F32)
        ot[0, f, pl.ds(16 * p, 16 * size)] = mixed[:, :8].reshape(16 * size, C)
        ot[1, f, pl.ds(16 * p, 16 * size)] = mixed[:, cols - 8 :].reshape(16 * size, C)
        o[f, pl.ds(2 * p, 2 * size), 8 : cols - 8] = mixed[:, 8 : cols - 8].astype(BF)

    pair_zeros(pw2)
    side_zeros(sw1, SIDE_IN)
    side_zeros(sw2, SIDE_OUT)
    for i, (_, dst) in enumerate(plan):
        @pl.when(jnp.logical_not(comes[i]))
        def _():
            dst[...] = jnp.zeros(dst.shape, BF)

    for c in placed[first_needed:then_needed]:
        c.wait()
    inner = [(1, half - 1), (half, half - 1)]

    def second_conv(n, which):
        q, size = chunks[n]
        p, deep = inner[n]
        for f in which:
            for i in range(q, q + size):
                settle(f, i)
            lhs = pair_rows([s3[f, 2 * p : 2 * p + 2 * deep + 2]], deep)
            finish(f, p, deep, mm(lhs, weights2[...]))

    hands[0].wait_recv()
    second_conv(0, range(count))
    hands[1].wait_recv()
    second_conv(1, range(count // 2))

    @pl.when(first)
    def _():
        for i, opposite in ((2, 3), (3, 2), (4, 7), (5, 6), (6, 5), (7, 4), (0, 1), (1, 0)):
            @pl.when(around[i][1])
            def _():
                pl.semaphore_wait(far_sem.at[opposite], 1)
                sends[i].start()

    def arrive(*which):
        for i in which:
            pl.when(comes[i])(sends[i].wait_recv)

    arrive(2, 3)
    for f in range(count):
        for t in range(2):
            wide = widen(f, t * (rows + 2), 2)
            rim[t, 0, 16 * f : 16 * f + 16] = wide[:, :8].reshape(16, C)
            rim[t, 1, 16 * f : 16 * f + 16] = wide[:, cols - 8 :].reshape(16, C)
    lhs = [pair_rows(frame_rows(f, pl.ds(2 * q, 4)), 1) for q in (0, pairs) for f in range(count)]
    drive = mm_halves(jnp.concatenate(lhs, axis=0), weights1[...])
    for n, q in enumerate((0, pairs)):
        for f in range(count):
            recur(f, q, 1, drive[(n * count + f) * cols : (n * count + f + 1) * cols])
    late_hands[0].start()
    late_hands[1].start()

    sides_at = jnp.where(first, 1, 0)

    @pl.loop(0, 2)
    def _(step):
        @pl.when(step == sides_at)
        def _():
            for c in placed[then_needed:]:
                c.wait()
            arrive(0, 4, 6, 1, 5, 7)
            for s in range(2):
                lines = [jnp.concatenate([z[s, 0, f], z[s, 1, f], edge[s, 0, f]], axis=-1) for f in range(count)]
                for t in range(2):
                    mine = jnp.concatenate([rim[t, s, pl.ds(7 * s, 8, stride=8), :], rest], axis=0).astype(BF)
                    lines.append(jnp.concatenate([zc[s, t, 0], zc[s, t, 1], mine], axis=-1))
                lhs = jnp.concatenate(lines, axis=0)
                for a in range(3):
                    result = mm(lhs, sw1[s, a].reshape(3 * C, 2 * C))
                    for e in range(2):
                        part = result[:, e * C : (e + 1) * C]
                        for f in range(count):
                            base = 2 * (8 + f * tall)
                            y[s, a, e, pl.ds(base + 16, rows, stride=2), :] = part[f * rows : (f + 1) * rows]
                            for t in range(2):
                                begin = count * rows + 16 * t + 2 * f
                                y[s, a, e, pl.ds(base + 12 + t * 2 * (rows + 2), 2, stride=2), :] = part[begin : begin + 2]

            for s in range(2):
                inside = jnp.where(left if s == 0 else right, 1.0, 0.0).astype(F32)
                for e in range(2):
                    state = None
                    for f in range(count):
                        base = 2 * (8 + f * tall)
                        drive = sum(y[s, a, e, pl.ds(base + 2 * (a - 1), tall, stride=2), :] for a in range(3))
                        if e == 0:
                            drive = drive * inside
                        state = drive if f == 0 else decay[f : f + 1, :] * state + drive
                        whole = state
                        if e == 1:
                            whole = state + loc[f, pl.ds(s * (cols - 1), tall, stride=cols), :]
                        ss[s, e, f] = whole
                    so[s, e] = whole.astype(BF)
            late_hands[2].start()

        @pl.when(step != sides_at)
        def _():
            second_conv(1, range(count // 2, count))
            late_hands[0].wait_recv()
            late_hands[1].wait_recv()
            for f in range(count):
                settle(f, 0, (up, None))
                settle(f, pairs, (None, down))
            lhs = [pair_rows([s3[f, 2 * p : 2 * p + 4]], 1) for p in (0, pairs - 1) for f in range(count)]
            result = mm_halves(jnp.concatenate(lhs, axis=0), weights2[...])
            for n, p in enumerate((0, pairs - 1)):
                for f in range(count):
                    finish(f, p, 1, result[(n * count + f) * cols : (n * count + f + 1) * cols])

    late_hands[2].wait_recv()
    place = lax.broadcasted_iota(jnp.int32, (tall, C), 0)
    off = jnp.logical_or(
        both(place == 7, jnp.logical_not(up)), both(place == rows + 8, jnp.logical_not(down))
    )
    for s in range(2):
        sides = []
        for f in range(count):
            pair = [
                jnp.where(off, 0.0, ss[s, e, f] + factors[f] * si[s, e].astype(F32)).astype(BF) for e in range(2)
            ]
            sides.append(jnp.concatenate(pair, axis=-1))
        lhs = jnp.concatenate(sides, axis=0)
        for a in range(3):
            result = mm(lhs, sw2[s, a].reshape(2 * C, 2 * C))
            for e in range(2):
                y2[s, a, e, pl.ds(16, count * tall, stride=2), :] = result[:, e * C : (e + 1) * C]

    for f in range(count):
        base = 2 * (8 + f * tall + 8)
        for s in range(2):
            for e in range(2):
                here = pl.ds(e if s == 0 else 7 - e, rows, stride=8)
                fix = sum(y2[s, a, e, pl.ds(base + 2 * (a - 1), rows, stride=2), :] for a in range(3))
                ot[s, f, here, :] = ot[s, f, here, :] + fix
        o[f, :, 0:8] = ot[0, f].reshape(rows, 8, C).astype(BF)
        o[f, :, cols - 8 :] = ot[1, f].reshape(rows, 8, C).astype(BF)

    for i, c in enumerate(sends):
        pl.when(around[i][1])(c.wait_send)
    for c in hands + late_hands:
        c.wait_send()


def write_out(o, out, sem):
    stores = [pltpu.make_async_copy(o.at[f], out.at[f], sem.at[f]) for f in range(o.shape[0])]
    for c in stores:
        c.start()
    for c in stores:
        c.wait()


def per_device(frames, w_in, w_out, decay, skip):
    count, _, rows, cols, _ = frames.shape
    tall = rows + 16
    spread = 2 * (count * tall + 16)
    hbm = pl.BlockSpec(memory_space=pltpu.HBM)
    vmem = pl.BlockSpec(memory_space=pltpu.VMEM)
    args = (frames[:, 0], w_in, w_out, decay, skip.reshape(1, C))
    out = pl.pallas_call(
        functools.partial(kernel, TROWS),
        out_shape=pltpu.VMEM((count, rows, cols, C), BF),
        in_specs=[hbm] * 5,
        out_specs=vmem,
        scratch_shapes=[
            pltpu.VMEM((count, rows + 4, cols, C), BF),
            pltpu.VMEM((count, rows + 4, cols, 2 * C), BF),
            pltpu.VMEM((count, rows + 2, cols, 3 * C), BF),
            pltpu.VMEM((count, tall * cols, C), F32),
            pltpu.VMEM((4 * TAPS, C, 2 * C), BF),
            pltpu.VMEM((4 * TAPS, C, 2 * C), BF),
            pltpu.VMEM((2, TAPS, 3, C, 2 * C), BF),
            pltpu.VMEM((2, TAPS, 2, C, 2 * C), BF),
            pltpu.VMEM((2, 2, count, rows, C), BF),
            pltpu.VMEM((2, 2, 2, 16, C), BF),
            pltpu.VMEM((2, 2, count, rows, C), BF),
            pltpu.VMEM((2, 2, 2, 16, C), BF),
            pltpu.VMEM((2, TAPS, 2, spread, C), F32),
            pltpu.VMEM((2, TAPS, 2, spread, C), F32),
            pltpu.VMEM((2, 2, count, tall, C), F32),
            pltpu.VMEM((2, rows * 8, C), F32),
            pltpu.VMEM((2, 2, 2, 8, C), F32),
            pltpu.VMEM((2, 2, 16 * count, C), F32),
            pltpu.VMEM((rows // 2 + 1, 2, cols, C), BF),
            pltpu.VMEM((rows // 2 + 1, 2, cols, C), BF),
            pltpu.VMEM((2, 2, tall, C), BF),
            pltpu.VMEM((2, 2, tall, C), BF),
            pltpu.VMEM((2, count, rows * 8, C), F32),
            pltpu.VMEM((count, C), F32),
            pltpu.VMEM((1, C), F32),
            pltpu.SemaphoreType.DMA((count,)),
            pltpu.SemaphoreType.DMA((28,)),
            pltpu.SemaphoreType.DMA((8,)),
            pltpu.SemaphoreType.DMA((8,)),
            pltpu.SemaphoreType.DMA((5,)),
            pltpu.SemaphoreType.DMA((5,)),
            pltpu.SemaphoreType.REGULAR((8,)),
        ],
        compiler_params=pltpu.CompilerParams(
            collective_id=0, has_side_effects=True, vmem_limit_bytes=48 * 2**20
        ),
    )(*(pltpu.with_memory_space_constraint(a, pltpu.HBM) for a in args))
    out = pl.pallas_call(
        write_out,
        out_shape=jax.ShapeDtypeStruct(out.shape, BF),
        in_specs=[vmem],
        out_specs=hbm,
        scratch_shapes=[pltpu.SemaphoreType.DMA((count,))],
        compiler_params=pltpu.CompilerParams(vmem_limit_bytes=2**20),
    )(pltpu.with_memory_space_constraint(out, pltpu.VMEM))
    return out.reshape(count, 1, rows, cols, C)


def solution(mesh):
    return jax.shard_map(
        per_device,
        mesh=mesh,
        in_specs=(P("tm", "tile", None, None, None), P(), P(), P("tm", None), P()),
        out_specs=P("tm", "tile", None, None, None),
        check_vma=False,
    )
```

```python
import functools

import jax
import jax.numpy as jnp
from jax import lax
from jax.experimental import pallas as pl
from jax.experimental.pallas import tpu as pltpu
from jax.sharding import PartitionSpec as P

TROWS = 4
LINE = 4
C = 128
BF = jnp.bfloat16
F32 = jnp.float32
MESH = pl.DeviceIdType.MESH

TAPS = 3


def mm(lhs, rhs):
    return jnp.dot(lhs, rhs, preferred_element_type=F32)


def mm_halves(lhs, rhs):
    half = lhs.shape[1] // 2
    return mm(lhs[:, :half], rhs[:half]) + mm(lhs[:, half:], rhs[half:])


def pair_zeros(pair):
    zero = jnp.zeros((TAPS, C, C), BF)
    pair[3 * TAPS : 4 * TAPS, :, 0:C] = zero
    pair[0:TAPS, :, C : 2 * C] = zero


def pair_copies(w, pair):
    return [
        (w.at[i], pair.at[pl.ds((i + e) * TAPS, TAPS), :, pl.ds(e * C, C)]) for i in range(TAPS) for e in range(2)
    ]


def side_blocks(table):
    return [(s, k, e, b) for s in range(2) for k, taps in enumerate(table[s]) for e, b in enumerate(taps)]


def side_zeros(side, table):
    for s, k, e, b in side_blocks(table):
        if b is None:
            side[s, :, k, :, e * C : (e + 1) * C] = jnp.zeros((TAPS, C, C), BF)


def side_copies(w, side, table):
    return [
        (w.at[:, b], side.at[s, :, k, :, pl.ds(e * C, C)]) for s, k, e, b in side_blocks(table) if b is not None
    ]


SIDE_IN = (((1, 0), (0, None), (2, None)), ((1, 2), (2, None), (0, None)))
SIDE_OUT = (((0, None), (1, 0)), ((2, None), (1, 2)))


def pair_rows(parts, pairs):
    cols = parts[0].shape[1]
    split = [p.reshape(pairs + 1, 2, cols, p.shape[2]) for p in parts]
    taps = []
    for first in (0, 1):
        for parity in (0, 1):
            taps += [p[first : first + pairs, parity] for p in split]
    return jnp.concatenate(taps, axis=-1).reshape(pairs * cols, 12 * C)


def kernel(
    trows, frames, w_in, w_out, decay_in, skip_in, o,
    x, x3, s3, loc, pw1, pw2, sw1, sw2, edge, corner, z, zc, y, y2, ss, stage, cstage, rim, lo, inc, so, si, ot, decay, skip,
    load_sem, w_sem, send_sem, recv_sem, tsend_sem, trecv_sem, far_sem,
):
    count, rows, cols, _ = frames.shape
    tiles = lax.axis_size("tile")
    tcols = tiles // trows
    me = lax.axis_index("tile")
    tm = lax.axis_index("tm")
    k = lax.rem(me + tiles - 1, tiles)
    column = lax.rem(k, tcols)
    row_index = k // tcols
    up, down = row_index > 0, row_index < trows - 1
    left, right = column > 0, column < tcols - 1
    pairs = rows // 2
    tall = rows + 16

    loads = [
        pltpu.make_async_copy(frames.at[f], x.at[f, pl.ds(2, rows)], load_sem.at[f])
        for f in range(count)
    ]
    for c in loads:
        c.start()

    both = jnp.logical_and
    around = [
        (-1, left), (1, right), (-tcols, up), (tcols, down),
        (-tcols - 1, both(up, left)), (-tcols + 1, both(up, right)),
        (tcols - 1, both(down, left)), (tcols + 1, both(down, right)),
    ]

    def at(by):
        return lax.rem(me + by + tiles, tiles)

    first = me == 0
    starts_line = lax.rem(me, LINE) == 0
    far, far_for = [], []
    for i, (by, there) in enumerate(around):
        far.append(both(there, starts_line if i in (0, 4, 6) else first))
        target_far = lax.rem(at(by), LINE) == 0 if i in (1, 5, 7) else at(by) == 0
        far_for.append(both(there, target_far))
    near = [both(there, jnp.logical_not(far[i])) for i, (_, there) in enumerate(around)]

    barrier = pltpu.get_barrier_semaphore()
    greeted = jnp.int32(1)
    for i, (by, there) in enumerate(around):
        greeted = greeted + near[i].astype(jnp.int32)

        @pl.when(both(there, jnp.logical_not(far_for[i])))
        def _():
            pl.semaphore_signal(barrier, inc=1, device_id=(tm, at(by)), device_id_type=MESH)

    pl.semaphore_signal(barrier, inc=1, device_id=(1 - tm, me), device_id_type=MESH)

    placed = pair_copies(w_in, pw1) + [(decay_in, decay), (skip_in, skip)]
    first_needed = len(placed)
    placed += pair_copies(w_out, pw2)
    then_needed = len(placed)
    placed += side_copies(w_in, sw1, SIDE_IN) + side_copies(w_out, sw2, SIDE_OUT)
    placed = [pltpu.make_async_copy(src, dst, w_sem.at[i]) for i, (src, dst) in enumerate(placed)]
    for c in placed[:first_needed]:
        c.start()

    pl.semaphore_wait(barrier, greeted)
    for i, (by, _) in enumerate(around):
        @pl.when(far_for[i])
        def _():
            pl.semaphore_signal(far_sem.at[i], inc=1, device_id=(tm, at(by)), device_id_type=MESH)

    for f in range(count):
        loads[f].wait()
        stage[0] = x[f, 2 : 2 + rows, 0:16, :].astype(F32)[:, 0:8, :].reshape(rows * 8, C)
        stage[1] = x[f, 2 : 2 + rows, cols - 16 : cols, :].astype(F32)[:, 8:16, :].reshape(rows * 8, C)
        for s in range(2):
            for n in range(2):
                offset = n if s == 0 else 7 - n
                edge[s, n, f] = stage[s, pl.ds(offset, rows, stride=8), :].astype(BF)
                for t in range(2):
                    ends = pl.ds(offset + t * (rows - 2) * 8, 2, stride=8)
                    cstage[s, t, n, 2 * f : 2 * f + 2] = stage[s, ends, :]
    rest = jnp.zeros((8, C), F32)
    for s in range(2):
        for t in range(2):
            for n in range(2):
                corner[s, t, n] = jnp.concatenate([cstage[s, t, n], rest], axis=0).astype(BF)

    plan = [
        (edge.at[0], z.at[1]),
        (edge.at[1], z.at[0]),
        (frames.at[:, pl.ds(0, 2)], x.at[:, pl.ds(rows + 2, 2)]),
        (frames.at[:, pl.ds(rows - 2, 2)], x.at[:, pl.ds(0, 2)]),
        (corner.at[0, 0], zc.at[1, 1]),
        (corner.at[1, 0], zc.at[0, 1]),
        (corner.at[0, 1], zc.at[1, 0]),
        (corner.at[1, 1], zc.at[0, 0]),
    ]
    sends = [
        pltpu.make_async_remote_copy(
            src_ref=src, dst_ref=dst, send_sem=send_sem.at[i], recv_sem=recv_sem.at[i],
            device_id=(tm, at(around[i][0])), device_id_type=MESH,
        )
        for i, (src, dst) in enumerate(plan)
    ]
    comes = [around[i ^ 1][1] if i < 4 else around[11 - i][1] for i in range(8)]
    in_tile = lax.broadcasted_iota(jnp.int32, (1, 8, C), 1)

    def widen(f, start, size):
        wide = x[f, pl.ds(start, size)].astype(F32)
        no_last = jnp.concatenate([wide[:, : cols - 8], jnp.where(in_tile == 7, 0.0, wide[:, cols - 8 :])], axis=1)
        no_first = jnp.concatenate([jnp.where(in_tile == 0, 0.0, wide[:, :8]), wide[:, 8:]], axis=1)
        x3[f, pl.ds(start, size), :, 0:C] = pltpu.roll(no_last, 1, 1).astype(BF)
        x3[f, pl.ds(start, size), :, C : 2 * C] = pltpu.roll(no_first, cols - 1, 1).astype(BF)
        return wide

    def frame_rows(f, here):
        return [x3[f, here, :, 0:C], x[f, here], x3[f, here, :, C : 2 * C]]

    def exchange(i, src, dst):
        return pltpu.make_async_remote_copy(
            src_ref=src, dst_ref=dst, send_sem=tsend_sem.at[i], recv_sem=trecv_sem.at[i],
            device_id=(1 - tm, me), device_id_type=MESH,
        )

    half = pairs // 2
    chunks = [(1, half), (1 + half, pairs - 1 - half)]
    hands = [exchange(n, lo.at[pl.ds(q, size)], inc.at[pl.ds(q, size)]) for n, (q, size) in enumerate(chunks)]
    late_hands = [
        exchange(2, lo.at[pl.ds(0, 1)], inc.at[pl.ds(0, 1)]),
        exchange(3, lo.at[pl.ds(pairs, 1)], inc.at[pl.ds(pairs, 1)]),
        exchange(4, so, si),
    ]
    weights1 = pw1.reshape(4 * TAPS * C, 2 * C)
    weights2 = pw2.reshape(4 * TAPS * C, 2 * C)

    def loc_rows(q, size):
        return pl.ds((2 * q + 7) * cols, size * 2 * cols)

    def recur(f, q, size, drive):
        drive = drive.reshape(size, cols, 2 * C)
        drive = jnp.stack([drive[:, :, :C], drive[:, :, C:]], axis=1).reshape(size * 2 * cols, C)
        here = loc_rows(q, size)
        if f > 0:
            drive = decay[f : f + 1, :] * loc[f - 1, here] + drive
        loc[f, here] = drive
        if f == count - 1:
            lo[pl.ds(q, size)] = drive.astype(BF).reshape(size, 2, cols, C)

    def first_conv(n):
        q, size = chunks[n]
        for f in range(count):
            end = rows + 2 if n else 2 * half + 4
            for start in range(2 + n * (2 * half + 2), end, 2):
                widen(f, start, 2)
            lhs = pair_rows(frame_rows(f, pl.ds(2 * q, 2 * size + 2)), size)
            recur(f, q, size, mm(lhs, weights1[...]))

    def send_far():
        for i, opposite in ((2, 3), (3, 2), (4, 7), (5, 6), (6, 5), (7, 4), (0, 1), (1, 0)):
            @pl.when(far[i])
            def _():
                pl.semaphore_wait(far_sem.at[opposite], 1)
                sends[i].start()

    for i in (1, 5, 7, 4, 6, 3, 2):
        pl.when(near[i])(sends[i].start)
    for c in placed[first_needed:]:
        c.start()
    pair_zeros(pw1)
    for c in placed[:first_needed]:
        c.wait()
    first_conv(0)
    hands[0].start()
    pl.when(near[0])(sends[0].start)
    first_conv(1)
    hands[1].start()
    pl.when(both(starts_line, jnp.logical_not(first)))(send_far)

    factors = []
    for f in range(count):
        keep = decay[f : f + 1, :]
        factors.append(keep * jnp.where(tm == 0, 0.0, 1.0) if f == 0 else factors[-1] * keep)

    def settle(f, q, real=(None, None)):
        state = loc[f, loc_rows(q, 1)].reshape(2, cols, C) + factors[f] * inc[q].astype(F32)
        first = jnp.where(in_tile == 0, 0.0, state[:, :8])
        last = jnp.where(in_tile == 7, 0.0, state[:, cols - 8 :])
        state = jnp.concatenate([first, state[:, 8 : cols - 8], last], axis=1)
        state = jnp.concatenate(
            [state[e : e + 1] if r is None else jnp.where(r, state[e : e + 1], 0.0) for e, r in enumerate(real)],
            axis=0,
        )
        here = pl.ds(2 * q, 2)
        s3[f, here, :, 0:C] = pltpu.roll(state, 1, 1).astype(BF)
        s3[f, here, :, C : 2 * C] = state.astype(BF)
        s3[f, here, :, 2 * C : 3 * C] = pltpu.roll(state, cols - 1, 1).astype(BF)

    def finish(f, p, size, result):
        result = result.reshape(size, cols, 2 * C)
        result = jnp.stack([result[:, :, :C], result[:, :, C:]], axis=1).reshape(2 * size, cols, C)
        mixed = result + skip[...] * x[f, pl.ds(2 + 2 * p, 2 * size)].astype(F32)
        ot[0, f, pl.ds(16 * p, 16 * size)] = mixed[:, :8].reshape(16 * size, C)
        ot[1, f, pl.ds(16 * p, 16 * size)] = mixed[:, cols - 8 :].reshape(16 * size, C)
        o[f, pl.ds(2 * p, 2 * size), 8 : cols - 8] = mixed[:, 8 : cols - 8].astype(BF)

    pair_zeros(pw2)
    side_zeros(sw1, SIDE_IN)
    side_zeros(sw2, SIDE_OUT)
    for i, (_, dst) in enumerate(plan):
        @pl.when(jnp.logical_not(comes[i]))
        def _():
            dst[...] = jnp.zeros(dst.shape, BF)

    for c in placed[first_needed:then_needed]:
        c.wait()
    inner = [(1, half - 1), (half, half - 1)]

    def second_conv(n, which):
        q, size = chunks[n]
        p, deep = inner[n]
        for f in which:
            for i in range(q, q + size):
                settle(f, i)
            lhs = pair_rows([s3[f, 2 * p : 2 * p + 2 * deep + 2]], deep)
            finish(f, p, deep, mm(lhs, weights2[...]))

    hands[0].wait_recv()
    second_conv(0, range(count))
    hands[1].wait_recv()
    second_conv(1, range(count // 2))

    pl.when(first)(send_far)

    def arrive(*which):
        for i in which:
            pl.when(comes[i])(sends[i].wait_recv)

    arrive(2, 3)
    for f in range(count):
        for t in range(2):
            wide = widen(f, t * (rows + 2), 2)
            rim[t, 0, 16 * f : 16 * f + 16] = wide[:, :8].reshape(16, C)
            rim[t, 1, 16 * f : 16 * f + 16] = wide[:, cols - 8 :].reshape(16, C)
    lhs = [pair_rows(frame_rows(f, pl.ds(2 * q, 4)), 1) for q in (0, pairs) for f in range(count)]
    drive = mm_halves(jnp.concatenate(lhs, axis=0), weights1[...])
    for n, q in enumerate((0, pairs)):
        for f in range(count):
            recur(f, q, 1, drive[(n * count + f) * cols : (n * count + f + 1) * cols])
    late_hands[0].start()
    late_hands[1].start()

    sides_at = jnp.where(first, 1, 0)

    @pl.loop(0, 2)
    def _(step):
        @pl.when(step == sides_at)
        def _():
            for c in placed[then_needed:]:
                c.wait()
            arrive(0, 4, 6, 1, 5, 7)
            for s in range(2):
                lines = [jnp.concatenate([z[s, 0, f], z[s, 1, f], edge[s, 0, f]], axis=-1) for f in range(count)]
                for t in range(2):
                    mine = jnp.concatenate([rim[t, s, pl.ds(7 * s, 8, stride=8), :], rest], axis=0).astype(BF)
                    lines.append(jnp.concatenate([zc[s, t, 0], zc[s, t, 1], mine], axis=-1))
                lhs = jnp.concatenate(lines, axis=0)
                for a in range(3):
                    result = mm(lhs, sw1[s, a].reshape(3 * C, 2 * C))
                    for e in range(2):
                        part = result[:, e * C : (e + 1) * C]
                        for f in range(count):
                            base = 2 * (8 + f * tall)
                            y[s, a, e, pl.ds(base + 16, rows, stride=2), :] = part[f * rows : (f + 1) * rows]
                            for t in range(2):
                                begin = count * rows + 16 * t + 2 * f
                                y[s, a, e, pl.ds(base + 12 + t * 2 * (rows + 2), 2, stride=2), :] = part[begin : begin + 2]

            for s in range(2):
                inside = jnp.where(left if s == 0 else right, 1.0, 0.0).astype(F32)
                for e in range(2):
                    state = None
                    for f in range(count):
                        base = 2 * (8 + f * tall)
                        drive = sum(y[s, a, e, pl.ds(base + 2 * (a - 1), tall, stride=2), :] for a in range(3))
                        if e == 0:
                            drive = drive * inside
                        state = drive if f == 0 else decay[f : f + 1, :] * state + drive
                        whole = state
                        if e == 1:
                            whole = state + loc[f, pl.ds(s * (cols - 1), tall, stride=cols), :]
                        ss[s, e, f] = whole
                    so[s, e] = whole.astype(BF)
            late_hands[2].start()

        @pl.when(step != sides_at)
        def _():
            second_conv(1, range(count // 2, count))
            late_hands[0].wait_recv()
            late_hands[1].wait_recv()
            for f in range(count):
                settle(f, 0, (up, None))
                settle(f, pairs, (None, down))
            lhs = [pair_rows([s3[f, 2 * p : 2 * p + 4]], 1) for p in (0, pairs - 1) for f in range(count)]
            result = mm_halves(jnp.concatenate(lhs, axis=0), weights2[...])
            for n, p in enumerate((0, pairs - 1)):
                for f in range(count):
                    finish(f, p, 1, result[(n * count + f) * cols : (n * count + f + 1) * cols])

    late_hands[2].wait_recv()
    place = lax.broadcasted_iota(jnp.int32, (tall, C), 0)
    off = jnp.logical_or(
        both(place == 7, jnp.logical_not(up)), both(place == rows + 8, jnp.logical_not(down))
    )
    for s in range(2):
        sides = []
        for f in range(count):
            pair = [
                jnp.where(off, 0.0, ss[s, e, f] + factors[f] * si[s, e].astype(F32)).astype(BF) for e in range(2)
            ]
            sides.append(jnp.concatenate(pair, axis=-1))
        lhs = jnp.concatenate(sides, axis=0)
        for a in range(3):
            result = mm(lhs, sw2[s, a].reshape(2 * C, 2 * C))
            for e in range(2):
                y2[s, a, e, pl.ds(16, count * tall, stride=2), :] = result[:, e * C : (e + 1) * C]

    for f in range(count):
        base = 2 * (8 + f * tall + 8)
        for s in range(2):
            for e in range(2):
                here = pl.ds(e if s == 0 else 7 - e, rows, stride=8)
                fix = sum(y2[s, a, e, pl.ds(base + 2 * (a - 1), rows, stride=2), :] for a in range(3))
                ot[s, f, here, :] = ot[s, f, here, :] + fix
        o[f, :, 0:8] = ot[0, f].reshape(rows, 8, C).astype(BF)
        o[f, :, cols - 8 :] = ot[1, f].reshape(rows, 8, C).astype(BF)

    for i, c in enumerate(sends):
        pl.when(around[i][1])(c.wait_send)
    for c in hands + late_hands:
        c.wait_send()


def write_out(o, out, sem):
    stores = [pltpu.make_async_copy(o.at[f], out.at[f], sem.at[f]) for f in range(o.shape[0])]
    for c in stores:
        c.start()
    for c in stores:
        c.wait()


def per_device(frames, w_in, w_out, decay, skip):
    count, _, rows, cols, _ = frames.shape
    tall = rows + 16
    spread = 2 * (count * tall + 16)
    hbm = pl.BlockSpec(memory_space=pltpu.HBM)
    vmem = pl.BlockSpec(memory_space=pltpu.VMEM)
    args = (frames[:, 0], w_in, w_out, decay, skip.reshape(1, C))
    out = pl.pallas_call(
        functools.partial(kernel, TROWS),
        out_shape=pltpu.VMEM((count, rows, cols, C), BF),
        in_specs=[hbm] * 5,
        out_specs=vmem,
        scratch_shapes=[
            pltpu.VMEM((count, rows + 4, cols, C), BF),
            pltpu.VMEM((count, rows + 4, cols, 2 * C), BF),
            pltpu.VMEM((count, rows + 2, cols, 3 * C), BF),
            pltpu.VMEM((count, tall * cols, C), F32),
            pltpu.VMEM((4 * TAPS, C, 2 * C), BF),
            pltpu.VMEM((4 * TAPS, C, 2 * C), BF),
            pltpu.VMEM((2, TAPS, 3, C, 2 * C), BF),
            pltpu.VMEM((2, TAPS, 2, C, 2 * C), BF),
            pltpu.VMEM((2, 2, count, rows, C), BF),
            pltpu.VMEM((2, 2, 2, 16, C), BF),
            pltpu.VMEM((2, 2, count, rows, C), BF),
            pltpu.VMEM((2, 2, 2, 16, C), BF),
            pltpu.VMEM((2, TAPS, 2, spread, C), F32),
            pltpu.VMEM((2, TAPS, 2, spread, C), F32),
            pltpu.VMEM((2, 2, count, tall, C), F32),
            pltpu.VMEM((2, rows * 8, C), F32),
            pltpu.VMEM((2, 2, 2, 8, C), F32),
            pltpu.VMEM((2, 2, 16 * count, C), F32),
            pltpu.VMEM((rows // 2 + 1, 2, cols, C), BF),
            pltpu.VMEM((rows // 2 + 1, 2, cols, C), BF),
            pltpu.VMEM((2, 2, tall, C), BF),
            pltpu.VMEM((2, 2, tall, C), BF),
            pltpu.VMEM((2, count, rows * 8, C), F32),
            pltpu.VMEM((count, C), F32),
            pltpu.VMEM((1, C), F32),
            pltpu.SemaphoreType.DMA((count,)),
            pltpu.SemaphoreType.DMA((28,)),
            pltpu.SemaphoreType.DMA((8,)),
            pltpu.SemaphoreType.DMA((8,)),
            pltpu.SemaphoreType.DMA((5,)),
            pltpu.SemaphoreType.DMA((5,)),
            pltpu.SemaphoreType.REGULAR((8,)),
        ],
        compiler_params=pltpu.CompilerParams(
            collective_id=0, has_side_effects=True, vmem_limit_bytes=48 * 2**20
        ),
    )(*(pltpu.with_memory_space_constraint(a, pltpu.HBM) for a in args))
    out = pl.pallas_call(
        write_out,
        out_shape=jax.ShapeDtypeStruct(out.shape, BF),
        in_specs=[vmem],
        out_specs=hbm,
        scratch_shapes=[pltpu.SemaphoreType.DMA((count,))],
        compiler_params=pltpu.CompilerParams(vmem_limit_bytes=2**20),
    )(pltpu.with_memory_space_constraint(out, pltpu.VMEM))
    return out.reshape(count, 1, rows, cols, C)


def solution(mesh):
    return jax.shard_map(
        per_device,
        mesh=mesh,
        in_specs=(P("tm", "tile", None, None, None), P(), P(), P("tm", None), P()),
        out_specs=P("tm", "tile", None, None, None),
        check_vma=False,
    )
```

```python
import functools

import jax
import jax.numpy as jnp
from jax import lax
from jax.experimental import pallas as pl
from jax.experimental.pallas import tpu as pltpu
from jax.sharding import PartitionSpec as P

TROWS = 4
LINE = 4
C = 128
BF = jnp.bfloat16
F32 = jnp.float32
MESH = pl.DeviceIdType.MESH

TAPS = 3
PIECES = 1


def mm(lhs, rhs):
    return jnp.dot(lhs, rhs, preferred_element_type=F32)


def mm_halves(lhs, rhs):
    half = lhs.shape[1] // 2
    return mm(lhs[:, :half], rhs[:half]) + mm(lhs[:, half:], rhs[half:])


def pair_zeros(pair):
    zero = jnp.zeros((TAPS, C, C), BF)
    pair[3 * TAPS : 4 * TAPS, :, 0:C] = zero
    pair[0:TAPS, :, C : 2 * C] = zero


def pair_copies(w, pair):
    return [
        (w.at[i], pair.at[pl.ds((i + e) * TAPS, TAPS), :, pl.ds(e * C, C)]) for i in range(TAPS) for e in range(2)
    ]


def side_blocks(table):
    return [(s, k, e, b) for s in range(2) for k, taps in enumerate(table[s]) for e, b in enumerate(taps)]


def side_zeros(side, table):
    for s, k, e, b in side_blocks(table):
        if b is None:
            side[s, :, k, :, e * C : (e + 1) * C] = jnp.zeros((TAPS, C, C), BF)


def side_copies(w, side, table):
    return [
        (w.at[:, b], side.at[s, :, k, :, pl.ds(e * C, C)]) for s, k, e, b in side_blocks(table) if b is not None
    ]


SIDE_IN = (((1, 0), (0, None), (2, None)), ((1, 2), (2, None), (0, None)))
SIDE_OUT = (((0, None), (1, 0)), ((2, None), (1, 2)))


def pair_rows(parts, pairs):
    cols = parts[0].shape[1]
    split = [p.reshape(pairs + 1, 2, cols, p.shape[2]) for p in parts]
    taps = []
    for first in (0, 1):
        for parity in (0, 1):
            taps += [p[first : first + pairs, parity] for p in split]
    return jnp.concatenate(taps, axis=-1).reshape(pairs * cols, 12 * C)


def kernel(
    trows, frames, w_in, w_out, decay_in, skip_in, o,
    x, x3, s3, loc, pw1, pw2, sw1, sw2, edge, corner, z, zc, y, y2, ss, stage, cstage, rim, lo, inc, so, si, ot, decay, skip,
    load_sem, w_sem, send_sem, recv_sem, tsend_sem, trecv_sem, far_sem,
):
    count, rows, cols, _ = frames.shape
    tiles = lax.axis_size("tile")
    tcols = tiles // trows
    me = lax.axis_index("tile")
    tm = lax.axis_index("tm")
    k = lax.rem(me + tiles - 1, tiles)
    column = lax.rem(k, tcols)
    row_index = k // tcols
    up, down = row_index > 0, row_index < trows - 1
    left, right = column > 0, column < tcols - 1
    pairs = rows // 2
    tall = rows + 16

    loads = [
        pltpu.make_async_copy(frames.at[f], x.at[f, pl.ds(2, rows)], load_sem.at[f])
        for f in range(count)
    ]
    for c in loads:
        c.start()

    both = jnp.logical_and
    around = [
        (-1, left), (1, right), (-tcols, up), (tcols, down),
        (-tcols - 1, both(up, left)), (-tcols + 1, both(up, right)),
        (tcols - 1, both(down, left)), (tcols + 1, both(down, right)),
    ]

    def at(by):
        return lax.rem(me + by + tiles, tiles)

    first = me == 0
    starts_line = lax.rem(me, LINE) == 0
    far, far_for = [], []
    for i, (by, there) in enumerate(around):
        far.append(both(there, starts_line if i in (0, 4, 6) else first))
        target_far = lax.rem(at(by), LINE) == 0 if i in (1, 5, 7) else at(by) == 0
        far_for.append(both(there, target_far))
    near = [both(there, jnp.logical_not(far[i])) for i, (_, there) in enumerate(around)]

    barrier = pltpu.get_barrier_semaphore()
    greeted = jnp.int32(1)
    for i, (by, there) in enumerate(around):
        greeted = greeted + near[i].astype(jnp.int32)

        @pl.when(both(there, jnp.logical_not(far_for[i])))
        def _():
            pl.semaphore_signal(barrier, inc=1, device_id=(tm, at(by)), device_id_type=MESH)

    pl.semaphore_signal(barrier, inc=1, device_id=(1 - tm, me), device_id_type=MESH)

    placed = pair_copies(w_in, pw1) + [(decay_in, decay), (skip_in, skip)]
    first_needed = len(placed)
    placed += pair_copies(w_out, pw2)
    then_needed = len(placed)
    placed += side_copies(w_in, sw1, SIDE_IN) + side_copies(w_out, sw2, SIDE_OUT)
    placed = [pltpu.make_async_copy(src, dst, w_sem.at[i]) for i, (src, dst) in enumerate(placed)]
    for c in placed[:first_needed]:
        c.start()

    pl.semaphore_wait(barrier, greeted)
    for i, (by, _) in enumerate(around):
        @pl.when(far_for[i])
        def _():
            pl.semaphore_signal(far_sem.at[i], inc=1, device_id=(tm, at(by)), device_id_type=MESH)

    def edges(s, f):
        begin, keep = (0, slice(0, 8)) if s == 0 else (cols - 16, slice(8, 16))
        stage[s] = x[f, 2 : 2 + rows, begin : begin + 16, :].astype(F32)[:, keep, :].reshape(rows * 8, C)
        for n in range(2):
            offset = n if s == 0 else 7 - n
            edge[s, n, f] = stage[s, pl.ds(offset, rows, stride=8), :].astype(BF)
            for t in range(2):
                ends = pl.ds(offset + t * (rows - 2) * 8, 2, stride=8)
                cstage[s, t, n, 2 * f : 2 * f + 2] = stage[s, ends, :]

    plan = [
        (edge.at[0], z.at[1]),
        (edge.at[1], z.at[0]),
        (frames.at[:, pl.ds(0, 2)], x.at[:, pl.ds(rows + 2, 2)]),
        (frames.at[:, pl.ds(rows - 2, 2)], x.at[:, pl.ds(0, 2)]),
        (corner.at[0, 0], zc.at[1, 1]),
        (corner.at[1, 0], zc.at[0, 1]),
        (corner.at[0, 1], zc.at[1, 0]),
        (corner.at[1, 1], zc.at[0, 0]),
    ]
    sends = [
        pltpu.make_async_remote_copy(
            src_ref=src, dst_ref=dst, send_sem=send_sem.at[i], recv_sem=recv_sem.at[i],
            device_id=(tm, at(around[i][0])), device_id_type=MESH,
        )
        for i, (src, dst) in enumerate(plan)
    ]
    for f in range(count):
        loads[f].wait()
        edges(1, f)
    pl.when(near[1])(sends[1].start)
    for f in range(count):
        edges(0, f)
    rest = jnp.zeros((8, C), F32)
    for s in range(2):
        for t in range(2):
            for n in range(2):
                corner[s, t, n] = jnp.concatenate([cstage[s, t, n], rest], axis=0).astype(BF)

    comes = [around[i ^ 1][1] if i < 4 else around[11 - i][1] for i in range(8)]
    in_tile = lax.broadcasted_iota(jnp.int32, (1, 8, C), 1)

    def widen(f, start, size):
        wide = x[f, pl.ds(start, size)].astype(F32)
        no_last = jnp.concatenate([wide[:, : cols - 8], jnp.where(in_tile == 7, 0.0, wide[:, cols - 8 :])], axis=1)
        no_first = jnp.concatenate([jnp.where(in_tile == 0, 0.0, wide[:, :8]), wide[:, 8:]], axis=1)
        x3[f, pl.ds(start, size), :, 0:C] = pltpu.roll(no_last, 1, 1).astype(BF)
        x3[f, pl.ds(start, size), :, C : 2 * C] = pltpu.roll(no_first, cols - 1, 1).astype(BF)
        return wide

    def frame_rows(f, here):
        return [x3[f, here, :, 0:C], x[f, here], x3[f, here, :, C : 2 * C]]

    def exchange(i, src, dst):
        return pltpu.make_async_remote_copy(
            src_ref=src, dst_ref=dst, send_sem=tsend_sem.at[i], recv_sem=trecv_sem.at[i],
            device_id=(1 - tm, me), device_id_type=MESH,
        )

    half = pairs // 2
    chunks = [(1, half), (1 + half, pairs - 1 - half)]
    hands = [exchange(n, lo.at[pl.ds(q, size)], inc.at[pl.ds(q, size)]) for n, (q, size) in enumerate(chunks)]
    late_hands = [
        exchange(2, lo.at[pl.ds(0, 1)], inc.at[pl.ds(0, 1)]),
        exchange(3, lo.at[pl.ds(pairs, 1)], inc.at[pl.ds(pairs, 1)]),
        exchange(4, so.at[0], si.at[0]),
        exchange(5, so.at[1], si.at[1]),
    ]
    weights1 = pw1.reshape(4 * TAPS * C, 2 * C)
    weights2 = pw2.reshape(4 * TAPS * C, 2 * C)

    def loc_rows(q, size):
        return pl.ds((2 * q + 7) * cols, size * 2 * cols)

    def recur(f, q, size, drive):
        drive = drive.reshape(size, cols, 2 * C)
        drive = jnp.stack([drive[:, :, :C], drive[:, :, C:]], axis=1).reshape(size * 2 * cols, C)
        here = loc_rows(q, size)
        if f > 0:
            drive = decay[f : f + 1, :] * loc[f - 1, here] + drive
        loc[f, here] = drive
        if f == count - 1:
            lo[pl.ds(q, size)] = drive.astype(BF).reshape(size, 2, cols, C)

    def first_conv(n):
        q, size = chunks[n]
        for f in range(count):
            end = rows + 2 if n else 2 * half + 4
            for start in range(2 + n * (2 * half + 2), end, 2):
                widen(f, start, 2)
            lhs = pair_rows(frame_rows(f, pl.ds(2 * q, 2 * size + 2)), size)
            recur(f, q, size, mm(lhs, weights1[...]))

    def send_far():
        for i, opposite in ((0, 1), (4, 7), (6, 5), (2, 3), (3, 2), (1, 0), (5, 6), (7, 4)):
            @pl.when(far[i])
            def _():
                pl.semaphore_wait(far_sem.at[opposite], 1)
                sends[i].start()

    for i in (5, 7, 4, 6, 3, 2):
        pl.when(near[i])(sends[i].start)
    for c in placed[first_needed:]:
        c.start()
    pair_zeros(pw1)
    for c in placed[:first_needed]:
        c.wait()
    first_conv(0)
    hands[0].start()
    pl.when(near[0])(sends[0].start)
    first_conv(1)
    hands[1].start()
    pl.when(both(starts_line, jnp.logical_not(first)))(send_far)

    factors = []
    for f in range(count):
        keep = decay[f : f + 1, :]
        factors.append(keep * jnp.where(tm == 0, 0.0, 1.0) if f == 0 else factors[-1] * keep)

    def settle(f, q, real=(None, None)):
        state = loc[f, loc_rows(q, 1)].reshape(2, cols, C) + factors[f] * inc[q].astype(F32)
        first = jnp.where(in_tile == 0, 0.0, state[:, :8])
        last = jnp.where(in_tile == 7, 0.0, state[:, cols - 8 :])
        state = jnp.concatenate([first, state[:, 8 : cols - 8], last], axis=1)
        state = jnp.concatenate(
            [state[e : e + 1] if r is None else jnp.where(r, state[e : e + 1], 0.0) for e, r in enumerate(real)],
            axis=0,
        )
        here = pl.ds(2 * q, 2)
        s3[f, here, :, 0:C] = pltpu.roll(state, 1, 1).astype(BF)
        s3[f, here, :, C : 2 * C] = state.astype(BF)
        s3[f, here, :, 2 * C : 3 * C] = pltpu.roll(state, cols - 1, 1).astype(BF)

    def finish(f, p, size, result):
        result = result.reshape(size, cols, 2 * C)
        result = jnp.stack([result[:, :, :C], result[:, :, C:]], axis=1).reshape(2 * size, cols, C)
        mixed = result + skip[...] * x[f, pl.ds(2 + 2 * p, 2 * size)].astype(F32)
        ot[0, f, pl.ds(16 * p, 16 * size)] = mixed[:, :8].reshape(16 * size, C)
        ot[1, f, pl.ds(16 * p, 16 * size)] = mixed[:, cols - 8 :].reshape(16 * size, C)
        o[f, pl.ds(2 * p, 2 * size), 8 : cols - 8] = mixed[:, 8 : cols - 8].astype(BF)

    pair_zeros(pw2)
    side_zeros(sw1, SIDE_IN)
    side_zeros(sw2, SIDE_OUT)
    for i, (_, dst) in enumerate(plan):
        @pl.when(jnp.logical_not(comes[i]))
        def _():
            dst[...] = jnp.zeros(dst.shape, BF)

    for c in placed[first_needed:then_needed]:
        c.wait()
    inner = [(1, half - 1), (half, half - 1)]

    def second_conv(n, which):
        q, size = chunks[n]
        p, deep = inner[n]
        for f in which:
            for i in range(q, q + size):
                settle(f, i)
            lhs = pair_rows([s3[f, 2 * p : 2 * p + 2 * deep + 2]], deep)
            finish(f, p, deep, mm(lhs, weights2[...]))

    hands[0].wait_recv()
    second_conv(0, range(count))
    hands[1].wait_recv()
    second_conv(1, range(count // 2))

    pl.when(first)(send_far)

    def arrive(*which):
        for i in which:
            pl.when(comes[i])(sends[i].wait_recv)

    arrive(2, 3)
    for f in range(count):
        for t in range(2):
            wide = widen(f, t * (rows + 2), 2)
            rim[t, 0, 16 * f : 16 * f + 16] = wide[:, :8].reshape(16, C)
            rim[t, 1, 16 * f : 16 * f + 16] = wide[:, cols - 8 :].reshape(16, C)
    lhs = [pair_rows(frame_rows(f, pl.ds(2 * q, 4)), 1) for q in (0, pairs) for f in range(count)]
    drive = mm_halves(jnp.concatenate(lhs, axis=0), weights1[...])
    for n, q in enumerate((0, pairs)):
        for f in range(count):
            recur(f, q, 1, drive[(n * count + f) * cols : (n * count + f + 1) * cols])
    late_hands[0].start()
    late_hands[1].start()

    def side_in(s):
        arrive(*((1, 5, 7) if s == 0 else (0, 4, 6)))
        lines = [jnp.concatenate([z[s, 0, f], z[s, 1, f], edge[s, 0, f]], axis=-1) for f in range(count)]
        for t in range(2):
            mine = jnp.concatenate([rim[t, s, pl.ds(7 * s, 8, stride=8), :], rest], axis=0).astype(BF)
            lines.append(jnp.concatenate([zc[s, t, 0], zc[s, t, 1], mine], axis=-1))
        lhs = jnp.concatenate(lines, axis=0)
        for a in range(3):
            result = mm(lhs, sw1[s, a].reshape(3 * C, 2 * C))
            for e in range(2):
                part = result[:, e * C : (e + 1) * C]
                for f in range(count):
                    base = 2 * (8 + f * tall)
                    y[s, a, e, pl.ds(base + 16, rows, stride=2), :] = part[f * rows : (f + 1) * rows]
                    for t in range(2):
                        begin = count * rows + 16 * t + 2 * f
                        y[s, a, e, pl.ds(base + 12 + t * 2 * (rows + 2), 2, stride=2), :] = part[begin : begin + 2]
        inside = jnp.where(left if s == 0 else right, 1.0, 0.0).astype(F32)
        for e in range(2):
            state = None
            for f in range(count):
                base = 2 * (8 + f * tall)
                drive = sum(y[s, a, e, pl.ds(base + 2 * (a - 1), tall, stride=2), :] for a in range(3))
                if e == 0:
                    drive = drive * inside
                state = drive if f == 0 else decay[f : f + 1, :] * state + drive
                whole = state
                if e == 1:
                    whole = state + loc[f, pl.ds(s * (cols - 1), tall, stride=cols), :]
                ss[s, e, f] = whole
            so[s, e] = whole.astype(BF)
        late_hands[2 + s].start()

    def side_out(s):
        late_hands[2 + s].wait_recv()
        place = lax.broadcasted_iota(jnp.int32, (tall, C), 0)
        off = jnp.logical_or(
            both(place == 7, jnp.logical_not(up)), both(place == rows + 8, jnp.logical_not(down))
        )
        sides = []
        for f in range(count):
            pair = [
                jnp.where(off, 0.0, ss[s, e, f] + factors[f] * si[s, e].astype(F32)).astype(BF) for e in range(2)
            ]
            sides.append(jnp.concatenate(pair, axis=-1))
        lhs = jnp.concatenate(sides, axis=0)
        for a in range(3):
            result = mm(lhs, sw2[s, a].reshape(2 * C, 2 * C))
            for e in range(2):
                y2[s, a, e, pl.ds(16, count * tall, stride=2), :] = result[:, e * C : (e + 1) * C]
        begin = s * (cols - 8)
        for f in range(count):
            base = 2 * (8 + f * tall + 8)
            for e in range(2):
                here = pl.ds(e if s == 0 else 7 - e, rows, stride=8)
                fix = sum(y2[s, a, e, pl.ds(base + 2 * (a - 1), rows, stride=2), :] for a in range(3))
                ot[s, f, here, :] = ot[s, f, here, :] + fix
            o[f, :, begin : begin + 8] = ot[s, f].reshape(rows, 8, C).astype(BF)

    for c in placed[then_needed:]:
        c.wait()
    ends_line = lax.rem(me, LINE) == LINE - 1
    orders = ((ends_line, 0, 1), (jnp.logical_not(ends_line), 1, 0))
    for here, early, last in orders:
        @pl.when(here)
        def _():
            side_in(early)

    second_conv(1, range(count // 2, count))
    late_hands[0].wait_recv()
    late_hands[1].wait_recv()
    for f in range(count):
        settle(f, 0, (up, None))
        settle(f, pairs, (None, down))
    lhs = [pair_rows([s3[f, 2 * p : 2 * p + 4]], 1) for p in (0, pairs - 1) for f in range(count)]
    result = mm_halves(jnp.concatenate(lhs, axis=0), weights2[...])
    for n, p in enumerate((0, pairs - 1)):
        for f in range(count):
            finish(f, p, 1, result[(n * count + f) * cols : (n * count + f + 1) * cols])

    for here, early, last in orders:
        @pl.when(here)
        def _():
            side_in(last)
            side_out(early)
            side_out(last)

    for i, c in enumerate(sends):
        pl.when(around[i][1])(c.wait_send)
    for c in hands + late_hands:
        c.wait_send()


def write_out(o, out, sem):
    size = o.shape[1] // PIECES
    stores = [
        pltpu.make_async_copy(
            o.at[f, pl.ds(n * size, size)], out.at[f, pl.ds(n * size, size)], sem.at[f, n]
        )
        for f in range(o.shape[0])
        for n in range(PIECES)
    ]
    for c in stores:
        c.start()
    for c in stores:
        c.wait()


def per_device(frames, w_in, w_out, decay, skip):
    count, _, rows, cols, _ = frames.shape
    tall = rows + 16
    spread = 2 * (count * tall + 16)
    hbm = pl.BlockSpec(memory_space=pltpu.HBM)
    vmem = pl.BlockSpec(memory_space=pltpu.VMEM)
    args = (frames[:, 0], w_in, w_out, decay, skip.reshape(1, C))
    out = pl.pallas_call(
        functools.partial(kernel, TROWS),
        out_shape=pltpu.VMEM((count, rows, cols, C), BF),
        in_specs=[hbm] * 5,
        out_specs=vmem,
        scratch_shapes=[
            pltpu.VMEM((count, rows + 4, cols, C), BF),
            pltpu.VMEM((count, rows + 4, cols, 2 * C), BF),
            pltpu.VMEM((count, rows + 2, cols, 3 * C), BF),
            pltpu.VMEM((count, tall * cols, C), F32),
            pltpu.VMEM((4 * TAPS, C, 2 * C), BF),
            pltpu.VMEM((4 * TAPS, C, 2 * C), BF),
            pltpu.VMEM((2, TAPS, 3, C, 2 * C), BF),
            pltpu.VMEM((2, TAPS, 2, C, 2 * C), BF),
            pltpu.VMEM((2, 2, count, rows, C), BF),
            pltpu.VMEM((2, 2, 2, 16, C), BF),
            pltpu.VMEM((2, 2, count, rows, C), BF),
            pltpu.VMEM((2, 2, 2, 16, C), BF),
            pltpu.VMEM((2, TAPS, 2, spread, C), F32),
            pltpu.VMEM((2, TAPS, 2, spread, C), F32),
            pltpu.VMEM((2, 2, count, tall, C), F32),
            pltpu.VMEM((2, rows * 8, C), F32),
            pltpu.VMEM((2, 2, 2, 8, C), F32),
            pltpu.VMEM((2, 2, 16 * count, C), F32),
            pltpu.VMEM((rows // 2 + 1, 2, cols, C), BF),
            pltpu.VMEM((rows // 2 + 1, 2, cols, C), BF),
            pltpu.VMEM((2, 2, tall, C), BF),
            pltpu.VMEM((2, 2, tall, C), BF),
            pltpu.VMEM((2, count, rows * 8, C), F32),
            pltpu.VMEM((count, C), F32),
            pltpu.VMEM((1, C), F32),
            pltpu.SemaphoreType.DMA((count,)),
            pltpu.SemaphoreType.DMA((28,)),
            pltpu.SemaphoreType.DMA((8,)),
            pltpu.SemaphoreType.DMA((8,)),
            pltpu.SemaphoreType.DMA((6,)),
            pltpu.SemaphoreType.DMA((6,)),
            pltpu.SemaphoreType.REGULAR((8,)),
        ],
        compiler_params=pltpu.CompilerParams(
            collective_id=0, has_side_effects=True, vmem_limit_bytes=48 * 2**20
        ),
    )(*(pltpu.with_memory_space_constraint(a, pltpu.HBM) for a in args))
    out = pl.pallas_call(
        write_out,
        out_shape=jax.ShapeDtypeStruct(out.shape, BF),
        in_specs=[vmem],
        out_specs=hbm,
        scratch_shapes=[pltpu.SemaphoreType.DMA((count, PIECES))],
        compiler_params=pltpu.CompilerParams(vmem_limit_bytes=2**20),
    )(pltpu.with_memory_space_constraint(out, pltpu.VMEM))
    return out.reshape(count, 1, rows, cols, C)


def solution(mesh):
    return jax.shard_map(
        per_device,
        mesh=mesh,
        in_specs=(P("tm", "tile", None, None, None), P(), P(), P("tm", None), P()),
        out_specs=P("tm", "tile", None, None, None),
        check_vma=False,
    )
```

```python
import functools

import jax
import jax.numpy as jnp
from jax import lax
from jax.experimental import pallas as pl
from jax.experimental.pallas import tpu as pltpu
from jax.sharding import PartitionSpec as P

TROWS = 4
LINE = 4
C = 128
BF = jnp.bfloat16
F32 = jnp.float32
MESH = pl.DeviceIdType.MESH

TAPS = 3
PIECES = 1


def mm(lhs, rhs):
    return jnp.dot(lhs, rhs, preferred_element_type=F32)


def mm_halves(lhs, rhs):
    half = lhs.shape[1] // 2
    return mm(lhs[:, :half], rhs[:half]) + mm(lhs[:, half:], rhs[half:])


def pair_zeros(pair):
    zero = jnp.zeros((TAPS, C, C), BF)
    pair[3 * TAPS : 4 * TAPS, :, 0:C] = zero
    pair[0:TAPS, :, C : 2 * C] = zero


def pair_copies(w, pair):
    return [
        (w.at[i], pair.at[pl.ds((i + e) * TAPS, TAPS), :, pl.ds(e * C, C)]) for i in range(TAPS) for e in range(2)
    ]


def side_blocks(table):
    return [(s, k, e, b) for s in range(2) for k, taps in enumerate(table[s]) for e, b in enumerate(taps)]


def side_zeros(side, table):
    for s, k, e, b in side_blocks(table):
        if b is None:
            side[s, :, k, :, e * C : (e + 1) * C] = jnp.zeros((TAPS, C, C), BF)


def side_copies(w, side, table):
    return [
        (w.at[:, b], side.at[s, :, k, :, pl.ds(e * C, C)]) for s, k, e, b in side_blocks(table) if b is not None
    ]


SIDE_IN = (((1, 0), (0, None), (2, None)), ((1, 2), (2, None), (0, None)))
SIDE_OUT = (((0, None), (1, 0)), ((2, None), (1, 2)))


def pair_rows(parts, pairs):
    cols = parts[0].shape[1]
    split = [p.reshape(pairs + 1, 2, cols, p.shape[2]) for p in parts]
    taps = []
    for first in (0, 1):
        for parity in (0, 1):
            taps += [p[first : first + pairs, parity] for p in split]
    return jnp.concatenate(taps, axis=-1).reshape(pairs * cols, 12 * C)


def kernel(
    trows, frames, w_in, w_out, decay_in, skip_in, o,
    x, x3, s3, loc, pw1, pw2, sw1, sw2, edge, corner, z, zc, y, y2, ss, stage, cstage, rim, lo, inc, so, si, ot, decay, skip,
    load_sem, w_sem, send_sem, recv_sem, tsend_sem, trecv_sem, far_sem,
):
    count, rows, cols, _ = frames.shape
    tiles = lax.axis_size("tile")
    tcols = tiles // trows
    me = lax.axis_index("tile")
    tm = lax.axis_index("tm")
    k = lax.rem(me + tiles - 1, tiles)
    column = lax.rem(k, tcols)
    row_index = k // tcols
    up, down = row_index > 0, row_index < trows - 1
    left, right = column > 0, column < tcols - 1
    pairs = rows // 2
    tall = rows + 16

    loads = [
        pltpu.make_async_copy(frames.at[f], x.at[f, pl.ds(2, rows)], load_sem.at[f])
        for f in range(count)
    ]
    for c in loads:
        c.start()

    both = jnp.logical_and
    around = [
        (-1, left), (1, right), (-tcols, up), (tcols, down),
        (-tcols - 1, both(up, left)), (-tcols + 1, both(up, right)),
        (tcols - 1, both(down, left)), (tcols + 1, both(down, right)),
    ]

    def at(by):
        return lax.rem(me + by + tiles, tiles)

    first = me == 0
    starts_line = lax.rem(me, LINE) == 0
    far, far_for = [], []
    for i, (by, there) in enumerate(around):
        far.append(both(there, starts_line if i in (0, 4, 6) else first))
        target_far = lax.rem(at(by), LINE) == 0 if i in (1, 5, 7) else at(by) == 0
        far_for.append(both(there, target_far))
    near = [both(there, jnp.logical_not(far[i])) for i, (_, there) in enumerate(around)]

    barrier = pltpu.get_barrier_semaphore()
    greeted = jnp.int32(1)
    for i, (by, there) in enumerate(around):
        greeted = greeted + near[i].astype(jnp.int32)

        @pl.when(both(there, jnp.logical_not(far_for[i])))
        def _():
            pl.semaphore_signal(barrier, inc=1, device_id=(tm, at(by)), device_id_type=MESH)

    pl.semaphore_signal(barrier, inc=1, device_id=(1 - tm, me), device_id_type=MESH)

    placed = pair_copies(w_in, pw1) + [(decay_in, decay), (skip_in, skip)]
    first_needed = len(placed)
    placed += pair_copies(w_out, pw2)
    then_needed = len(placed)
    placed += side_copies(w_in, sw1, SIDE_IN) + side_copies(w_out, sw2, SIDE_OUT)
    placed = [pltpu.make_async_copy(src, dst, w_sem.at[i]) for i, (src, dst) in enumerate(placed)]
    for c in placed[:first_needed]:
        c.start()

    pl.semaphore_wait(barrier, greeted)
    for i, (by, _) in enumerate(around):
        @pl.when(far_for[i])
        def _():
            pl.semaphore_signal(far_sem.at[i], inc=1, device_id=(tm, at(by)), device_id_type=MESH)

    def edges(s, f):
        begin, keep = (0, slice(0, 8)) if s == 0 else (cols - 16, slice(8, 16))
        stage[s] = x[f, 2 : 2 + rows, begin : begin + 16, :].astype(F32)[:, keep, :].reshape(rows * 8, C)
        for n in range(2):
            offset = n if s == 0 else 7 - n
            edge[s, n, f] = stage[s, pl.ds(offset, rows, stride=8), :].astype(BF)
            for t in range(2):
                ends = pl.ds(offset + t * (rows - 2) * 8, 2, stride=8)
                cstage[s, t, n, 2 * f : 2 * f + 2] = stage[s, ends, :]

    plan = [
        (edge.at[0], z.at[1]),
        (edge.at[1], z.at[0]),
        (frames.at[:, pl.ds(0, 2)], x.at[:, pl.ds(rows + 2, 2)]),
        (frames.at[:, pl.ds(rows - 2, 2)], x.at[:, pl.ds(0, 2)]),
        (corner.at[0, 0], zc.at[1, 1]),
        (corner.at[1, 0], zc.at[0, 1]),
        (corner.at[0, 1], zc.at[1, 0]),
        (corner.at[1, 1], zc.at[0, 0]),
    ]
    sends = [
        pltpu.make_async_remote_copy(
            src_ref=src, dst_ref=dst, send_sem=send_sem.at[i], recv_sem=recv_sem.at[i],
            device_id=(tm, at(around[i][0])), device_id_type=MESH,
        )
        for i, (src, dst) in enumerate(plan)
    ]
    for f in range(count):
        loads[f].wait()
        edges(1, f)
    pl.when(near[1])(sends[1].start)
    for f in range(count):
        edges(0, f)
    rest = jnp.zeros((8, C), F32)
    for s in range(2):
        for t in range(2):
            for n in range(2):
                corner[s, t, n] = jnp.concatenate([cstage[s, t, n], rest], axis=0).astype(BF)

    comes = [around[i ^ 1][1] if i < 4 else around[11 - i][1] for i in range(8)]
    in_tile = lax.broadcasted_iota(jnp.int32, (1, 8, C), 1)

    def widen(f, start, size):
        wide = x[f, pl.ds(start, size)].astype(F32)
        no_last = jnp.concatenate([wide[:, : cols - 8], jnp.where(in_tile == 7, 0.0, wide[:, cols - 8 :])], axis=1)
        no_first = jnp.concatenate([jnp.where(in_tile == 0, 0.0, wide[:, :8]), wide[:, 8:]], axis=1)
        x3[f, pl.ds(start, size), :, 0:C] = pltpu.roll(no_last, 1, 1).astype(BF)
        x3[f, pl.ds(start, size), :, C : 2 * C] = pltpu.roll(no_first, cols - 1, 1).astype(BF)
        return wide

    def frame_rows(f, here):
        return [x3[f, here, :, 0:C], x[f, here], x3[f, here, :, C : 2 * C]]

    def exchange(i, src, dst):
        return pltpu.make_async_remote_copy(
            src_ref=src, dst_ref=dst, send_sem=tsend_sem.at[i], recv_sem=trecv_sem.at[i],
            device_id=(1 - tm, me), device_id_type=MESH,
        )

    half = pairs // 2
    chunks = [(1, half), (1 + half, pairs - 1 - half)]
    hands = [exchange(n, lo.at[pl.ds(q, size)], inc.at[pl.ds(q, size)]) for n, (q, size) in enumerate(chunks)]
    late_hands = [
        exchange(2, lo.at[pl.ds(0, 1)], inc.at[pl.ds(0, 1)]),
        exchange(3, lo.at[pl.ds(pairs, 1)], inc.at[pl.ds(pairs, 1)]),
        exchange(4, so.at[0], si.at[0]),
        exchange(5, so.at[1], si.at[1]),
    ]
    weights1 = pw1.reshape(4 * TAPS * C, 2 * C)
    weights2 = pw2.reshape(4 * TAPS * C, 2 * C)

    def loc_rows(q, size):
        return pl.ds((2 * q + 7) * cols, size * 2 * cols)

    def recur(f, q, size, drive):
        drive = drive.reshape(size, cols, 2 * C)
        drive = jnp.stack([drive[:, :, :C], drive[:, :, C:]], axis=1).reshape(size * 2 * cols, C)
        here = loc_rows(q, size)
        if f > 0:
            drive = decay[f : f + 1, :] * loc[f - 1, here] + drive
        loc[f, here] = drive
        if f == count - 1:
            lo[pl.ds(q, size)] = drive.astype(BF).reshape(size, 2, cols, C)

    def first_conv(n):
        q, size = chunks[n]
        for f in range(count):
            end = rows + 2 if n else 2 * half + 4
            for start in range(2 + n * (2 * half + 2), end, 2):
                widen(f, start, 2)
            lhs = pair_rows(frame_rows(f, pl.ds(2 * q, 2 * size + 2)), size)
            recur(f, q, size, mm(lhs, weights1[...]))

    def send_far(*which):
        for i, opposite in which:
            @pl.when(far[i])
            def _():
                pl.semaphore_wait(far_sem.at[opposite], 1)
                sends[i].start()

    for i in (5, 7, 4, 6, 3, 2):
        pl.when(near[i])(sends[i].start)
    for c in placed[first_needed:]:
        c.start()
    pair_zeros(pw1)
    for c in placed[:first_needed]:
        c.wait()
    first_conv(0)
    hands[0].start()
    pl.when(near[0])(sends[0].start)
    first_conv(1)
    hands[1].start()
    to_left, to_rest = ((0, 1), (4, 7), (6, 5)), ((2, 3), (3, 2), (1, 0), (5, 6), (7, 4))
    pl.when(both(starts_line, jnp.logical_not(first)))(functools.partial(send_far, *to_left))

    factors = []
    for f in range(count):
        keep = decay[f : f + 1, :]
        factors.append(keep * jnp.where(tm == 0, 0.0, 1.0) if f == 0 else factors[-1] * keep)

    def settle(f, q, real=(None, None)):
        state = loc[f, loc_rows(q, 1)].reshape(2, cols, C) + factors[f] * inc[q].astype(F32)
        first = jnp.where(in_tile == 0, 0.0, state[:, :8])
        last = jnp.where(in_tile == 7, 0.0, state[:, cols - 8 :])
        state = jnp.concatenate([first, state[:, 8 : cols - 8], last], axis=1)
        state = jnp.concatenate(
            [state[e : e + 1] if r is None else jnp.where(r, state[e : e + 1], 0.0) for e, r in enumerate(real)],
            axis=0,
        )
        here = pl.ds(2 * q, 2)
        s3[f, here, :, 0:C] = pltpu.roll(state, 1, 1).astype(BF)
        s3[f, here, :, C : 2 * C] = state.astype(BF)
        s3[f, here, :, 2 * C : 3 * C] = pltpu.roll(state, cols - 1, 1).astype(BF)

    def finish(f, p, size, result):
        result = result.reshape(size, cols, 2 * C)
        result = jnp.stack([result[:, :, :C], result[:, :, C:]], axis=1).reshape(2 * size, cols, C)
        mixed = result + skip[...] * x[f, pl.ds(2 + 2 * p, 2 * size)].astype(F32)
        ot[0, f, pl.ds(16 * p, 16 * size)] = mixed[:, :8].reshape(16 * size, C)
        ot[1, f, pl.ds(16 * p, 16 * size)] = mixed[:, cols - 8 :].reshape(16 * size, C)
        o[f, pl.ds(2 * p, 2 * size), 8 : cols - 8] = mixed[:, 8 : cols - 8].astype(BF)

    pair_zeros(pw2)
    side_zeros(sw1, SIDE_IN)
    side_zeros(sw2, SIDE_OUT)
    for i, (_, dst) in enumerate(plan):
        @pl.when(jnp.logical_not(comes[i]))
        def _():
            dst[...] = jnp.zeros(dst.shape, BF)

    for c in placed[first_needed:then_needed]:
        c.wait()
    inner = [(1, half - 1), (half, half - 1)]

    def second_conv(n, which):
        q, size = chunks[n]
        p, deep = inner[n]
        for f in which:
            for i in range(q, q + size):
                settle(f, i)
            lhs = pair_rows([s3[f, 2 * p : 2 * p + 2 * deep + 2]], deep)
            finish(f, p, deep, mm(lhs, weights2[...]))

    hands[0].wait_recv()
    second_conv(0, range(count))
    hands[1].wait_recv()
    second_conv(1, range(count // 2))

    pl.when(first)(functools.partial(send_far, *to_rest))

    def arrive(*which):
        for i in which:
            pl.when(comes[i])(sends[i].wait_recv)

    arrive(2, 3)
    for f in range(count):
        for t in range(2):
            wide = widen(f, t * (rows + 2), 2)
            rim[t, 0, 16 * f : 16 * f + 16] = wide[:, :8].reshape(16, C)
            rim[t, 1, 16 * f : 16 * f + 16] = wide[:, cols - 8 :].reshape(16, C)
    lhs = [pair_rows(frame_rows(f, pl.ds(2 * q, 4)), 1) for q in (0, pairs) for f in range(count)]
    drive = mm_halves(jnp.concatenate(lhs, axis=0), weights1[...])
    for n, q in enumerate((0, pairs)):
        for f in range(count):
            recur(f, q, 1, drive[(n * count + f) * cols : (n * count + f + 1) * cols])
    late_hands[0].start()
    late_hands[1].start()
    pl.when(first)(functools.partial(send_far, *to_left))

    def side_in(s):
        arrive(*((1, 5, 7) if s == 0 else (0, 4, 6)))
        lines = [jnp.concatenate([z[s, 0, f], z[s, 1, f], edge[s, 0, f]], axis=-1) for f in range(count)]
        for t in range(2):
            mine = jnp.concatenate([rim[t, s, pl.ds(7 * s, 8, stride=8), :], rest], axis=0).astype(BF)
            lines.append(jnp.concatenate([zc[s, t, 0], zc[s, t, 1], mine], axis=-1))
        lhs = jnp.concatenate(lines, axis=0)
        for a in range(3):
            result = mm(lhs, sw1[s, a].reshape(3 * C, 2 * C))
            for e in range(2):
                part = result[:, e * C : (e + 1) * C]
                for f in range(count):
                    base = 2 * (8 + f * tall)
                    y[s, a, e, pl.ds(base + 16, rows, stride=2), :] = part[f * rows : (f + 1) * rows]
                    for t in range(2):
                        begin = count * rows + 16 * t + 2 * f
                        y[s, a, e, pl.ds(base + 12 + t * 2 * (rows + 2), 2, stride=2), :] = part[begin : begin + 2]
        inside = jnp.where(left if s == 0 else right, 1.0, 0.0).astype(F32)
        for e in range(2):
            state = None
            for f in range(count):
                base = 2 * (8 + f * tall)
                drive = sum(y[s, a, e, pl.ds(base + 2 * (a - 1), tall, stride=2), :] for a in range(3))
                if e == 0:
                    drive = drive * inside
                state = drive if f == 0 else decay[f : f + 1, :] * state + drive
                whole = state
                if e == 1:
                    whole = state + loc[f, pl.ds(s * (cols - 1), tall, stride=cols), :]
                ss[s, e, f] = whole
            so[s, e] = whole.astype(BF)
        late_hands[2 + s].start()

    def side_out(s):
        late_hands[2 + s].wait_recv()
        place = lax.broadcasted_iota(jnp.int32, (tall, C), 0)
        off = jnp.logical_or(
            both(place == 7, jnp.logical_not(up)), both(place == rows + 8, jnp.logical_not(down))
        )
        sides = []
        for f in range(count):
            pair = [
                jnp.where(off, 0.0, ss[s, e, f] + factors[f] * si[s, e].astype(F32)).astype(BF) for e in range(2)
            ]
            sides.append(jnp.concatenate(pair, axis=-1))
        lhs = jnp.concatenate(sides, axis=0)
        for a in range(3):
            result = mm(lhs, sw2[s, a].reshape(2 * C, 2 * C))
            for e in range(2):
                y2[s, a, e, pl.ds(16, count * tall, stride=2), :] = result[:, e * C : (e + 1) * C]
        begin = s * (cols - 8)
        for f in range(count):
            base = 2 * (8 + f * tall + 8)
            for e in range(2):
                here = pl.ds(e if s == 0 else 7 - e, rows, stride=8)
                fix = sum(y2[s, a, e, pl.ds(base + 2 * (a - 1), rows, stride=2), :] for a in range(3))
                ot[s, f, here, :] = ot[s, f, here, :] + fix
            o[f, :, begin : begin + 8] = ot[s, f].reshape(rows, 8, C).astype(BF)

    for c in placed[then_needed:]:
        c.wait()
    ends_line = lax.rem(me, LINE) == LINE - 1
    orders = ((ends_line, 0, 1), (jnp.logical_not(ends_line), 1, 0))
    for here, early, last in orders:
        @pl.when(here)
        def _():
            side_in(early)

    second_conv(1, range(count // 2, count))
    late_hands[0].wait_recv()
    late_hands[1].wait_recv()
    for f in range(count):
        settle(f, 0, (up, None))
        settle(f, pairs, (None, down))
    lhs = [pair_rows([s3[f, 2 * p : 2 * p + 4]], 1) for p in (0, pairs - 1) for f in range(count)]
    result = mm_halves(jnp.concatenate(lhs, axis=0), weights2[...])
    for n, p in enumerate((0, pairs - 1)):
        for f in range(count):
            finish(f, p, 1, result[(n * count + f) * cols : (n * count + f + 1) * cols])

    for here, early, last in orders:
        @pl.when(here)
        def _():
            side_in(last)
            side_out(early)
            side_out(last)

    for i, c in enumerate(sends):
        pl.when(around[i][1])(c.wait_send)
    for c in hands + late_hands:
        c.wait_send()


def write_out(o, out, sem):
    size = o.shape[1] // PIECES
    stores = [
        pltpu.make_async_copy(
            o.at[f, pl.ds(n * size, size)], out.at[f, pl.ds(n * size, size)], sem.at[f, n]
        )
        for f in range(o.shape[0])
        for n in range(PIECES)
    ]
    for c in stores:
        c.start()
    for c in stores:
        c.wait()


def per_device(frames, w_in, w_out, decay, skip):
    count, _, rows, cols, _ = frames.shape
    tall = rows + 16
    spread = 2 * (count * tall + 16)
    hbm = pl.BlockSpec(memory_space=pltpu.HBM)
    vmem = pl.BlockSpec(memory_space=pltpu.VMEM)
    args = (frames[:, 0], w_in, w_out, decay, skip.reshape(1, C))
    out = pl.pallas_call(
        functools.partial(kernel, TROWS),
        out_shape=pltpu.VMEM((count, rows, cols, C), BF),
        in_specs=[hbm] * 5,
        out_specs=vmem,
        scratch_shapes=[
            pltpu.VMEM((count, rows + 4, cols, C), BF),
            pltpu.VMEM((count, rows + 4, cols, 2 * C), BF),
            pltpu.VMEM((count, rows + 2, cols, 3 * C), BF),
            pltpu.VMEM((count, tall * cols, C), F32),
            pltpu.VMEM((4 * TAPS, C, 2 * C), BF),
            pltpu.VMEM((4 * TAPS, C, 2 * C), BF),
            pltpu.VMEM((2, TAPS, 3, C, 2 * C), BF),
            pltpu.VMEM((2, TAPS, 2, C, 2 * C), BF),
            pltpu.VMEM((2, 2, count, rows, C), BF),
            pltpu.VMEM((2, 2, 2, 16, C), BF),
            pltpu.VMEM((2, 2, count, rows, C), BF),
            pltpu.VMEM((2, 2, 2, 16, C), BF),
            pltpu.VMEM((2, TAPS, 2, spread, C), F32),
            pltpu.VMEM((2, TAPS, 2, spread, C), F32),
            pltpu.VMEM((2, 2, count, tall, C), F32),
            pltpu.VMEM((2, rows * 8, C), F32),
            pltpu.VMEM((2, 2, 2, 8, C), F32),
            pltpu.VMEM((2, 2, 16 * count, C), F32),
            pltpu.VMEM((rows // 2 + 1, 2, cols, C), BF),
            pltpu.VMEM((rows // 2 + 1, 2, cols, C), BF),
            pltpu.VMEM((2, 2, tall, C), BF),
            pltpu.VMEM((2, 2, tall, C), BF),
            pltpu.VMEM((2, count, rows * 8, C), F32),
            pltpu.VMEM((count, C), F32),
            pltpu.VMEM((1, C), F32),
            pltpu.SemaphoreType.DMA((count,)),
            pltpu.SemaphoreType.DMA((28,)),
            pltpu.SemaphoreType.DMA((8,)),
            pltpu.SemaphoreType.DMA((8,)),
            pltpu.SemaphoreType.DMA((6,)),
            pltpu.SemaphoreType.DMA((6,)),
            pltpu.SemaphoreType.REGULAR((8,)),
        ],
        compiler_params=pltpu.CompilerParams(
            collective_id=0, has_side_effects=True, vmem_limit_bytes=48 * 2**20
        ),
    )(*(pltpu.with_memory_space_constraint(a, pltpu.HBM) for a in args))
    out = pl.pallas_call(
        write_out,
        out_shape=jax.ShapeDtypeStruct(out.shape, BF),
        in_specs=[vmem],
        out_specs=hbm,
        scratch_shapes=[pltpu.SemaphoreType.DMA((count, PIECES))],
        compiler_params=pltpu.CompilerParams(vmem_limit_bytes=2**20),
    )(pltpu.with_memory_space_constraint(out, pltpu.VMEM))
    return out.reshape(count, 1, rows, cols, C)


def solution(mesh):
    return jax.shard_map(
        per_device,
        mesh=mesh,
        in_specs=(P("tm", "tile", None, None, None), P(), P(), P("tm", None), P()),
        out_specs=P("tm", "tile", None, None, None),
        check_vma=False,
    )
```

```python
import functools

import jax
import jax.numpy as jnp
from jax import lax
from jax.experimental import pallas as pl
from jax.experimental.pallas import tpu as pltpu
from jax.sharding import PartitionSpec as P

TROWS = 4
LINE = 4
C = 128
BF = jnp.bfloat16
F32 = jnp.float32
MESH = pl.DeviceIdType.MESH

TAPS = 3
PIECES = 1


def mm(lhs, rhs):
    return jnp.dot(lhs, rhs, preferred_element_type=F32)


def mm_halves(lhs, rhs):
    half = lhs.shape[1] // 2
    return mm(lhs[:, :half], rhs[:half]) + mm(lhs[:, half:], rhs[half:])


def pair_zeros(pair):
    zero = jnp.zeros((TAPS, C, C), BF)
    pair[3 * TAPS : 4 * TAPS, :, 0:C] = zero
    pair[0:TAPS, :, C : 2 * C] = zero


def pair_copies(w, pair):
    return [
        (w.at[i], pair.at[pl.ds((i + e) * TAPS, TAPS), :, pl.ds(e * C, C)]) for i in range(TAPS) for e in range(2)
    ]


def side_blocks(table):
    return [(s, k, e, b) for s in range(2) for k, taps in enumerate(table[s]) for e, b in enumerate(taps)]


def side_zeros(side, table):
    for s, k, e, b in side_blocks(table):
        if b is None:
            side[s, :, k, :, e * C : (e + 1) * C] = jnp.zeros((TAPS, C, C), BF)


def side_copies(w, side, table):
    return [
        (w.at[:, b], side.at[s, :, k, :, pl.ds(e * C, C)]) for s, k, e, b in side_blocks(table) if b is not None
    ]


SIDE_IN = (((1, 0), (0, None), (2, None)), ((1, 2), (2, None), (0, None)))
SIDE_OUT = (((0, None), (1, 0)), ((2, None), (1, 2)))


def pair_rows(parts, pairs):
    cols = parts[0].shape[1]
    split = [p.reshape(pairs + 1, 2, cols, p.shape[2]) for p in parts]
    taps = []
    for first in (0, 1):
        for parity in (0, 1):
            taps += [p[first : first + pairs, parity] for p in split]
    return jnp.concatenate(taps, axis=-1).reshape(pairs * cols, 12 * C)


def kernel(
    trows, frames, w_in, w_out, decay_in, skip_in, o,
    x, x3, s3, loc, pw1, pw2, sw1, sw2, edge, corner, z, zc, y, y2, ss, stage, cstage, rim, lo, inc, so, si, ot, decay, skip,
    load_sem, w_sem, send_sem, recv_sem, tsend_sem, trecv_sem, far_sem, right_send, right_recv,
):
    count, rows, cols, _ = frames.shape
    tiles = lax.axis_size("tile")
    tcols = tiles // trows
    me = lax.axis_index("tile")
    tm = lax.axis_index("tm")
    k = lax.rem(me + tiles - 1, tiles)
    column = lax.rem(k, tcols)
    row_index = k // tcols
    up, down = row_index > 0, row_index < trows - 1
    left, right = column > 0, column < tcols - 1
    pairs = rows // 2
    tall = rows + 16

    loads = [
        pltpu.make_async_copy(frames.at[f], x.at[f, pl.ds(2, rows)], load_sem.at[f])
        for f in range(count)
    ]
    for c in loads:
        c.start()

    both = jnp.logical_and
    around = [
        (-1, left), (1, right), (-tcols, up), (tcols, down),
        (-tcols - 1, both(up, left)), (-tcols + 1, both(up, right)),
        (tcols - 1, both(down, left)), (tcols + 1, both(down, right)),
    ]

    def at(by):
        return lax.rem(me + by + tiles, tiles)

    first = me == 0
    starts_line = lax.rem(me, LINE) == 0
    far, far_for = [], []
    for i, (by, there) in enumerate(around):
        far.append(both(there, starts_line if i in (0, 4, 6) else first))
        target_far = lax.rem(at(by), LINE) == 0 if i in (1, 5, 7) else at(by) == 0
        far_for.append(both(there, target_far))
    near = [both(there, jnp.logical_not(far[i])) for i, (_, there) in enumerate(around)]

    barrier = pltpu.get_barrier_semaphore()
    greeted = jnp.int32(1)
    for i, (by, there) in enumerate(around):
        greeted = greeted + near[i].astype(jnp.int32)

        @pl.when(both(there, jnp.logical_not(far_for[i])))
        def _():
            pl.semaphore_signal(barrier, inc=1, device_id=(tm, at(by)), device_id_type=MESH)

    pl.semaphore_signal(barrier, inc=1, device_id=(1 - tm, me), device_id_type=MESH)

    placed = pair_copies(w_in, pw1) + [(decay_in, decay), (skip_in, skip)]
    first_needed = len(placed)
    placed += pair_copies(w_out, pw2)
    then_needed = len(placed)
    placed += side_copies(w_in, sw1, SIDE_IN) + side_copies(w_out, sw2, SIDE_OUT)
    placed = [pltpu.make_async_copy(src, dst, w_sem.at[i]) for i, (src, dst) in enumerate(placed)]
    for c in placed[:first_needed]:
        c.start()

    pl.semaphore_wait(barrier, greeted)
    for i, (by, _) in enumerate(around):
        @pl.when(far_for[i])
        def _():
            pl.semaphore_signal(far_sem.at[i], inc=1, device_id=(tm, at(by)), device_id_type=MESH)

    def edges(s, f):
        begin, keep = (0, slice(0, 8)) if s == 0 else (cols - 16, slice(8, 16))
        stage[s] = x[f, 2 : 2 + rows, begin : begin + 16, :].astype(F32)[:, keep, :].reshape(rows * 8, C)
        for n in range(2):
            offset = n if s == 0 else 7 - n
            edge[s, n, f] = stage[s, pl.ds(offset, rows, stride=8), :].astype(BF)
            for t in range(2):
                ends = pl.ds(offset + t * (rows - 2) * 8, 2, stride=8)
                cstage[s, t, n, 2 * f : 2 * f + 2] = stage[s, ends, :]

    plan = [
        (edge.at[0], z.at[1]),
        (edge.at[1], z.at[0]),
        (frames.at[:, pl.ds(0, 2)], x.at[:, pl.ds(rows + 2, 2)]),
        (frames.at[:, pl.ds(rows - 2, 2)], x.at[:, pl.ds(0, 2)]),
        (corner.at[0, 0], zc.at[1, 1]),
        (corner.at[1, 0], zc.at[0, 1]),
        (corner.at[0, 1], zc.at[1, 0]),
        (corner.at[1, 1], zc.at[0, 0]),
    ]
    sends = [
        pltpu.make_async_remote_copy(
            src_ref=src, dst_ref=dst, send_sem=send_sem.at[i], recv_sem=recv_sem.at[i],
            device_id=(tm, at(around[i][0])), device_id_type=MESH,
        )
        for i, (src, dst) in enumerate(plan)
    ]
    rights = [
        pltpu.make_async_remote_copy(
            src_ref=edge.at[1, :, f], dst_ref=z.at[0, :, f], send_sem=right_send.at[f], recv_sem=right_recv.at[f],
            device_id=(tm, at(1)), device_id_type=MESH,
        )
        for f in range(count)
    ]

    for f in range(count):
        loads[f].wait()
        edges(1, f)
        pl.when(near[1])(rights[f].start)
    for f in range(count):
        edges(0, f)
    rest = jnp.zeros((8, C), F32)
    for s in range(2):
        for t in range(2):
            for n in range(2):
                corner[s, t, n] = jnp.concatenate([cstage[s, t, n], rest], axis=0).astype(BF)

    comes = [around[i ^ 1][1] if i < 4 else around[11 - i][1] for i in range(8)]
    in_tile = lax.broadcasted_iota(jnp.int32, (1, 8, C), 1)

    def widen(f, start, size):
        wide = x[f, pl.ds(start, size)].astype(F32)
        no_last = jnp.concatenate([wide[:, : cols - 8], jnp.where(in_tile == 7, 0.0, wide[:, cols - 8 :])], axis=1)
        no_first = jnp.concatenate([jnp.where(in_tile == 0, 0.0, wide[:, :8]), wide[:, 8:]], axis=1)
        x3[f, pl.ds(start, size), :, 0:C] = pltpu.roll(no_last, 1, 1).astype(BF)
        x3[f, pl.ds(start, size), :, C : 2 * C] = pltpu.roll(no_first, cols - 1, 1).astype(BF)
        return wide

    def frame_rows(f, here):
        return [x3[f, here, :, 0:C], x[f, here], x3[f, here, :, C : 2 * C]]

    def exchange(i, src, dst):
        return pltpu.make_async_remote_copy(
            src_ref=src, dst_ref=dst, send_sem=tsend_sem.at[i], recv_sem=trecv_sem.at[i],
            device_id=(1 - tm, me), device_id_type=MESH,
        )

    half = pairs // 2
    chunks = [(1, half), (1 + half, pairs - 1 - half)]
    hands = [exchange(n, lo.at[pl.ds(q, size)], inc.at[pl.ds(q, size)]) for n, (q, size) in enumerate(chunks)]
    late_hands = [
        exchange(2, lo.at[pl.ds(0, 1)], inc.at[pl.ds(0, 1)]),
        exchange(3, lo.at[pl.ds(pairs, 1)], inc.at[pl.ds(pairs, 1)]),
        exchange(4, so.at[0], si.at[0]),
        exchange(5, so.at[1], si.at[1]),
    ]
    weights1 = pw1.reshape(4 * TAPS * C, 2 * C)
    weights2 = pw2.reshape(4 * TAPS * C, 2 * C)

    def loc_rows(q, size):
        return pl.ds((2 * q + 7) * cols, size * 2 * cols)

    def recur(f, q, size, drive):
        drive = drive.reshape(size, cols, 2 * C)
        drive = jnp.stack([drive[:, :, :C], drive[:, :, C:]], axis=1).reshape(size * 2 * cols, C)
        here = loc_rows(q, size)
        if f > 0:
            drive = decay[f : f + 1, :] * loc[f - 1, here] + drive
        loc[f, here] = drive
        if f == count - 1:
            lo[pl.ds(q, size)] = drive.astype(BF).reshape(size, 2, cols, C)

    def first_conv(n):
        q, size = chunks[n]
        for f in range(count):
            end = rows + 2 if n else 2 * half + 4
            for start in range(2 + n * (2 * half + 2), end, 2):
                widen(f, start, 2)
            lhs = pair_rows(frame_rows(f, pl.ds(2 * q, 2 * size + 2)), size)
            recur(f, q, size, mm(lhs, weights1[...]))

    def send_far(*which):
        for i, opposite in which:
            @pl.when(far[i])
            def _():
                pl.semaphore_wait(far_sem.at[opposite], 1)
                for c in rights if i == 1 else [sends[i]]:
                    c.start()

    for i in (5, 7, 4, 6, 3, 2):
        pl.when(near[i])(sends[i].start)
    for c in placed[first_needed:]:
        c.start()
    pair_zeros(pw1)
    for c in placed[:first_needed]:
        c.wait()
    first_conv(0)
    hands[0].start()
    pl.when(near[0])(sends[0].start)
    first_conv(1)
    hands[1].start()
    to_left, to_rest = ((0, 1), (4, 7), (6, 5)), ((2, 3), (3, 2), (1, 0), (5, 6), (7, 4))
    pl.when(both(starts_line, jnp.logical_not(first)))(functools.partial(send_far, *to_left))

    factors = []
    for f in range(count):
        keep = decay[f : f + 1, :]
        factors.append(keep * jnp.where(tm == 0, 0.0, 1.0) if f == 0 else factors[-1] * keep)

    def settle(f, q, real=(None, None)):
        state = loc[f, loc_rows(q, 1)].reshape(2, cols, C) + factors[f] * inc[q].astype(F32)
        first = jnp.where(in_tile == 0, 0.0, state[:, :8])
        last = jnp.where(in_tile == 7, 0.0, state[:, cols - 8 :])
        state = jnp.concatenate([first, state[:, 8 : cols - 8], last], axis=1)
        state = jnp.concatenate(
            [state[e : e + 1] if r is None else jnp.where(r, state[e : e + 1], 0.0) for e, r in enumerate(real)],
            axis=0,
        )
        here = pl.ds(2 * q, 2)
        s3[f, here, :, 0:C] = pltpu.roll(state, 1, 1).astype(BF)
        s3[f, here, :, C : 2 * C] = state.astype(BF)
        s3[f, here, :, 2 * C : 3 * C] = pltpu.roll(state, cols - 1, 1).astype(BF)

    def finish(f, p, size, result):
        result = result.reshape(size, cols, 2 * C)
        result = jnp.stack([result[:, :, :C], result[:, :, C:]], axis=1).reshape(2 * size, cols, C)
        mixed = result + skip[...] * x[f, pl.ds(2 + 2 * p, 2 * size)].astype(F32)
        ot[0, f, pl.ds(16 * p, 16 * size)] = mixed[:, :8].reshape(16 * size, C)
        ot[1, f, pl.ds(16 * p, 16 * size)] = mixed[:, cols - 8 :].reshape(16 * size, C)
        o[f, pl.ds(2 * p, 2 * size), 8 : cols - 8] = mixed[:, 8 : cols - 8].astype(BF)

    pair_zeros(pw2)
    side_zeros(sw1, SIDE_IN)
    side_zeros(sw2, SIDE_OUT)
    for i, (_, dst) in enumerate(plan):
        @pl.when(jnp.logical_not(comes[i]))
        def _():
            dst[...] = jnp.zeros(dst.shape, BF)

    for c in placed[first_needed:then_needed]:
        c.wait()
    inner = [(1, half - 1), (half, half - 1)]

    def second_conv(n, which):
        q, size = chunks[n]
        p, deep = inner[n]
        for f in which:
            for i in range(q, q + size):
                settle(f, i)
            lhs = pair_rows([s3[f, 2 * p : 2 * p + 2 * deep + 2]], deep)
            finish(f, p, deep, mm(lhs, weights2[...]))

    hands[0].wait_recv()
    second_conv(0, range(count))
    hands[1].wait_recv()
    second_conv(1, range(count // 2))

    pl.when(first)(functools.partial(send_far, *to_rest))

    def arrive(*which):
        for i in which:
            for c in rights if i == 1 else [sends[i]]:
                pl.when(comes[i])(c.wait_recv)

    arrive(2, 3)
    for f in range(count):
        for t in range(2):
            wide = widen(f, t * (rows + 2), 2)
            rim[t, 0, 16 * f : 16 * f + 16] = wide[:, :8].reshape(16, C)
            rim[t, 1, 16 * f : 16 * f + 16] = wide[:, cols - 8 :].reshape(16, C)
    lhs = [pair_rows(frame_rows(f, pl.ds(2 * q, 4)), 1) for q in (0, pairs) for f in range(count)]
    drive = mm_halves(jnp.concatenate(lhs, axis=0), weights1[...])
    for n, q in enumerate((0, pairs)):
        for f in range(count):
            recur(f, q, 1, drive[(n * count + f) * cols : (n * count + f + 1) * cols])
    late_hands[0].start()
    late_hands[1].start()
    pl.when(first)(functools.partial(send_far, *to_left))

    def side_in(s):
        arrive(*((1, 5, 7) if s == 0 else (0, 4, 6)))
        lines = [jnp.concatenate([z[s, 0, f], z[s, 1, f], edge[s, 0, f]], axis=-1) for f in range(count)]
        for t in range(2):
            mine = jnp.concatenate([rim[t, s, pl.ds(7 * s, 8, stride=8), :], rest], axis=0).astype(BF)
            lines.append(jnp.concatenate([zc[s, t, 0], zc[s, t, 1], mine], axis=-1))
        lhs = jnp.concatenate(lines, axis=0)
        for a in range(3):
            result = mm(lhs, sw1[s, a].reshape(3 * C, 2 * C))
            for e in range(2):
                part = result[:, e * C : (e + 1) * C]
                for f in range(count):
                    base = 2 * (8 + f * tall)
                    y[s, a, e, pl.ds(base + 16, rows, stride=2), :] = part[f * rows : (f + 1) * rows]
                    for t in range(2):
                        begin = count * rows + 16 * t + 2 * f
                        y[s, a, e, pl.ds(base + 12 + t * 2 * (rows + 2), 2, stride=2), :] = part[begin : begin + 2]
        inside = jnp.where(left if s == 0 else right, 1.0, 0.0).astype(F32)
        for e in range(2):
            state = None
            for f in range(count):
                base = 2 * (8 + f * tall)
                drive = sum(y[s, a, e, pl.ds(base + 2 * (a - 1), tall, stride=2), :] for a in range(3))
                if e == 0:
                    drive = drive * inside
                state = drive if f == 0 else decay[f : f + 1, :] * state + drive
                whole = state
                if e == 1:
                    whole = state + loc[f, pl.ds(s * (cols - 1), tall, stride=cols), :]
                ss[s, e, f] = whole
            so[s, e] = whole.astype(BF)
        late_hands[2 + s].start()

    def side_out(s):
        late_hands[2 + s].wait_recv()
        place = lax.broadcasted_iota(jnp.int32, (tall, C), 0)
        off = jnp.logical_or(
            both(place == 7, jnp.logical_not(up)), both(place == rows + 8, jnp.logical_not(down))
        )
        sides = []
        for f in range(count):
            pair = [
                jnp.where(off, 0.0, ss[s, e, f] + factors[f] * si[s, e].astype(F32)).astype(BF) for e in range(2)
            ]
            sides.append(jnp.concatenate(pair, axis=-1))
        lhs = jnp.concatenate(sides, axis=0)
        for a in range(3):
            result = mm(lhs, sw2[s, a].reshape(2 * C, 2 * C))
            for e in range(2):
                y2[s, a, e, pl.ds(16, count * tall, stride=2), :] = result[:, e * C : (e + 1) * C]
        begin = s * (cols - 8)
        for f in range(count):
            base = 2 * (8 + f * tall + 8)
            for e in range(2):
                here = pl.ds(e if s == 0 else 7 - e, rows, stride=8)
                fix = sum(y2[s, a, e, pl.ds(base + 2 * (a - 1), rows, stride=2), :] for a in range(3))
                ot[s, f, here, :] = ot[s, f, here, :] + fix
            o[f, :, begin : begin + 8] = ot[s, f].reshape(rows, 8, C).astype(BF)

    for c in placed[then_needed:]:
        c.wait()
    ends_line = lax.rem(me, LINE) == LINE - 1
    orders = ((ends_line, 0, 1), (jnp.logical_not(ends_line), 1, 0))
    for here, early, last in orders:
        @pl.when(here)
        def _():
            side_in(early)

    second_conv(1, range(count // 2, count))
    late_hands[0].wait_recv()
    late_hands[1].wait_recv()
    for f in range(count):
        settle(f, 0, (up, None))
        settle(f, pairs, (None, down))
    lhs = [pair_rows([s3[f, 2 * p : 2 * p + 4]], 1) for p in (0, pairs - 1) for f in range(count)]
    result = mm_halves(jnp.concatenate(lhs, axis=0), weights2[...])
    for n, p in enumerate((0, pairs - 1)):
        for f in range(count):
            finish(f, p, 1, result[(n * count + f) * cols : (n * count + f + 1) * cols])

    for here, early, last in orders:
        @pl.when(here)
        def _():
            side_in(last)
            side_out(early)
            side_out(last)

    for i, (_, there) in enumerate(around):
        for c in rights if i == 1 else [sends[i]]:
            pl.when(there)(c.wait_send)
    for c in hands + late_hands:
        c.wait_send()


def write_out(o, out, sem):
    size = o.shape[1] // PIECES
    stores = [
        pltpu.make_async_copy(
            o.at[f, pl.ds(n * size, size)], out.at[f, pl.ds(n * size, size)], sem.at[f, n]
        )
        for f in range(o.shape[0])
        for n in range(PIECES)
    ]
    for c in stores:
        c.start()
    for c in stores:
        c.wait()


def per_device(frames, w_in, w_out, decay, skip):
    count, _, rows, cols, _ = frames.shape
    tall = rows + 16
    spread = 2 * (count * tall + 16)
    hbm = pl.BlockSpec(memory_space=pltpu.HBM)
    vmem = pl.BlockSpec(memory_space=pltpu.VMEM)
    args = (frames[:, 0], w_in, w_out, decay, skip.reshape(1, C))
    out = pl.pallas_call(
        functools.partial(kernel, TROWS),
        out_shape=pltpu.VMEM((count, rows, cols, C), BF),
        in_specs=[hbm] * 5,
        out_specs=vmem,
        scratch_shapes=[
            pltpu.VMEM((count, rows + 4, cols, C), BF),
            pltpu.VMEM((count, rows + 4, cols, 2 * C), BF),
            pltpu.VMEM((count, rows + 2, cols, 3 * C), BF),
            pltpu.VMEM((count, tall * cols, C), F32),
            pltpu.VMEM((4 * TAPS, C, 2 * C), BF),
            pltpu.VMEM((4 * TAPS, C, 2 * C), BF),
            pltpu.VMEM((2, TAPS, 3, C, 2 * C), BF),
            pltpu.VMEM((2, TAPS, 2, C, 2 * C), BF),
            pltpu.VMEM((2, 2, count, rows, C), BF),
            pltpu.VMEM((2, 2, 2, 16, C), BF),
            pltpu.VMEM((2, 2, count, rows, C), BF),
            pltpu.VMEM((2, 2, 2, 16, C), BF),
            pltpu.VMEM((2, TAPS, 2, spread, C), F32),
            pltpu.VMEM((2, TAPS, 2, spread, C), F32),
            pltpu.VMEM((2, 2, count, tall, C), F32),
            pltpu.VMEM((2, rows * 8, C), F32),
            pltpu.VMEM((2, 2, 2, 8, C), F32),
            pltpu.VMEM((2, 2, 16 * count, C), F32),
            pltpu.VMEM((rows // 2 + 1, 2, cols, C), BF),
            pltpu.VMEM((rows // 2 + 1, 2, cols, C), BF),
            pltpu.VMEM((2, 2, tall, C), BF),
            pltpu.VMEM((2, 2, tall, C), BF),
            pltpu.VMEM((2, count, rows * 8, C), F32),
            pltpu.VMEM((count, C), F32),
            pltpu.VMEM((1, C), F32),
            pltpu.SemaphoreType.DMA((count,)),
            pltpu.SemaphoreType.DMA((28,)),
            pltpu.SemaphoreType.DMA((8,)),
            pltpu.SemaphoreType.DMA((8,)),
            pltpu.SemaphoreType.DMA((6,)),
            pltpu.SemaphoreType.DMA((6,)),
            pltpu.SemaphoreType.REGULAR((8,)),
            pltpu.SemaphoreType.DMA((count,)),
            pltpu.SemaphoreType.DMA((count,)),
        ],
        compiler_params=pltpu.CompilerParams(
            collective_id=0, has_side_effects=True, vmem_limit_bytes=48 * 2**20
        ),
    )(*(pltpu.with_memory_space_constraint(a, pltpu.HBM) for a in args))
    out = pl.pallas_call(
        write_out,
        out_shape=jax.ShapeDtypeStruct(out.shape, BF),
        in_specs=[vmem],
        out_specs=hbm,
        scratch_shapes=[pltpu.SemaphoreType.DMA((count, PIECES))],
        compiler_params=pltpu.CompilerParams(vmem_limit_bytes=2**20),
    )(pltpu.with_memory_space_constraint(out, pltpu.VMEM))
    return out.reshape(count, 1, rows, cols, C)


def solution(mesh):
    return jax.shard_map(
        per_device,
        mesh=mesh,
        in_specs=(P("tm", "tile", None, None, None), P(), P(), P("tm", None), P()),
        out_specs=P("tm", "tile", None, None, None),
        check_vma=False,
    )
```
